32 devices in a mesh: pipe: 2 (over x), dp: 2 (over y), tensor: 8 (over z, core).
Axes of the slice: x: 2, y: 2, z: 4, core: 2. Of those that a mesh axis runs over, the one named last changes fastest.
Arguments:
- states: bfloat16 [1152, 8, 1024], P('tensor', 'dp'), may hold values from -6 to 6
- cotangent: bfloat16 [1152, 8, 1024], P('tensor', 'dp'), may hold values from -6 to 6
- lengths: int32 [8, 4], P('dp'), may hold values from 1 to 525, 1152 in all within a row
- timesteps: int32 [8, 4], P('dp'), may hold values from 0 to 4999
- time_weight: float32 [2, 1024], P('pipe'), may hold values from -6 to 6
- time_bias: float32 [2, 1024], P('pipe'), may hold values from -3 to 3
- query_weight: bfloat16 [2, 1024, 1024], P('pipe', None, 'tensor'), may hold values from -0.1875 to 0.1875
- query_bias: float32 [2, 1024], P('pipe', 'tensor'), may hold values from -3 to 3
- key_weight: bfloat16 [2, 1024, 1024], P('pipe', None, 'tensor'), may hold values from -0.1875 to 0.1875
- value_weight: bfloat16 [2, 1024, 1024], P('pipe', None, 'tensor'), may hold values from -0.1875 to 0.1875
- value_bias: float32 [2, 1024], P('pipe', 'tensor'), may hold values from -3 to 3
- out_weight: bfloat16 [2, 1024, 1024], P('pipe', 'tensor'), may hold values from -3.5 to 3.5
- out_bias: float32 [2, 1024], P('pipe'), may hold values from -3 to 3
- attn_gain: float32 [2, 1024], P('pipe'), may hold values from 0.5 to 1.5
- attn_shift: float32 [2, 1024], P('pipe'), may hold values from -3 to 3
- ffn_in: bfloat16 [2, 1024, 4096], P('pipe', None, 'tensor'), may hold values from -0.1875 to 0.1875
- ffn_in_bias: bfloat16 [2, 4096], P('pipe', 'tensor'), may hold values from -3 to 3
- ffn_out: bfloat16 [2, 4096, 1024], P('pipe', 'tensor'), may hold values from -0.09375 to 0.09375
- ffn_out_bias: float32 [2, 1024], P('pipe'), may hold values from -3 to 3
- ffn_gain: float32 [2, 1024], P('pipe'), may hold values from 0.5 to 1.5
- ffn_shift: float32 [2, 1024], P('pipe'), may hold values from -3 to 3
Outputs:
- layer_out: bfloat16 [2, 1152, 8, 1024], P('pipe', 'tensor', 'dp')
- input_grad: bfloat16 [2, 1152, 8, 1024], P('pipe', 'tensor', 'dp')
- time_weight_grad: float32 [2, 1024], P('pipe')
- time_bias_grad: float32 [2, 1024], P('pipe')
- query_weight_grad: float32 [2, 1024, 1024], P('pipe', 'dp', 'tensor')
- query_bias_grad: float32 [2, 1024], P('pipe', 'tensor')
- key_weight_grad: float32 [2, 1024, 1024], P('pipe', 'dp', 'tensor')
- value_weight_grad: float32 [2, 1024, 1024], P('pipe', 'dp', 'tensor')
- value_bias_grad: float32 [2, 1024], P('pipe', 'tensor')
- out_weight_grad: float32 [2, 1024, 1024], P('pipe', 'tensor', 'dp')
- out_bias_grad: float32 [2, 1024], P('pipe')
- attn_gain_grad: float32 [2, 1024], P('pipe')
- attn_shift_grad: float32 [2, 1024], P('pipe')
- ffn_in_grad: float32 [2, 1024, 4096], P('pipe', 'dp', 'tensor')
- ffn_in_bias_grad: float32 [2, 4096], P('pipe', 'tensor')
- ffn_out_grad: float32 [2, 4096, 1024], P('pipe', 'tensor', 'dp')
- ffn_out_bias_grad: float32 [2, 1024], P('pipe')
- ffn_gain_grad: float32 [2, 1024], P('pipe')
- ffn_shift_grad: float32 [2, 1024], P('pipe')
- stats: float32 [2, 3], P('pipe')
The draws below stay inside these ranges and needn't reach their ends.
Inputs may be any that keep to these rules, and one draw needn't show every extreme that they name: `lengths`: each row sums to 1152, and its largest entry is exactly 525.
All inputs are finite; a program needn't handle non-finite values.
Results may differ from the reference program's by a relative error of at most 0.03.
Values may be sent and summed in bfloat16 or wider, within the bound.
A program may use at most 256 MiB of HBM per device.

```python
import math
import jax
import jax.numpy as jnp
import numpy as np
from jax import lax

D = 1024
HEADS = 16
HDIM = 64
FF = 4096
SEQ_LEN = 1152
ITEMS = 4
ITEM_MOST = 525
STEPS = 5000
NSEQ = 8
LAYERS = 2


def plant(result, own_key, low, top_value):
    index_at = [jax.random.randint(jax.random.fold_in(own_key, axis), (), 0, length) for axis, length in enumerate(result.shape)]
    widest = result.shape.index(max(result.shape))
    next_to = index_at[:widest] + [(index_at[widest] + 1) % result.shape[widest]] + index_at[widest + 1:]
    return result.at[tuple(index_at)].set(low).at[tuple(next_to)].set(top_value)


def block_scale(stream_key, shape, split, least, top_value):
    level, own = 1.0, jax.random.fold_in(stream_key, 6)
    for position, parts in split:
        steps = jnp.exp(jax.random.uniform(jax.random.fold_in(own, position), (parts,), jnp.float32, least / len(split), top_value / len(split)))
        level = level * jnp.repeat(steps, shape[position] // parts).reshape([-1 if axis == position else 1 for axis in range(len(shape))])
    return level


def rank_table(number_of, slope):
    weights = [(1 << 20) // math.isqrt(standing ** slope) + 1 for standing in range(1, number_of + 1)]
    scale = 1 + sum(weights) // (1 << 30)
    return np.cumsum(np.array([max(1, weight // scale) for weight in weights]))


def ranked(rng, dims, number_of, slope):
    table = rank_table(number_of, slope)
    pick = jax.random.randint(jax.random.fold_in(rng, 1), dims, 0, int(table[number_of - 1]))
    grade = jnp.searchsorted(jnp.asarray(table, jnp.int32), pick, side="right")
    return jax.random.permutation(jax.random.fold_in(rng, 2), number_of)[grade].astype(jnp.int32)


def split_up(amount, total, reach, slope):
    portions = [(1 << 20) // math.isqrt(grade ** slope) + 1 for grade in range(2, amount + 1)]
    rest, holding = total - reach - (amount - 1), [1] * (amount - 1)
    while rest > 0:
        candidates = [i for i in range(amount - 1) if holding[i] < reach]
        pool, left = sum([portions[i] for i in candidates]), rest
        for i in candidates:
            more = min(reach - holding[i], max(1, left * portions[i] // pool), rest)
            holding[i] = holding[i] + more
            rest = rest - more
    return np.array([reach] + holding)


def ragged_sizes(key, number_of, total, bound, skew):
    if number_of == 2:
        one = jax.random.randint(key, (), max(1, total - bound), min(bound, total - 1) + 1)
        return jnp.stack([one, total - one])
    sizes = jnp.asarray(split_up(number_of, total, bound, skew), jnp.int32)
    couples = (number_of - 1) // 2
    giver, taker = sizes[1:1 + 2 * couples:2], sizes[2:2 + 2 * couples:2]
    margin = jnp.minimum(giver - 1, bound - taker)
    shifted = jax.random.randint(jax.random.fold_in(key, 1), (couples,), 0, 1 << 20) % (margin + 1)
    sizes = sizes.at[1:1 + 2 * couples:2].set(giver - shifted).at[2:2 + 2 * couples:2].set(taker + shifted)
    return sizes[jax.random.permutation(jax.random.fold_in(key, 2), number_of)]


def scatter_about(key, dims, scale, bound, cuts=(), held_as=jnp.bfloat16):
    values = jax.random.normal(key, dims, jnp.float32) * scale
    if len(cuts) > 0:
        values = block_scale(key, dims, cuts, -0.22, 0.18) * values
    return jnp.clip(values, min=-bound, max=bound).astype(held_as)


def setup_inputs(seed: int = 0) -> dict:
    keys = jax.random.split(jax.random.key(seed), 22)
    states = scatter_about(keys[0], (SEQ_LEN, NSEQ, D), 1.0, 6.0, ((0, 8), (1, 2)))
    cotangent = scatter_about(keys[1], (SEQ_LEN, NSEQ, D), 1.0, 6.0, ((0, 8), (1, 2)))
    lengths = jax.vmap(lambda own: ragged_sizes(own, ITEMS, SEQ_LEN, ITEM_MOST, 2))(jax.random.split(keys[2], NSEQ)).reshape((NSEQ, ITEMS)).astype(jnp.int32)
    timesteps = plant(ranked(keys[3], (NSEQ, ITEMS), STEPS, 2), jax.random.fold_in(keys[3], 3), 0, STEPS - 1).astype(jnp.int32)
    time_weight = scatter_about(keys[4], (LAYERS, D), 1.0, 6.0, ((0, 2),), jnp.float32)
    time_bias = scatter_about(keys[5], (LAYERS, D), 0.5, 3.0, ((0, 2),), jnp.float32)
    query_weight = scatter_about(keys[6], (LAYERS, D, D), D ** -0.5, 0.1875, ((0, 2), (2, 8)))
    query_bias = scatter_about(keys[7], (LAYERS, D), 0.5, 3.0, ((0, 2), (1, 8)), jnp.float32)
    key_weight = scatter_about(keys[8], (LAYERS, D, D), D ** -0.5, 0.1875, ((0, 2), (2, 8)))
    value_weight = scatter_about(keys[9], (LAYERS, D, D), D ** -0.5, 0.1875, ((0, 2), (2, 8)))
    value_bias = scatter_about(keys[10], (LAYERS, D), 0.5, 3.0, ((0, 2), (1, 8)), jnp.float32)
    out_weight = scatter_about(keys[11], (LAYERS, D, D), (max(D * ITEMS // SEQ_LEN, 1)) ** -0.5, 3.5, ((0, 2), (1, 8)))
    out_bias = scatter_about(keys[12], (LAYERS, D), 0.5, 3.0, ((0, 2),), jnp.float32)
    attn_gain = jnp.clip(1.0 + 0.1 * jax.random.normal(keys[13], (LAYERS, D), jnp.float32), 0.5, 1.5)
    attn_shift = scatter_about(keys[14], (LAYERS, D), 0.5, 3.0, ((0, 2),), jnp.float32)
    ffn_in = scatter_about(keys[15], (LAYERS, D, FF), D ** -0.5, 0.1875, ((0, 2), (2, 8)))
    ffn_in_bias = scatter_about(keys[16], (LAYERS, FF), 0.5, 3.0, ((0, 2), (1, 8)))
    ffn_out = scatter_about(keys[17], (LAYERS, FF, D), FF ** -0.5, 0.09375, ((0, 2), (1, 8)))
    ffn_out_bias = scatter_about(keys[18], (LAYERS, D), 0.5, 3.0, ((0, 2),), jnp.float32)
    ffn_gain = jnp.clip(1.0 + 0.1 * jax.random.normal(keys[19], (LAYERS, D), jnp.float32), 0.5, 1.5)
    ffn_shift = scatter_about(keys[20], (LAYERS, D), 0.5, 3.0, ((0, 2),), jnp.float32)
    return dict(states=states, cotangent=cotangent, lengths=lengths, timesteps=timesteps, time_weight=time_weight, time_bias=time_bias, query_weight=query_weight, query_bias=query_bias, key_weight=key_weight, value_weight=value_weight, value_bias=value_bias, out_weight=out_weight, out_bias=out_bias, attn_gain=attn_gain, attn_shift=attn_shift, ffn_in=ffn_in, ffn_in_bias=ffn_in_bias, ffn_out=ffn_out, ffn_out_bias=ffn_out_bias, ffn_gain=ffn_gain, ffn_shift=ffn_shift)


@jax.custom_vjp
def low(v):
    return lax.optimization_barrier(v.astype(jnp.bfloat16)).astype(jnp.float32)

@jax.custom_vjp
def low_back(v):
    return v

def low_keep(v):
    return (low(v), None)

def low_pass(kept, grad):
    return (grad,)

def back_keep(v):
    return (v, None)

def back_low(kept, grad):
    return (low(grad),)
low.defvjp(low_keep, low_pass)
low_back.defvjp(back_keep, back_low)
epsilon = 1e-05
highest = lax.Precision.HIGHEST

def layer_norm(summed, gain, shift):
    centered = summed - lax.optimization_barrier(jnp.mean(summed, axis=-1, keepdims=True))
    inverse = lax.rsqrt(lax.optimization_barrier(jnp.mean(centered * centered, axis=-1, keepdims=True)) + epsilon)
    return centered * inverse * gain + shift

def item_tables(lengths, timesteps):
    item_ends = jnp.cumsum(lengths, axis=1).astype(jnp.int32)
    places = jnp.arange(SEQ_LEN, dtype=jnp.int32)
    segment = lax.optimization_barrier(jnp.sum((item_ends[None, :, :] <= places[:, None, None]).astype(jnp.int32), axis=2)).astype(jnp.int32)
    item_pick = segment[:, :, None] == jnp.arange(ITEMS, dtype=jnp.int32)[None, None, :]
    time_frac = lax.optimization_barrier(jnp.sum(jnp.where(item_pick, timesteps[None, :, :].astype(jnp.float32), jnp.float32(0.0)), axis=2)) / STEPS
    return (segment, time_frac)

def project(activ, weight):
    return jnp.einsum('tsd,de->tse', activ, weight, precision=highest)

def heads_first(activ):
    return jnp.transpose(activ, (1, 0, 2)).reshape(activ.shape[1], SEQ_LEN, HEADS, HDIM)

def attend(block):
    queries, keys_all, values, segment = block
    scores = jnp.einsum('qhd,khd->hqk', queries, keys_all, precision=highest) / math.sqrt(HDIM)
    scores = low_back(scores)
    same_item = segment[:, None] == segment[None, :]
    scores = jnp.where(same_item[None], scores, -1e+30)
    row_top = lax.optimization_barrier(jnp.max(scores, axis=-1, keepdims=True))
    weights = jnp.exp(scores - row_top)
    probs = weights / lax.optimization_barrier(jnp.sum(weights, axis=-1, keepdims=True))
    return jnp.einsum('hqk,khd->qhd', low(probs), values, precision=highest)

def encoder_layer(inputs, time_frac, segment, weight_set):
    time_weight, time_bias, query_weight, query_bias, key_weight, value_weight, value_bias, out_weight, out_bias, attn_gain, attn_shift, ffn_in, ffn_in_bias, ffn_out, ffn_out_bias, ffn_gain, ffn_shift = weight_set
    residual = inputs + time_frac[:, :, None] * time_weight + time_bias
    rounded = low(residual)
    queries = low(low_back(project(rounded, query_weight) + query_bias))
    keys_all = low(low_back(project(rounded, key_weight)))
    values = low(low_back(project(rounded, value_weight) + value_bias))
    attended = lax.map(jax.checkpoint(attend), (heads_first(queries), heads_first(keys_all), heads_first(values), segment.T))
    joined_heads = attended.reshape(attended.shape[0], SEQ_LEN, HEADS * HDIM)
    mixed = low(low_back(jnp.transpose(joined_heads, (1, 0, 2))))
    branch = low_back(project(mixed, out_weight) + out_bias)
    first_out = layer_norm(residual + branch, attn_gain, attn_shift)
    first_low = low(first_out)
    pre_act = low_back(project(first_low, ffn_in) + ffn_in_bias)
    hidden = low(jax.nn.gelu(pre_act, approximate=False))
    ffn_branch = low_back(project(hidden, ffn_out) + ffn_out_bias)
    layer_y = layer_norm(first_out + ffn_branch, ffn_gain, ffn_shift)
    stat_terms = jnp.stack([jnp.sqrt(jnp.mean(residual * residual)), jnp.sqrt(jnp.mean(branch * branch)), jnp.sqrt(jnp.mean(ffn_branch * ffn_branch))])
    return (layer_y, stat_terms)

def reference(states, cotangent, lengths, timesteps, time_weight, time_bias, query_weight, query_bias, key_weight, value_weight, value_bias, out_weight, out_bias, attn_gain, attn_shift, ffn_in, ffn_in_bias, ffn_out, ffn_out_bias, ffn_gain, ffn_shift):
    segment, time_frac = item_tables(lengths, timesteps)
    floats = tuple((array.astype(jnp.float32) for array in (time_weight, time_bias, query_weight, query_bias, key_weight, value_weight, value_bias, out_weight, out_bias, attn_gain, attn_shift, ffn_in, ffn_in_bias, ffn_out, ffn_out_bias, ffn_gain, ffn_shift)))
    start_rows = states.astype(jnp.float32)
    entry = jnp.zeros_like(start_rows)

    def forward(start_rows, entry, *weight_sets):
        first_y, first_stats = encoder_layer(start_rows, time_frac, segment, tuple((stack[0] for stack in weight_sets)))
        passed = low_back(low(first_y)) + entry
        second_y, second_stats = encoder_layer(passed, time_frac, segment, tuple((stack[1] for stack in weight_sets)))
        return (second_y, (first_y, second_y, jnp.stack([first_stats, second_stats])))
    final_y, pullback, (first_y, second_y, stats) = jax.vjp(forward, start_rows, entry, *floats, has_aux=True)
    grads = pullback(cotangent.astype(jnp.float32))
    layer_out = jnp.stack([first_y, second_y]).astype(jnp.bfloat16)
    input_grad = jnp.stack([grads[0], grads[1]]).astype(jnp.bfloat16)
    return (layer_out, input_grad, grads[2], grads[3], grads[4], grads[5], grads[6], grads[7], grads[8], grads[9], grads[10], grads[11], grads[12], grads[13], grads[14], grads[15], grads[16], grads[17], grads[18], stats)
```

```python
import functools
import math

import jax
import jax.numpy as jnp
from jax import lax
from jax.experimental import pallas as pl
from jax.experimental.pallas import tpu as pltpu
from jax.sharding import Mesh
from jax.sharding import PartitionSpec as P

HDIM = 64
SEQ_LEN = 1152
STEPS = 5000
PAIR = 2 * HDIM
TILE = 128
WIDTHS = (2, 3, 4, 5, 6, 7, 9)
LOG2E = math.log2(math.e)
SCALE = 1.0 / math.sqrt(HDIM)
TENSOR = ("zs", "tp")

epsilon = 1e-05
f32 = jnp.float32
bf16 = jnp.bfloat16


def received(shard, axis, by):
    size = lax.axis_size(axis)
    by = by % size
    if by == 0:
        return shard
    return lax.ppermute(shard, axis, [((i + by) % size, i) for i in range(size)])


def passed_along(shard, axis, by):
    size = lax.axis_size(axis)
    pairs = [(i, i + by) for i in range(size) if 0 <= i + by < size]
    return lax.ppermute(shard, axis, pairs)


def summed_over(values, axis):
    total = values
    for by in range(1, lax.axis_size(axis)):
        total = total + received(values, axis, by)
    return total


def after(value, *others):
    return lax.optimization_barrier((value, *others))[0]


def norm_parts(summed):
    centered = summed - jnp.mean(summed, axis=-1, keepdims=True)
    inverse = lax.rsqrt(jnp.mean(centered * centered, axis=-1, keepdims=True) + epsilon)
    return (centered * inverse, inverse)


def norm_back(upstream, normed, inverse, gain):
    scaled = upstream * gain
    return inverse * (
        scaled
        - jnp.mean(scaled, axis=-1, keepdims=True)
        - normed * jnp.mean(scaled * normed, axis=-1, keepdims=True)
    )


def token_sum(values):
    return jnp.sum(values.astype(f32), axis=0)


def mm(a, b, dims=((1,), (0,))):
    return lax.dot_general(a, b, (dims, ((), ())), preferred_element_type=f32)


def key_spans(item_ends, length):
    tiles = length // TILE
    first = jnp.arange(tiles, dtype=jnp.int32)[:, None] * TILE
    ends = item_ends[None, :]
    start = jnp.max(jnp.where(ends <= first, ends, 0), axis=1) // TILE
    end = jnp.min(jnp.where(ends > first + TILE - 1, ends, length), axis=1)
    need = (end + TILE - 1) // TILE - start
    widths = jnp.array([min(w, tiles) for w in WIDTHS], jnp.int32)
    kind = jnp.sum((widths[None, :] < need[:, None]).astype(jnp.int32), axis=1)
    is_kind = jnp.arange(len(WIDTHS), dtype=jnp.int32)[None, :] == kind[:, None]
    width = jnp.sum(jnp.where(is_kind, widths[None, :], 0), axis=1)
    return jnp.stack([kind, jnp.minimum(start, tiles - width) * TILE]).astype(jnp.int32)


def place(order, source, target, rows, by_position):
    for block in range(source.shape[0] // rows):
        at = pl.ds(pl.multiple_of(order[block] * rows, 16), rows)
        if by_position:
            target[at, :] = source[block * rows : (block + 1) * rows, :]
        else:
            target[block * rows : (block + 1) * rows, :] = source[at, :]


def two_heads(pair):
    first = lax.broadcasted_iota(jnp.int32, pair.shape, 1) < HDIM
    zero = jnp.zeros_like(pair)
    return jnp.concatenate([jnp.where(first, pair, zero), jnp.where(first, zero, pair)], axis=0)


def one_pair(stacked):
    half = stacked.shape[0] // 2
    first = lax.broadcasted_iota(jnp.int32, (half, stacked.shape[1]), 1) < HDIM
    return jnp.where(first, stacked[:half], stacked[half:])


def each_tile(span, length, body):
    tiles = length // TILE

    def step(tile, carry):
        at = pl.ds(pl.multiple_of(tile * TILE, TILE), TILE)

        def branch(width):
            count = min(width, tiles) * TILE
            return lambda: body(at, pl.ds(pl.multiple_of(span[1, tile], TILE), count))

        lax.switch(span[0, tile], [branch(width) for width in WIDTHS])
        return carry

    lax.fori_loop(0, tiles, step, 0)


def attend_kernel(
    rows, order, span, seg_c, seg_r, q_ref, k_ref, v_ref, mixed_ref, lse_ref, q_s, k_s, v_s, mixed_s
):
    for source, target in ((q_ref, q_s), (k_ref, k_s), (v_ref, v_s)):
        place(order, source, target, rows, True)

    def body(at, to):
        same_item = seg_c[at, :] == seg_r[:, to]
        same_item = jnp.concatenate([same_item, same_item], axis=0)
        for pair in range(q_ref.shape[1] // PAIR):
            cols = slice(pair * PAIR, (pair + 1) * PAIR)
            scores = mm(two_heads(q_s[at, cols]), k_s[to, cols], ((1,), (1,))) * (SCALE * LOG2E)
            scores = jnp.where(same_item, scores, -1e30)
            top = jnp.max(scores, axis=1, keepdims=True)
            weights = jnp.exp2(scores - top)
            total = jnp.sum(weights, axis=1, keepdims=True)
            mixed = mm(weights.astype(bf16), v_s[to, cols]) * (1.0 / total)
            mixed_s[at, cols] = one_pair(mixed).astype(bf16)
            sums = top + jnp.log2(total)
            spread = one_pair(jnp.broadcast_to(sums, (2 * TILE, PAIR))).T
            lse_ref[pair, 0:1, at] = spread[0:1]
            lse_ref[pair, 1:2, at] = spread[HDIM : HDIM + 1]

    each_tile(span, q_ref.shape[0], body)
    place(order, mixed_s, mixed_ref, rows, False)


def attend(qkv, segment, span, order, rows):
    length, width = qkv.shape[0], qkv.shape[1] // 3
    pairs = width // PAIR
    small = pl.BlockSpec(memory_space=pltpu.SMEM)
    third = lambda i: pl.BlockSpec((length, width), lambda h: (0, i))
    return pl.pallas_call(
        functools.partial(attend_kernel, rows),
        grid=(1,),
        in_specs=[
            small,
            small,
            pl.BlockSpec((length, 1), lambda h: (0, 0)),
            pl.BlockSpec((1, length), lambda h: (0, 0)),
            third(0),
            third(1),
            third(2),
        ],
        out_specs=[third(0), pl.BlockSpec((pairs, 2, length), lambda h: (0, 0, 0))],
        out_shape=[
            jax.ShapeDtypeStruct((length, width), bf16),
            jax.ShapeDtypeStruct((pairs, 2, length), f32),
        ],
        scratch_shapes=[pltpu.VMEM((length, width), bf16)] * 4,
        compiler_params=pltpu.CompilerParams(vmem_limit_bytes=48 * 1024 * 1024),
        cost_estimate=pl.CostEstimate(
            flops=8 * length * length * width,
            bytes_accessed=8 * length * width,
            transcendentals=2 * pairs * length * length,
        ),
    )(order, span, segment[:, None], segment[None, :], qkv, qkv, qkv)


def attend_back_kernel(
    rows, order, span, seg_c, seg_r, q_ref, k_ref, v_ref, up_ref, lse_ref, dq_ref, dk_ref, dv_ref,
    q_s, k_s, v_s, up_s, dq_s, dk_s, dv_s,
):
    for source, target in ((q_ref, q_s), (k_ref, k_s), (v_ref, v_s), (up_ref, up_s)):
        place(order, source, target, rows, True)
    dk_s[...] = jnp.zeros_like(dk_s)
    dv_s[...] = jnp.zeros_like(dv_s)

    def body(at, to):
        same_item = seg_c[to, :] == seg_r[:, at]
        same_item = jnp.concatenate([same_item, same_item], axis=1)
        for pair in range(q_ref.shape[1] // PAIR):
            cols = slice(pair * PAIR, (pair + 1) * PAIR)
            keys_all = k_s[to, cols]
            queries, upstream = two_heads(q_s[at, cols]), two_heads(up_s[at, cols])
            lse = jnp.concatenate([lse_ref[pair, 0:1, at], lse_ref[pair, 1:2, at]], axis=1)
            scores = mm(keys_all, queries, ((1,), (1,))) * (SCALE * LOG2E)
            probs = jnp.where(same_item, jnp.exp2(scores - lse), 0.0)
            grad_probs = mm(v_s[to, cols], upstream, ((1,), (1,)))
            weighted = probs * grad_probs
            inner = jnp.sum(weighted, axis=0, keepdims=True)
            grad_scores = (weighted - probs * inner).astype(bf16)
            dv_s[to, cols] += mm(probs.astype(bf16), upstream)
            dk_s[to, cols] += mm(grad_scores, queries)
            dq_s[at, cols] = (one_pair(mm(grad_scores, keys_all, ((0,), (0,)))) * SCALE).astype(bf16)

    each_tile(span, q_ref.shape[0], body)
    q_s[...] = (dk_s[...] * SCALE).astype(bf16)
    v_s[...] = dv_s[...].astype(bf16)
    for source, target in ((dq_s, dq_ref), (q_s, dk_ref), (v_s, dv_ref)):
        place(order, source, target, rows, False)


def attend_back(qkv, segment, span, order, rows, grad_mixed, lse):
    length, width = grad_mixed.shape
    pairs = width // PAIR
    small = pl.BlockSpec(memory_space=pltpu.SMEM)
    third = lambda i: pl.BlockSpec((length, width), lambda h: (0, i))
    return pl.pallas_call(
        functools.partial(attend_back_kernel, rows),
        grid=(1,),
        in_specs=[
            small,
            small,
            pl.BlockSpec((length, 1), lambda h: (0, 0)),
            pl.BlockSpec((1, length), lambda h: (0, 0)),
            third(0),
            third(1),
            third(2),
            third(0),
            pl.BlockSpec((pairs, 2, length), lambda h: (0, 0, 0)),
        ],
        out_specs=[third(0)] * 3,
        out_shape=[jax.ShapeDtypeStruct((length, width), bf16)] * 3,
        scratch_shapes=[pltpu.VMEM((length, width), bf16)] * 5 + [pltpu.VMEM((length, width), f32)] * 2,
        compiler_params=pltpu.CompilerParams(vmem_limit_bytes=48 * 1024 * 1024),
        cost_estimate=pl.CostEstimate(
            flops=20 * length * length * width,
            bytes_accessed=16 * length * width,
            transcendentals=2 * pairs * length * length,
        ),
    )(order, span, segment[:, None], segment[None, :], qkv, qkv, qkv, grad_mixed, lse)


def gelu_parts(pre):
    size = jnp.abs(pre)
    t = 1.0 / (1.0 + (0.3275911 * math.sqrt(0.5)) * size)
    bell = jnp.exp2((-0.5 * LOG2E) * (pre * pre))
    poly = t * (0.127414796 + t * (-0.142248368 + t * (0.7107068705 + t * (-0.7265760135 + t * 0.5307027145))))
    below = poly * bell
    below = jnp.where(pre >= 0, 1.0 - below, below)
    return pre * below, below + (pre * bell) * (1.0 / math.sqrt(2.0 * math.pi))


def widen_kernel(chunk, x_ref, w_ref, bias_ref, hidden_ref, slope_ref):
    for at in range(0, x_ref.shape[0], chunk):
        rows = slice(at, at + chunk)
        hidden, slope = gelu_parts(mm(x_ref[rows, :], w_ref[...]) + bias_ref[...])
        hidden_ref[rows, :] = hidden.astype(bf16)
        slope_ref[rows, :] = slope.astype(bf16)


def widen(x, weight, bias):
    count, width = x.shape
    units = weight.shape[1]
    step = 256
    return pl.pallas_call(
        functools.partial(widen_kernel, 144),
        grid=(units // step,),
        in_specs=[
            pl.BlockSpec((count, width), lambda i: (0, 0)),
            pl.BlockSpec((width, step), lambda i: (0, i)),
            pl.BlockSpec((1, step), lambda i: (0, i)),
        ],
        out_specs=[pl.BlockSpec((count, step), lambda i: (0, i))] * 2,
        out_shape=[jax.ShapeDtypeStruct((count, units), bf16)] * 2,
        compiler_params=pltpu.CompilerParams(vmem_limit_bytes=48 * 1024 * 1024),
        cost_estimate=pl.CostEstimate(
            flops=2 * count * width * units,
            bytes_accessed=2 * (width * units + 2 * count * units),
            transcendentals=2 * count * units,
        ),
    )(x, weight, bias[None])


def per_device(
    states,
    cotangent,
    lengths,
    timesteps,
    time_weight,
    time_bias,
    query_weight,
    query_bias,
    key_weight,
    value_weight,
    value_bias,
    out_weight,
    out_bias,
    attn_gain,
    attn_shift,
    ffn_in,
    ffn_in_bias,
    ffn_out,
    ffn_out_bias,
    ffn_gain,
    ffn_shift,
):
    rows, seqs, width = states.shape
    own_count = seqs * rows
    sections, section_at = lax.axis_size("pipe"), lax.axis_index("pipe")
    dp_size, dp_at = lax.axis_size("dp"), lax.axis_index("dp")
    zs_at = lax.axis_index("zs")
    tp_size, tp_at = lax.axis_size("tp"), lax.axis_index("tp")
    length = own_count * tp_size
    part = width // dp_size
    head_cols, unit_cols = query_weight.shape[2], ffn_in.shape[2]
    heads_all, units_all = head_cols * seqs, unit_cols * seqs

    def rotated(array, axis=-1):
        axis = axis % array.ndim
        twice = jnp.concatenate([array, array], axis=axis)
        return lax.dynamic_slice_in_dim(twice, dp_at * part, width, axis)

    def straightened(array):
        twice = jnp.concatenate([array, array], axis=-1)
        back = (dp_size - dp_at) % dp_size
        return lax.dynamic_slice_in_dim(twice, back * part, width, array.ndim - 1)

    vectors = rotated(
        jnp.concatenate(
            [time_weight, time_bias, out_bias, attn_gain, attn_shift, ffn_out_bias, ffn_gain, ffn_shift]
        )
    )
    time_weight, time_bias, out_bias, attn_gain = vectors[0], vectors[1], vectors[2], vectors[3]
    attn_shift, ffn_out_bias, ffn_gain, ffn_shift = vectors[4], vectors[5], vectors[6], vectors[7]


    def to_sequence(array):
        by_seq = rotated(jnp.transpose(array, (1, 0, 2)))
        got = []
        for by in range(seqs):
            block = lax.dynamic_index_in_dim(by_seq, (zs_at - by) % seqs, 0, keepdims=False)
            got.append(received(block, "zs", by))
        return got

    def to_positions(array):
        by_block = straightened(array).reshape(seqs, rows, width)
        got = [received(by_block[(seqs - by) % seqs], "zs", by)[None] for by in range(seqs)]
        twice = jnp.concatenate(got + got)
        by_seq = lax.dynamic_slice_in_dim(twice, (seqs - zs_at) % seqs, seqs, 0)
        return jnp.transpose(by_seq, (1, 0, 2))

    item_ends = jnp.cumsum(lax.dynamic_index_in_dim(lengths, zs_at, 0, keepdims=False))
    own_times = lax.dynamic_index_in_dim(timesteps, zs_at, 0, keepdims=False).astype(f32)
    member = (tp_at + jnp.arange(tp_size, dtype=jnp.int32)) % tp_size
    chips = (zs_at + jnp.arange(seqs, dtype=jnp.int32)) % seqs
    order = (chips[None, :] * tp_size + member[:, None]).reshape(seqs * tp_size).astype(jnp.int32)

    def segment_at(places):
        return jnp.sum((item_ends[None, :] <= places[:, None]).astype(jnp.int32), axis=1)

    segment = segment_at(jnp.arange(length, dtype=jnp.int32))
    span = key_spans(item_ends, length)
    own_places = order[:seqs, None] * rows + jnp.arange(rows, dtype=jnp.int32)[None, :]
    own_segment = segment_at(own_places.reshape(own_count))
    own_pick = own_segment[:, None] == jnp.arange(lengths.shape[1], dtype=jnp.int32)[None, :]
    time_rows = (jnp.sum(jnp.where(own_pick, own_times[None, :], 0.0), axis=1) / STEPS)[:, None]
    aligned = rows % 16 == 0
    kernel_rows = rows if aligned else length
    kernel_order = order if aligned else jnp.zeros((1,), jnp.int32)

    def by_position(array):
        if aligned:
            return array
        blocks = array.reshape(seqs * tp_size, rows, array.shape[1])
        return jnp.take(blocks, jnp.argsort(order), axis=0).reshape(array.shape)

    def by_distance(array):
        if aligned:
            return array
        blocks = array.reshape(seqs * tp_size, rows, array.shape[1])
        return jnp.take(blocks, order, axis=0).reshape(array.shape)


    def over_zs(block, axis, *before):
        mine = lax.dynamic_slice_in_dim(block, dp_at * part, part, axis)
        mine = after(mine, *before)
        return [received(mine, "zs", by) for by in range(1, seqs)]

    def over_dp(pieces):
        return [[received(piece, "dp", other) for other in range(dp_size)] for piece in pieces]

    def assembled(block, axis, pieces, thirds):
        across = 1 - axis
        each = block.shape[across] // thirds
        shape = [0, 0]
        shape[axis], shape[across] = width, block.shape[across] * seqs
        whole = jnp.zeros(shape, block.dtype)

        def put(whole, piece, slot, at):
            for third in range(thirds):
                start = [0, 0]
                start[axis], start[across] = at, (third * seqs + slot) * each
                cut = lax.slice_in_dim(piece, third * each, (third + 1) * each, axis=across)
                whole = lax.dynamic_update_slice(whole, cut, start)
            return whole

        whole = put(whole, rotated(block, axis), 0, 0)
        for slot, row in enumerate(pieces):
            for other, piece in enumerate(row):
                whole = put(whole, piece, slot + 1, other * part)
        return whole

    joined_block = jnp.concatenate([query_weight[0], key_weight[0], value_weight[0]], axis=1)
    biases = jnp.concatenate([query_bias[0], value_bias[0], ffn_in_bias[0].astype(f32)])[None]
    start_pieces = to_sequence(states)
    bias_slots = [received(biases, "zs", by)[0] for by in range(seqs)]
    joined_zs = over_zs(joined_block, 0)
    out_zs = over_zs(out_weight[0], 1, *joined_zs, *start_pieces)
    in_zs = over_zs(ffn_in[0], 0, *out_zs)
    ffn_out_zs = over_zs(ffn_out[0], 1, *in_zs)
    joined = assembled(joined_block, 0, over_dp(joined_zs), 3)
    out_all = assembled(out_weight[0], 1, over_dp(out_zs), 1)
    in_all = assembled(ffn_in[0], 0, over_dp(in_zs), 1)
    ffn_out_all = assembled(ffn_out[0], 1, over_dp(ffn_out_zs), 1)
    query_bias_all = jnp.concatenate([b[:head_cols] for b in bias_slots])
    value_bias_all = jnp.concatenate([b[head_cols : 2 * head_cols] for b in bias_slots])
    in_bias_all = jnp.concatenate([b[2 * head_cols :] for b in bias_slots])
    joined_bias = jnp.concatenate([query_bias_all, jnp.zeros_like(query_bias_all), value_bias_all])

    def everyone(own):
        return jnp.concatenate([received(own, "tp", by) for by in range(tp_size)])

    def returned(full, weight, dims):
        total = 0.0
        for by in range(1, tp_size):
            theirs = mm(full[by * own_count : (by + 1) * own_count], weight, dims).astype(bf16)
            total = total + received(theirs, "tp", -by).astype(f32)
        return total + mm(full[:own_count], weight, dims)

    kept = []
    layer_rows, stat_terms = None, None
    inputs = jnp.concatenate(start_pieces)
    for tick in range(sections):
        residual = inputs.astype(f32) + time_rows * time_weight + time_bias
        rounded_all = everyone(residual.astype(bf16))
        qkv = by_position((mm(rounded_all, joined) + joined_bias).astype(bf16))
        mixed, lse = attend(qkv, segment, span, kernel_order, kernel_rows)
        mixed = by_distance(mixed)
        branch = returned(mixed, out_all, ((1,), (0,))) + out_bias
        first_normed, first_inverse = norm_parts(residual + branch)
        first_out = first_normed * attn_gain + attn_shift
        first_all = everyone(first_out.astype(bf16))
        hidden, slope = widen(first_all, in_all, in_bias_all)
        ffn_branch = returned(hidden, ffn_out_all, ((1,), (0,))) + ffn_out_bias
        second_normed, second_inverse = norm_parts(first_out + ffn_branch)
        layer_y = (second_normed * ffn_gain + ffn_shift).astype(bf16)
        terms = jnp.stack(
            [jnp.sum(residual * residual), jnp.sum(branch * branch), jnp.sum(ffn_branch * ffn_branch)]
        )
        kept.append(
            (
                rounded_all,
                qkv,
                mixed,
                lse,
                first_normed,
                first_inverse,
                first_all,
                hidden,
                slope,
                second_normed,
                second_inverse,
            )
        )
        if tick == 0:
            layer_rows, stat_terms = layer_y, terms
            upstream_pieces = to_sequence(after(cotangent, layer_y))
        else:
            here = section_at == tick
            layer_rows = jnp.where(here, layer_y, layer_rows)
            stat_terms = jnp.where(here, terms, stat_terms)
        if tick + 1 < sections:
            inputs = passed_along(layer_y, "pipe", 1)
    layer_out = to_positions(layer_rows)


    def parts_of(left, right, side):
        found = []
        for other in range(dp_size):
            cut = slice(other * part, (other + 1) * part)
            if side == 0:
                found.append(mm(left[:, cut], right, ((0,), (0,))).astype(bf16))
            else:
                found.append(mm(left, right[:, cut], ((0,), (0,))).astype(bf16))
        return found

    def chosen(found_at, operands):
        if sections == 1:
            return found_at(*operands[0])
        return lax.switch(
            sections - 1 - section_at, [functools.partial(found_at, *each) for each in operands]
        )

    def owned(parts, axis, thirds):
        total = parts[0].astype(f32)
        for other in range(1, dp_size):
            total = total + received(parts[other], "dp", -other).astype(f32)
        each = total.shape[axis] // (seqs * thirds)
        blocks = [
            jnp.concatenate(
                [
                    lax.slice_in_dim(total, (third * seqs + k) * each, (third * seqs + k + 1) * each, axis=axis)
                    for third in range(thirds)
                ],
                axis=axis,
            )
            for k in range(seqs)
        ]
        mine = blocks[0]
        for by in range(1, seqs):
            mine = mine + received(blocks[by].astype(bf16), "zs", -by).astype(f32)
        return mine

    results = None
    upstream_rows = jnp.concatenate(upstream_pieces)
    for_ffn, for_out, for_joined = [], [], []
    for step in range(sections):
        (
            rounded_all,
            qkv,
            mixed,
            lse,
            first_normed,
            first_inverse,
            first_all,
            hidden,
            slope,
            second_normed,
            second_inverse,
        ) = kept[sections - 1 - step]
        last = step + 1 == sections
        upstream = upstream_rows.astype(f32)
        gain_two, shift_two = token_sum(upstream * second_normed), token_sum(upstream)
        grad_second = norm_back(upstream, second_normed, second_inverse, ffn_gain)
        grad_ffn = grad_second.astype(bf16)
        ffn_out_bias_grad = token_sum(grad_ffn)
        grad_ffn_all = everyone(grad_ffn)
        grad_pre = (mm(grad_ffn_all, ffn_out_all, ((1,), (1,))) * slope.astype(f32)).astype(bf16)
        in_bias_sum = token_sum(grad_pre)
        for_ffn.append((hidden, grad_ffn_all, first_all, grad_pre))
        if last:
            ffn_out_parts = chosen(lambda a, b, c, d: parts_of(a, b, 1), for_ffn)
            ffn_in_parts = chosen(lambda a, b, c, d: parts_of(c, d, 0), for_ffn)
            grad_second = after(grad_second, *ffn_out_parts, *ffn_in_parts)
        grad_first = grad_second + returned(grad_pre, in_all, ((1,), (1,)))
        gain_one, shift_one = token_sum(grad_first * first_normed), token_sum(grad_first)
        grad_resid = norm_back(grad_first, first_normed, first_inverse, attn_gain)
        grad_branch = grad_resid.astype(bf16)
        out_bias_grad = token_sum(grad_branch)
        branch_all = everyone(grad_branch)
        grad_mixed = by_position(mm(branch_all, out_all, ((1,), (1,))).astype(bf16))
        for_out.append((mixed, branch_all))
        if last:
            out_parts = chosen(lambda a, b: parts_of(a, b, 1), for_out)
            grad_mixed = after(grad_mixed, *out_parts)
        grads = attend_back(qkv, segment, span, kernel_order, kernel_rows, grad_mixed, lse)
        grad_qkv = jnp.concatenate([by_distance(grad) for grad in grads], axis=1)
        bias_sums = token_sum(grad_qkv)
        for_joined.append((rounded_all, grad_qkv))
        if last:
            joined_parts = chosen(lambda a, b: parts_of(a, b, 0), for_joined)
            grad_resid = after(grad_resid, *joined_parts)
        grad_input = grad_resid + returned(grad_qkv, joined, ((1,), (1,)))
        tw_grad, tb_grad = token_sum(grad_input * time_rows), token_sum(grad_input)
        grad_in = grad_input.astype(bf16)
        slot_sums = jnp.concatenate(
            [
                bias_sums[:heads_all].reshape(seqs, head_cols),
                bias_sums[2 * heads_all :].reshape(seqs, head_cols),
                in_bias_sum.reshape(seqs, unit_cols),
            ],
            axis=1,
        )
        vector_sums = jnp.stack(
            [tw_grad, tb_grad, out_bias_grad, gain_one, shift_one, ffn_out_bias_grad, gain_two, shift_two]
        )
        these = (vector_sums, slot_sums, grad_in)
        if step == 0:
            results = these
        else:
            here = section_at == sections - 1 - step
            results = jax.tree.map(lambda a, b: jnp.where(here, a, b), these, results)
        if not last:
            upstream_rows = passed_along(grad_in, "pipe", -1)
    ffn_out_grad = owned(ffn_out_parts, 0, 1)
    ffn_in_grad = owned(ffn_in_parts, 1, 1)
    out_grad = owned(out_parts, 0, 1)
    joined_grad = owned(joined_parts, 1, 3)
    vector_sums, slot_sums, grad_in = results
    input_grad = to_positions(grad_in)

    stat_row = jnp.concatenate([stat_terms, jnp.zeros((width - 3,), f32)])[None]
    shared = jnp.concatenate([straightened(vector_sums), stat_row])
    shared = summed_over(summed_over(summed_over(shared, "tp"), "zs"), "dp")
    own_slot = slot_sums[0:1]
    for by in range(1, seqs):
        own_slot = own_slot + received(slot_sums[by : by + 1], "zs", -by)
    own_slot = summed_over(own_slot, "dp")
    element_count = float(SEQ_LEN * seqs * dp_size * width)
    stats = jnp.sqrt(shared[8:9, :3] / element_count)
    return (
        layer_out[None],
        input_grad[None],
        shared[0:1],
        shared[1:2],
        joined_grad[None, :, :head_cols],
        own_slot[:, :head_cols],
        joined_grad[None, :, head_cols : 2 * head_cols],
        joined_grad[None, :, 2 * head_cols :],
        own_slot[:, head_cols : 2 * head_cols],
        out_grad[None],
        shared[2:3],
        shared[3:4],
        shared[4:5],
        ffn_in_grad[None],
        own_slot[:, 2 * head_cols :],
        ffn_out_grad[None],
        shared[5:6],
        shared[6:7],
        shared[7:8],
        stats,
    )


def solution(mesh):
    def run(states, *rest):
        sizes = mesh.shape
        seqs = states.shape[1] // sizes["dp"]
        grouped = Mesh(
            mesh.devices.reshape(sizes["pipe"], sizes["dp"], seqs, sizes["tensor"] // seqs),
            ("pipe", "dp", "zs", "tp"),
        )
        return jax.shard_map(
            per_device,
            mesh=grouped,
            in_specs=(
                P(TENSOR, "dp", None),
                P(TENSOR, "dp", None),
                P("dp", None),
                P("dp", None),
                P("pipe", None),
                P("pipe", None),
                P("pipe", None, TENSOR),
                P("pipe", TENSOR),
                P("pipe", None, TENSOR),
                P("pipe", None, TENSOR),
                P("pipe", TENSOR),
                P("pipe", TENSOR, None),
                P("pipe", None),
                P("pipe", None),
                P("pipe", None),
                P("pipe", None, TENSOR),
                P("pipe", TENSOR),
                P("pipe", TENSOR, None),
                P("pipe", None),
                P("pipe", None),
                P("pipe", None),
            ),
            out_specs=(
                P("pipe", TENSOR, "dp", None),
                P("pipe", TENSOR, "dp", None),
                P("pipe", None),
                P("pipe", None),
                P("pipe", "dp", TENSOR),
                P("pipe", TENSOR),
                P("pipe", "dp", TENSOR),
                P("pipe", "dp", TENSOR),
                P("pipe", TENSOR),
                P("pipe", TENSOR, "dp"),
                P("pipe", None),
                P("pipe", None),
                P("pipe", None),
                P("pipe", "dp", TENSOR),
                P("pipe", TENSOR),
                P("pipe", TENSOR, "dp"),
                P("pipe", None),
                P("pipe", None),
                P("pipe", None),
                P("pipe", None),
            ),
            check_vma=False,
        )(states, *rest)

    return run
```

```python
import functools
import math

import jax
import jax.numpy as jnp
from jax import lax
from jax.experimental import pallas as pl
from jax.experimental.pallas import tpu as pltpu
from jax.sharding import Mesh
from jax.sharding import PartitionSpec as P

HDIM = 64
SEQ_LEN = 1152
STEPS = 5000
PAIR = 2 * HDIM
TILE = 128
AHEAD = 2
WIDTHS = (2, 3, 4, 5, 6, 7, 9)
LOG2E = math.log2(math.e)
SCALE = 1.0 / math.sqrt(HDIM)
TENSOR = ("zs", "tp")

epsilon = 1e-05
f32 = jnp.float32
bf16 = jnp.bfloat16


def received(shard, axis, by):
    size = lax.axis_size(axis)
    by = by % size
    if by == 0:
        return shard
    return lax.ppermute(shard, axis, [((i + by) % size, i) for i in range(size)])


def passed_along(shard, axis, by):
    size = lax.axis_size(axis)
    pairs = [(i, i + by) for i in range(size) if 0 <= i + by < size]
    return lax.ppermute(shard, axis, pairs)


def summed_over(values, axis):
    total = values
    for by in range(1, lax.axis_size(axis)):
        total = total + received(values, axis, by)
    return total


def after(value, *others):
    return lax.optimization_barrier((value, *others))[0]


def norm_parts(summed):
    centered = summed - jnp.mean(summed, axis=-1, keepdims=True)
    inverse = lax.rsqrt(jnp.mean(centered * centered, axis=-1, keepdims=True) + epsilon)
    return (centered * inverse, inverse)


def norm_back(upstream, normed, inverse, gain):
    scaled = upstream * gain
    return inverse * (
        scaled
        - jnp.mean(scaled, axis=-1, keepdims=True)
        - normed * jnp.mean(scaled * normed, axis=-1, keepdims=True)
    )


def token_sum(values):
    return jnp.sum(values.astype(f32), axis=0)


def mm(a, b, dims=((1,), (0,))):
    return lax.dot_general(a, b, (dims, ((), ())), preferred_element_type=f32)


def key_spans(item_ends, length):
    tiles = length // TILE
    first = jnp.arange(tiles, dtype=jnp.int32)[:, None] * TILE
    ends = item_ends[None, :]
    start = jnp.max(jnp.where(ends <= first, ends, 0), axis=1) // TILE
    end = jnp.min(jnp.where(ends > first + TILE - 1, ends, length), axis=1)
    need = (end + TILE - 1) // TILE - start
    widths = jnp.array([min(w, tiles) for w in WIDTHS], jnp.int32)
    kind = jnp.sum((widths[None, :] < need[:, None]).astype(jnp.int32), axis=1)
    is_kind = jnp.arange(len(WIDTHS), dtype=jnp.int32)[None, :] == kind[:, None]
    width = jnp.sum(jnp.where(is_kind, widths[None, :], 0), axis=1)
    return jnp.stack([kind, jnp.minimum(start, tiles - width) * TILE]).astype(jnp.int32)


def place(order, source, target, rows, by_position):
    for block in range(source.shape[0] // rows):
        at = pl.ds(pl.multiple_of(order[block] * rows, 16), rows)
        if by_position:
            target[at, :] = source[block * rows : (block + 1) * rows, :]
        else:
            target[block * rows : (block + 1) * rows, :] = source[at, :]


def two_heads(pair):
    first = lax.broadcasted_iota(jnp.int32, pair.shape, 1) < HDIM
    zero = jnp.zeros_like(pair)
    return jnp.concatenate([jnp.where(first, pair, zero), jnp.where(first, zero, pair)], axis=0)


def one_pair(stacked):
    half = stacked.shape[0] // 2
    first = lax.broadcasted_iota(jnp.int32, (half, stacked.shape[1]), 1) < HDIM
    return jnp.where(first, stacked[:half], stacked[half:])


def each_tile(span, length, body):
    tiles = length // TILE

    def step(tile, carry):
        at = pl.ds(pl.multiple_of(tile * TILE, TILE), TILE)

        def branch(width):
            count = min(width, tiles) * TILE
            return lambda: body(at, pl.ds(pl.multiple_of(span[1, tile], TILE), count))

        lax.switch(span[0, tile], [branch(width) for width in WIDTHS])
        return carry

    lax.fori_loop(0, tiles, step, 0)


def attend_kernel(
    rows, order, span, seg_c, seg_r, q_ref, k_ref, v_ref, mixed_ref, lse_ref, q_s, k_s, v_s, mixed_s
):
    for source, target in ((q_ref, q_s), (k_ref, k_s), (v_ref, v_s)):
        place(order, source, target, rows, True)

    def body(at, to):
        same_item = seg_c[at, :] == seg_r[:, to]
        same_item = jnp.concatenate([same_item, same_item], axis=0)
        for pair in range(q_ref.shape[1] // PAIR):
            cols = slice(pair * PAIR, (pair + 1) * PAIR)
            scores = mm(two_heads(q_s[at, cols]), k_s[to, cols], ((1,), (1,))) * (SCALE * LOG2E)
            scores = jnp.where(same_item, scores, -1e30)
            top = jnp.max(scores, axis=1, keepdims=True)
            weights = jnp.exp2(scores - top)
            total = jnp.sum(weights, axis=1, keepdims=True)
            mixed = mm(weights.astype(bf16), v_s[to, cols]) * (1.0 / total)
            mixed_s[at, cols] = one_pair(mixed).astype(bf16)
            sums = top + jnp.log2(total)
            spread = one_pair(jnp.broadcast_to(sums, (2 * TILE, PAIR))).T
            lse_ref[pair, 0:1, at] = spread[0:1]
            lse_ref[pair, 1:2, at] = spread[HDIM : HDIM + 1]

    each_tile(span, q_ref.shape[0], body)
    place(order, mixed_s, mixed_ref, rows, False)


def attend(qkv, segment, span, order, rows):
    length, width = qkv.shape[0], qkv.shape[1] // 3
    pairs = width // PAIR
    small = pl.BlockSpec(memory_space=pltpu.SMEM)
    third = lambda i: pl.BlockSpec((length, width), lambda h: (0, i))
    return pl.pallas_call(
        functools.partial(attend_kernel, rows),
        grid=(1,),
        in_specs=[
            small,
            small,
            pl.BlockSpec((length, 1), lambda h: (0, 0)),
            pl.BlockSpec((1, length), lambda h: (0, 0)),
            third(0),
            third(1),
            third(2),
        ],
        out_specs=[third(0), pl.BlockSpec((pairs, 2, length), lambda h: (0, 0, 0))],
        out_shape=[
            jax.ShapeDtypeStruct((length, width), bf16),
            jax.ShapeDtypeStruct((pairs, 2, length), f32),
        ],
        scratch_shapes=[pltpu.VMEM((length, width), bf16)] * 4,
        compiler_params=pltpu.CompilerParams(vmem_limit_bytes=48 * 1024 * 1024),
        cost_estimate=pl.CostEstimate(flops=0, bytes_accessed=0, transcendentals=0),
    )(order, span, segment[:, None], segment[None, :], qkv, qkv, qkv)


def attend_back_kernel(
    rows, order, span, seg_c, seg_r, q_ref, k_ref, v_ref, up_ref, lse_ref, dq_ref, dk_ref, dv_ref,
    q_s, k_s, v_s, up_s, dq_s, dk_s, dv_s,
):
    for source, target in ((q_ref, q_s), (k_ref, k_s), (v_ref, v_s), (up_ref, up_s)):
        place(order, source, target, rows, True)
    dk_s[...] = jnp.zeros_like(dk_s)
    dv_s[...] = jnp.zeros_like(dv_s)

    def body(at, to):
        same_item = seg_c[to, :] == seg_r[:, at]
        same_item = jnp.concatenate([same_item, same_item], axis=1)
        for pair in range(q_ref.shape[1] // PAIR):
            cols = slice(pair * PAIR, (pair + 1) * PAIR)
            keys_all = k_s[to, cols]
            queries, upstream = two_heads(q_s[at, cols]), two_heads(up_s[at, cols])
            lse = jnp.concatenate([lse_ref[pair, 0:1, at], lse_ref[pair, 1:2, at]], axis=1)
            scores = mm(keys_all, queries, ((1,), (1,))) * (SCALE * LOG2E)
            probs = jnp.where(same_item, jnp.exp2(scores - lse), 0.0)
            grad_probs = mm(v_s[to, cols], upstream, ((1,), (1,)))
            weighted = probs * grad_probs
            inner = jnp.sum(weighted, axis=0, keepdims=True)
            grad_scores = (weighted - probs * inner).astype(bf16)
            dv_s[to, cols] += mm(probs.astype(bf16), upstream)
            dk_s[to, cols] += mm(grad_scores, queries)
            dq_s[at, cols] = (one_pair(mm(grad_scores, keys_all, ((0,), (0,)))) * SCALE).astype(bf16)

    each_tile(span, q_ref.shape[0], body)
    q_s[...] = (dk_s[...] * SCALE).astype(bf16)
    v_s[...] = dv_s[...].astype(bf16)
    for source, target in ((dq_s, dq_ref), (q_s, dk_ref), (v_s, dv_ref)):
        place(order, source, target, rows, False)


def attend_back(qkv, segment, span, order, rows, grad_mixed, lse):
    length, width = grad_mixed.shape
    pairs = width // PAIR
    small = pl.BlockSpec(memory_space=pltpu.SMEM)
    third = lambda i: pl.BlockSpec((length, width), lambda h: (0, i))
    return pl.pallas_call(
        functools.partial(attend_back_kernel, rows),
        grid=(1,),
        in_specs=[
            small,
            small,
            pl.BlockSpec((length, 1), lambda h: (0, 0)),
            pl.BlockSpec((1, length), lambda h: (0, 0)),
            third(0),
            third(1),
            third(2),
            third(0),
            pl.BlockSpec((pairs, 2, length), lambda h: (0, 0, 0)),
        ],
        out_specs=[third(0)] * 3,
        out_shape=[jax.ShapeDtypeStruct((length, width), bf16)] * 3,
        scratch_shapes=[pltpu.VMEM((length, width), bf16)] * 5 + [pltpu.VMEM((length, width), f32)] * 2,
        compiler_params=pltpu.CompilerParams(vmem_limit_bytes=48 * 1024 * 1024),
        cost_estimate=pl.CostEstimate(flops=0, bytes_accessed=0, transcendentals=0),
    )(order, span, segment[:, None], segment[None, :], qkv, qkv, qkv, grad_mixed, lse)


def gelu_parts(pre):
    size = jnp.abs(pre)
    t = 1.0 / (1.0 + (0.3275911 * math.sqrt(0.5)) * size)
    bell = jnp.exp2((-0.5 * LOG2E) * (pre * pre))
    poly = t * (0.127414796 + t * (-0.142248368 + t * (0.7107068705 + t * (-0.7265760135 + t * 0.5307027145))))
    below = poly * bell
    below = jnp.where(pre >= 0, 1.0 - below, below)
    return pre * below, below + (pre * bell) * (1.0 / math.sqrt(2.0 * math.pi))


def widen_kernel(chunk, x_ref, w_ref, bias_ref, hidden_ref, slope_ref):
    for at in range(0, x_ref.shape[0], chunk):
        rows = slice(at, at + chunk)
        hidden, slope = gelu_parts(mm(x_ref[rows, :], w_ref[...]) + bias_ref[...])
        hidden_ref[rows, :] = hidden.astype(bf16)
        slope_ref[rows, :] = slope.astype(bf16)


def widen(x, weight, bias):
    count, width = x.shape
    units = weight.shape[1]
    step = 256
    return pl.pallas_call(
        functools.partial(widen_kernel, 144),
        grid=(units // step,),
        in_specs=[
            pl.BlockSpec((count, width), lambda i: (0, 0)),
            pl.BlockSpec((width, step), lambda i: (0, i)),
            pl.BlockSpec((1, step), lambda i: (0, i)),
        ],
        out_specs=[pl.BlockSpec((count, step), lambda i: (0, i))] * 2,
        out_shape=[jax.ShapeDtypeStruct((count, units), bf16)] * 2,
        compiler_params=pltpu.CompilerParams(vmem_limit_bytes=48 * 1024 * 1024),
        cost_estimate=pl.CostEstimate(flops=0, bytes_accessed=0, transcendentals=0),
    )(x, weight, bias[None])


def gather_kernel(seqs, dp_size, *refs):
    seq_ref, bias_ref = refs[:2]
    blocks = refs[2:8]
    start_ref, biases_ref, joined_ref, out_ref, in_ref, ffn_out_ref = refs[8:14]
    local_sem, seq_send, seq_get, up_send, up_get, down_send, down_get, side_send, side_get = refs[14:]
    zs, dp = lax.axis_index("zs"), lax.axis_index("dp")
    width, hc = blocks[0].shape
    units = blocks[4].shape[1]
    part = width // dp_size
    half = units // 2
    table = [(0, 0, hc), (1, 0, hc), (2, 0, hc), (3, 0, hc)]
    table += [(4, 0, half), (4, half, half), (5, 0, half), (5, half, half)]
    kinds = range(len(table))

    def home(kind, slot, other):
        array, first, size = table[kind]
        features = slice(other * part, (other + 1) * part)
        if array < 3:
            at = (array * seqs + slot) * hc
            return joined_ref.at[features, at : at + hc]
        if array == 3:
            return out_ref.at[slot * hc : (slot + 1) * hc, features]
        at = slice(slot * units + first, slot * units + first + size)
        return in_ref.at[features, at] if array == 4 else ffn_out_ref.at[at, features]

    def own(kind, other):
        array, first, size = table[kind]
        features = pl.ds(pl.multiple_of(lax.rem(dp + other, dp_size) * part, part), part)
        if array in (3, 5):
            return blocks[array].at[first : first + size, features]
        return blocks[array].at[features, first : first + size]

    def to(axis, at, source, target, send, get):
        return pltpu.make_async_remote_copy(
            src_ref=source,
            dst_ref=target,
            send_sem=send,
            recv_sem=get,
            device_id={axis: at},
            device_id_type=pl.DeviceIdType.MESH,
        )

    def sequence(by):
        at = lax.rem(zs - by + seqs, seqs)
        return to("zs", at, seq_ref.at[at], start_ref.at[by], seq_send.at[by], seq_get.at[by])

    def bias(by):
        at = lax.rem(zs - by + seqs, seqs)
        return to("zs", at, bias_ref, biases_ref.at[by], seq_send.at[seqs + by], seq_get.at[seqs + by])

    def up(kind, hop):
        source = own(kind, 0) if hop == 0 else home(kind, seqs - hop, 0)
        target = home(kind, seqs - hop - 1, 0)
        return to("zs", zs + 1, source, target, up_send.at[kind, hop], up_get.at[kind, hop])

    def down(kind, hop):
        source = own(kind, 0) if hop == 0 else home(kind, hop, 0)
        target = home(kind, hop + 1, 0)
        return to("zs", zs - 1, source, target, down_send.at[kind, hop], down_get.at[kind, hop])

    def side(kind, slot, other):
        at = lax.rem(dp - other + dp_size, dp_size)
        place = side_send.at[kind, slot, other], side_get.at[kind, slot, other]
        return to("dp", at, home(kind, slot, 0), home(kind, slot, other), *place)

    def local(kind, other):
        return pltpu.make_async_copy(own(kind, other), home(kind, 0, other), local_sem.at[kind, other])

    barrier = pltpu.get_barrier_semaphore()
    for axis, at, size in (("zs", zs, seqs), ("dp", dp, dp_size)):
        for by in range(1, size):
            pl.semaphore_signal(
                barrier,
                inc=1,
                device_id={axis: lax.rem(at + by, size)},
                device_id_type=pl.DeviceIdType.MESH,
            )
    pl.semaphore_wait(barrier, seqs + dp_size - 2)

    for by in range(1, seqs):
        sequence(by).start()
        bias(by).start()
    def begin(kind):
        @pl.when(zs < seqs - 1)
        def _():
            up(kind, 0).start()

        @pl.when(zs > 0)
        def _():
            down(kind, 0).start()

    for kind in kinds[:AHEAD]:
        begin(kind)

    own_seq = pltpu.make_async_copy(seq_ref.at[zs], start_ref.at[0], local_sem.at[len(table), 0])
    own_bias = pltpu.make_async_copy(bias_ref, biases_ref.at[0], local_sem.at[len(table), 1])
    own_seq.start()
    own_bias.start()
    for kind in kinds:
        for other in range(dp_size):
            local(kind, other).start()

    def pass_on(kind, hop):
        @pl.when(zs >= hop)
        def _():
            up(kind, hop - 1).wait_recv()
            if hop < seqs - 1:

                @pl.when(zs < seqs - 1)
                def _():
                    up(kind, hop).start()

            for other in range(1, dp_size):
                side(kind, seqs - hop, other).start()

        @pl.when(zs + hop < seqs)
        def _():
            down(kind, hop - 1).wait_recv()
            if hop < seqs - 1:

                @pl.when(zs > 0)
                def _():
                    down(kind, hop).start()

            for other in range(1, dp_size):
                side(kind, hop, other).start()

    for step in range(len(kinds) + seqs - 2):
        for hop in range(1, seqs):
            if 0 <= step - hop + 1 < len(kinds):
                pass_on(step - hop + 1, hop)
        if step + AHEAD < len(kinds):
            begin(step + AHEAD)

    own_seq.wait()
    own_bias.wait()
    for by in range(1, seqs):
        sequence(by).wait()
        bias(by).wait()
    for kind in kinds:
        for other in range(dp_size):
            local(kind, other).wait()
        for slot in range(1, seqs):
            for other in range(1, dp_size):
                side(kind, slot, other).wait()
        for hop in range(seqs - 1):

            @pl.when((zs >= hop) & (zs < seqs - 1))
            def _():
                up(kind, hop).wait_send()

            @pl.when((zs + hop < seqs) & (zs > 0))
            def _():
                down(kind, hop).wait_send()


def gather_all(by_seq, biases, blocks, dp_size):
    seqs, _, width = by_seq.shape
    hc, units = blocks[0].shape[1], blocks[4].shape[1]
    anywhere = pl.BlockSpec(memory_space=pl.ANY)
    low = lambda *shape: jax.ShapeDtypeStruct(shape, bf16)
    dma = pltpu.SemaphoreType.DMA
    kinds = 8
    return pl.pallas_call(
        functools.partial(gather_kernel, seqs, dp_size),
        in_specs=[anywhere] * (2 + len(blocks)),
        out_specs=[anywhere] * 6,
        out_shape=[
            jax.ShapeDtypeStruct(by_seq.shape, bf16),
            jax.ShapeDtypeStruct((seqs,) + biases.shape, f32),
            low(width, 3 * seqs * hc),
            low(seqs * hc, width),
            low(width, seqs * units),
            low(seqs * units, width),
        ],
        scratch_shapes=[
            dma((kinds + 1, max(dp_size, 2))),
            dma((2 * seqs,)),
            dma((2 * seqs,)),
            dma((kinds, seqs - 1)),
            dma((kinds, seqs - 1)),
            dma((kinds, seqs - 1)),
            dma((kinds, seqs - 1)),
            dma((kinds, seqs, dp_size)),
            dma((kinds, seqs, dp_size)),
        ],
        compiler_params=pltpu.CompilerParams(collective_id=0, has_side_effects=True),
    )(by_seq, biases, *blocks)


def scatter_kernel(seqs, dp_size, tp_size, *refs):
    seq_ref, small_ref, slots_ref = refs[:3]
    mine, theirs = refs[3:7], refs[7:11]
    seq_out, small_out, slots_out = refs[11:14]
    outs = refs[14:20]
    sides, ups, downs = refs[20:24], refs[24:28], refs[28:32]
    small_zs, small_all, slots_zs, slots_dp = refs[32:36]
    seq_send, seq_get, local_sem, small_send, small_get = refs[36:41]
    side_send, side_get, up_send, up_get, down_send, down_get = refs[41:47]
    zs, dp, tp = lax.axis_index("zs"), lax.axis_index("dp"), lax.axis_index("tp")
    units = mine[0].shape[0] // seqs
    hc = mine[2].shape[0] // seqs
    half = units // 2
    kinds = [(0, 0, 0, half), (0, 0, half, half), (1, 1, 0, half), (1, 1, half, half), (2, 0, 0, hc)]
    kinds += [(3, 1, third * seqs * hc, hc) for third in range(3)]

    def cut(arrays, kind, slot):
        array, axis, first, size = kinds[kind]
        apart = units if array < 2 else hc
        at = slice(first + slot * apart, first + slot * apart + size)
        return arrays[array].at[at, :] if axis == 0 else arrays[array].at[:, at]

    def to(where, source, target, send, get):
        return pltpu.make_async_remote_copy(
            src_ref=source,
            dst_ref=target,
            send_sem=send,
            recv_sem=get,
            device_id=where,
            device_id_type=pl.DeviceIdType.MESH,
        )

    def sequence(by):
        at = lax.rem(zs + by, seqs)
        return to({"zs": at}, seq_ref.at[by], seq_out.at[by], seq_send.at[by], seq_get.at[by])

    def side(kind, slot):
        place = side_send.at[kind, slot], side_get.at[kind, slot]
        return to({"dp": 1 - dp}, cut(theirs, kind, slot), cut(sides, kind, slot), *place)

    def up(kind, far):
        place = up_send.at[kind, far], up_get.at[kind, far]
        return to({"zs": zs + 1}, cut(sides, kind, far), cut(ups, kind, far - 1), *place)

    def down(kind, far):
        place = down_send.at[kind, far], down_get.at[kind, far]
        return to({"zs": zs - 1}, cut(sides, kind, seqs - far), cut(downs, kind, far - 1), *place)

    def small(by):
        at = {"zs": lax.rem(zs + by, seqs)}
        return to(at, small_ref, small_zs.at[by], small_send.at[0, by], small_get.at[0, by])

    def slots(by):
        at = {"zs": lax.rem(zs + by, seqs)}
        return to(at, slots_ref.at[by], slots_zs.at[by], small_send.at[1, by], small_get.at[1, by])

    def small_across(by):
        at = lax.rem(dp * tp_size + tp + by, dp_size * tp_size)
        where = {"dp": lax.div(at, tp_size), "tp": lax.rem(at, tp_size)}
        return to(where, small_all.at[0], small_all.at[by], small_send.at[2, by], small_get.at[2, by])

    def slots_across():
        return to({"dp": 1 - dp}, slots_dp.at[0], slots_dp.at[1], small_send.at[3, 0], small_get.at[3, 0])

    def added(target, *others):
        rows = target.shape[0]
        step = 64

        def body(i, carry):
            at = pl.ds(pl.multiple_of(i * step, step), step)
            total = target[at, :].astype(f32)
            for other in others:
                total = total + other[at, :].astype(f32)
            target[at, :] = total.astype(target.dtype)
            return carry

        lax.fori_loop(0, rows // step, body, 0)

    barrier = pltpu.get_barrier_semaphore()
    greeted = [{"zs": lax.rem(zs + by, seqs)} for by in range(1, seqs)]
    for by in range(1, dp_size * tp_size):
        at = lax.rem(dp * tp_size + tp + by, dp_size * tp_size)
        greeted.append({"dp": lax.div(at, tp_size), "tp": lax.rem(at, tp_size)})
    for where in greeted:
        pl.semaphore_signal(barrier, inc=1, device_id=where, device_id_type=pl.DeviceIdType.MESH)
    pl.semaphore_wait(barrier, len(greeted))

    slot_order = list(range(1, seqs)) + [0]

    def begin(kind):
        for slot in slot_order:
            side(kind, slot).start()

    for kind in range(AHEAD):
        begin(kind)
    for by in range(1, seqs):
        small(by).start()
        slots(by).start()
    for by in range(1, seqs):
        sequence(by).start()
    own_seq = pltpu.make_async_copy(seq_ref.at[0], seq_out.at[0], local_sem.at[0])
    own_seq.start()

    total, slot_total = small_ref[...], slots_ref[0]
    for by in range(1, seqs):
        small(by).wait()
        slots(by).wait()
        total = total + small_zs[by]
        slot_total = slot_total + slots_zs[by]
    small_all[0] = total
    slots_dp[0] = slot_total
    for by in range(1, dp_size * tp_size):
        small_across(by).start()
    slots_across().start()

    def taken(kind):
        for slot in slot_order:
            side(kind, slot).wait()
            added(cut(sides, kind, slot), cut(mine, kind, slot))

    def pass_on(kind, hop):
        @pl.when((zs == hop) & (zs < seqs - 1))
        def _():
            for far in range(seqs - 1 - hop, 0, -1):
                if hop > 0:
                    up(kind, far + 1).wait_recv()
                    added(cut(sides, kind, far), cut(ups, kind, far))
                up(kind, far).start()

        @pl.when((zs == seqs - 1 - hop) & (zs > 0))
        def _():
            for far in range(seqs - 1 - hop, 0, -1):
                if hop > 0:
                    down(kind, far + 1).wait_recv()
                    added(cut(sides, kind, seqs - far), cut(downs, kind, far))
                down(kind, far).start()

    for step in range(len(kinds) + seqs - 2):
        if step < len(kinds):
            taken(step)
            if step + AHEAD < len(kinds):
                begin(step + AHEAD)
        for hop in range(seqs - 1):
            if 0 <= step - hop < len(kinds):
                pass_on(step - hop, hop)

    for by in range(1, dp_size * tp_size):
        small_across(by).wait()
        total = total + small_all[by]
    slots_across().wait()
    small_out[...] = total
    slots_out[...] = slot_total + slots_dp[1]

    for kind, (array, axis, first, size) in enumerate(kinds):
        out = outs[array] if array < 3 else outs[3 + first // (seqs * hc)]
        if array < 2:
            out = out.at[first : first + size, :] if axis == 0 else out.at[:, first : first + size]
        out[...] = cut(sides, kind, 0)[...].astype(f32)

        @pl.when(zs > 0)
        def _():
            up(kind, 1).wait_recv()
            added(out, cut(ups, kind, 0))

        @pl.when(zs < seqs - 1)
        def _():
            down(kind, 1).wait_recv()
            added(out, cut(downs, kind, 0))

        for far in range(1, seqs):

            @pl.when(zs + far < seqs)
            def _():
                up(kind, far).wait_send()

            @pl.when(zs >= far)
            def _():
                down(kind, far).wait_send()

    own_seq.wait()
    for by in range(1, seqs):
        sequence(by).wait()


def scatter_all(by_block, small, slots, mine, theirs, tp_size):
    seqs = by_block.shape[0]
    units, part = mine[0].shape[0] // seqs, mine[0].shape[1]
    hc = mine[2].shape[0] // seqs
    dp_size = 2
    anywhere = pl.BlockSpec(memory_space=pl.ANY)
    inside = pl.BlockSpec(memory_space=pltpu.VMEM)
    wide = lambda *shape: jax.ShapeDtypeStruct(shape, f32)
    dma = pltpu.SemaphoreType.DMA
    like = [pltpu.VMEM(block.shape, bf16) for block in mine]
    kinds = 8
    return pl.pallas_call(
        functools.partial(scatter_kernel, seqs, dp_size, tp_size),
        in_specs=[anywhere, inside, inside] + [inside] * 4 + [anywhere] * 4,
        out_specs=[anywhere] + [inside] * 8,
        out_shape=[
            jax.ShapeDtypeStruct(by_block.shape, bf16),
            wide(*small.shape),
            wide(*slots.shape[1:]),
            wide(units, part),
            wide(part, units),
            wide(hc, part),
            wide(part, hc),
            wide(part, hc),
            wide(part, hc),
        ],
        scratch_shapes=like * 3
        + [
            pltpu.VMEM((seqs,) + small.shape, f32),
            pltpu.VMEM((dp_size * tp_size,) + small.shape, f32),
            pltpu.VMEM(slots.shape, f32),
            pltpu.VMEM((2,) + slots.shape[1:], f32),
            dma((seqs,)),
            dma((seqs,)),
            dma((1,)),
            dma((4, max(seqs, dp_size * tp_size))),
            dma((4, max(seqs, dp_size * tp_size))),
        ]
        + [dma((kinds, seqs))] * 6,
        input_output_aliases={},
        compiler_params=pltpu.CompilerParams(
            collective_id=1, has_side_effects=True, vmem_limit_bytes=56 * 1024 * 1024
        ),
    )(by_block, small, slots, *mine, *theirs)


def per_device(
    states,
    cotangent,
    lengths,
    timesteps,
    time_weight,
    time_bias,
    query_weight,
    query_bias,
    key_weight,
    value_weight,
    value_bias,
    out_weight,
    out_bias,
    attn_gain,
    attn_shift,
    ffn_in,
    ffn_in_bias,
    ffn_out,
    ffn_out_bias,
    ffn_gain,
    ffn_shift,
):
    rows, seqs, width = states.shape
    own_count = seqs * rows
    sections, section_at = lax.axis_size("pipe"), lax.axis_index("pipe")
    dp_size, dp_at = lax.axis_size("dp"), lax.axis_index("dp")
    zs_at = lax.axis_index("zs")
    tp_size, tp_at = lax.axis_size("tp"), lax.axis_index("tp")
    length = own_count * tp_size
    part = width // dp_size
    head_cols, unit_cols = query_weight.shape[2], ffn_in.shape[2]
    heads_all, units_all = head_cols * seqs, unit_cols * seqs

    def rotated(array, axis=-1):
        axis = axis % array.ndim
        twice = jnp.concatenate([array, array], axis=axis)
        return lax.dynamic_slice_in_dim(twice, dp_at * part, width, axis)

    def straightened(array):
        twice = jnp.concatenate([array, array], axis=-1)
        back = (dp_size - dp_at) % dp_size
        return lax.dynamic_slice_in_dim(twice, back * part, width, array.ndim - 1)

    vectors = rotated(
        jnp.concatenate(
            [time_weight, time_bias, out_bias, attn_gain, attn_shift, ffn_out_bias, ffn_gain, ffn_shift]
        )
    )
    time_weight, time_bias, out_bias, attn_gain = vectors[0], vectors[1], vectors[2], vectors[3]
    attn_shift, ffn_out_bias, ffn_gain, ffn_shift = vectors[4], vectors[5], vectors[6], vectors[7]


    def to_sequence(array):
        by_seq = rotated(jnp.transpose(array, (1, 0, 2)))
        got = []
        for by in range(seqs):
            block = lax.dynamic_index_in_dim(by_seq, (zs_at - by) % seqs, 0, keepdims=False)
            got.append(received(block, "zs", by))
        return got

    def to_positions(array):
        by_block = straightened(array).reshape(seqs, rows, width)
        return [received(by_block[(seqs - by) % seqs], "zs", by)[None] for by in range(seqs)]

    def in_positions(got, *before):
        got = [after(piece, *before) for piece in got]
        twice = jnp.concatenate(got + got)
        by_seq = lax.dynamic_slice_in_dim(twice, (seqs - zs_at) % seqs, seqs, 0)
        return jnp.transpose(by_seq, (1, 0, 2))

    item_ends = jnp.cumsum(lax.dynamic_index_in_dim(lengths, zs_at, 0, keepdims=False))
    own_times = lax.dynamic_index_in_dim(timesteps, zs_at, 0, keepdims=False).astype(f32)
    member = (tp_at + jnp.arange(tp_size, dtype=jnp.int32)) % tp_size
    chips = (zs_at + jnp.arange(seqs, dtype=jnp.int32)) % seqs
    order = (chips[None, :] * tp_size + member[:, None]).reshape(seqs * tp_size).astype(jnp.int32)

    def segment_at(places):
        return jnp.sum((item_ends[None, :] <= places[:, None]).astype(jnp.int32), axis=1)

    segment = segment_at(jnp.arange(length, dtype=jnp.int32))
    span = key_spans(item_ends, length)
    own_places = order[:seqs, None] * rows + jnp.arange(rows, dtype=jnp.int32)[None, :]
    own_segment = segment_at(own_places.reshape(own_count))
    own_pick = own_segment[:, None] == jnp.arange(lengths.shape[1], dtype=jnp.int32)[None, :]
    time_rows = (jnp.sum(jnp.where(own_pick, own_times[None, :], 0.0), axis=1) / STEPS)[:, None]
    aligned = rows % 16 == 0
    kernel_rows = rows if aligned else length
    kernel_order = order if aligned else jnp.zeros((1,), jnp.int32)

    def by_position(array):
        if aligned:
            return array
        blocks = array.reshape(seqs * tp_size, rows, array.shape[1])
        return jnp.take(blocks, jnp.argsort(order), axis=0).reshape(array.shape)

    def by_distance(array):
        if aligned:
            return array
        blocks = array.reshape(seqs * tp_size, rows, array.shape[1])
        return jnp.take(blocks, order, axis=0).reshape(array.shape)


    def over_zs(block, axis, *before):
        mine = lax.dynamic_slice_in_dim(block, dp_at * part, part, axis)
        mine = after(mine, *before)
        return [received(mine, "zs", by) for by in range(1, seqs)]

    def over_dp(pieces):
        return [[received(piece, "dp", other) for other in range(dp_size)] for piece in pieces]

    def assembled(block, axis, pieces, thirds):
        across = 1 - axis
        each = block.shape[across] // thirds
        shape = [0, 0]
        shape[axis], shape[across] = width, block.shape[across] * seqs
        whole = jnp.zeros(shape, block.dtype)

        def put(whole, piece, slot, at):
            for third in range(thirds):
                start = [0, 0]
                start[axis], start[across] = at, (third * seqs + slot) * each
                cut = lax.slice_in_dim(piece, third * each, (third + 1) * each, axis=across)
                whole = lax.dynamic_update_slice(whole, cut, start)
            return whole

        whole = put(whole, rotated(block, axis), 0, 0)
        for slot, row in enumerate(pieces):
            for other, piece in enumerate(row):
                whole = put(whole, piece, slot + 1, other * part)
        return whole

    biases = jnp.concatenate([query_bias[0], value_bias[0], ffn_in_bias[0].astype(f32)])[None]
    in_kernels = dp_size == 2 and head_cols % 128 == 0 and part % 128 == 0 and unit_cols % 128 == 0
    if in_kernels:
        by_seq = rotated(jnp.transpose(states, (1, 0, 2)))
        blocks = (query_weight, key_weight, value_weight, out_weight, ffn_in, ffn_out)
        start, bias_slots, joined, out_all, in_all, ffn_out_all = gather_all(
            by_seq, biases, [block[0] for block in blocks], dp_size
        )
        start_rows = start.reshape(own_count, width)
        bias_slots = bias_slots[:, 0]
    else:
        joined_block = jnp.concatenate([query_weight[0], key_weight[0], value_weight[0]], axis=1)
        start_pieces = to_sequence(states)
        start_rows = jnp.concatenate(start_pieces)
        bias_slots = [received(biases, "zs", by)[0] for by in range(seqs)]
        joined_zs = over_zs(joined_block, 0)
        out_zs = over_zs(out_weight[0], 1, *joined_zs, *start_pieces)
        in_zs = over_zs(ffn_in[0], 0, *out_zs)
        ffn_out_zs = over_zs(ffn_out[0], 1, *in_zs)
        joined = assembled(joined_block, 0, over_dp(joined_zs), 3)
        out_all = assembled(out_weight[0], 1, over_dp(out_zs), 1)
        in_all = assembled(ffn_in[0], 0, over_dp(in_zs), 1)
        ffn_out_all = assembled(ffn_out[0], 1, over_dp(ffn_out_zs), 1)
    query_bias_all = jnp.concatenate([b[:head_cols] for b in bias_slots])
    value_bias_all = jnp.concatenate([b[head_cols : 2 * head_cols] for b in bias_slots])
    in_bias_all = jnp.concatenate([b[2 * head_cols :] for b in bias_slots])
    joined_bias = jnp.concatenate([query_bias_all, jnp.zeros_like(query_bias_all), value_bias_all])

    def everyone(own):
        return jnp.concatenate([received(own, "tp", by) for by in range(tp_size)])

    def returned(full, weight, dims):
        total = 0.0
        for by in range(1, tp_size):
            theirs = mm(full[by * own_count : (by + 1) * own_count], weight, dims).astype(bf16)
            total = total + received(theirs, "tp", -by).astype(f32)
        return total + mm(full[:own_count], weight, dims)

    kept = []
    layer_rows, stat_terms = None, None
    inputs = start_rows
    for tick in range(sections):
        residual = inputs.astype(f32) + time_rows * time_weight + time_bias
        rounded_all = everyone(residual.astype(bf16))
        qkv = by_position((mm(rounded_all, joined) + joined_bias).astype(bf16))
        mixed, lse = attend(qkv, segment, span, kernel_order, kernel_rows)
        if tick == 1:
            mixed = after(mixed, *upstream_pieces)
        mixed = by_distance(mixed)
        branch = returned(mixed, out_all, ((1,), (0,))) + out_bias
        first_normed, first_inverse = norm_parts(residual + branch)
        first_out = first_normed * attn_gain + attn_shift
        first_all = everyone(first_out.astype(bf16))
        hidden, slope = widen(first_all, in_all, in_bias_all)
        ffn_branch = returned(hidden, ffn_out_all, ((1,), (0,))) + ffn_out_bias
        second_normed, second_inverse = norm_parts(first_out + ffn_branch)
        layer_y = (second_normed * ffn_gain + ffn_shift).astype(bf16)
        terms = jnp.stack(
            [jnp.sum(residual * residual), jnp.sum(branch * branch), jnp.sum(ffn_branch * ffn_branch)]
        )
        kept.append(
            (
                rounded_all,
                qkv,
                mixed,
                lse,
                first_normed,
                first_inverse,
                first_all,
                hidden,
                slope,
                second_normed,
                second_inverse,
            )
        )
        if tick == 0:
            layer_rows, stat_terms = layer_y, terms
            upstream_pieces = to_sequence(after(cotangent, layer_y))
        else:
            here = section_at == tick
            layer_rows = jnp.where(here, layer_y, layer_rows)
            stat_terms = jnp.where(here, terms, stat_terms)
        if tick + 1 < sections:
            inputs = passed_along(layer_y, "pipe", 1)
    layer_pieces = to_positions(layer_rows)


    def parts_of(left, right, side):
        found = []
        for other in range(dp_size):
            cut = slice(other * part, (other + 1) * part)
            if side == 0:
                found.append(mm(left[:, cut], right, ((0,), (0,))).astype(bf16))
            else:
                found.append(mm(left, right[:, cut], ((0,), (0,))).astype(bf16))
        return found

    def chosen(found_at, operands):
        if sections == 1:
            return found_at(*operands[0])
        return lax.switch(
            sections - 1 - section_at, [functools.partial(found_at, *each) for each in operands]
        )

    def owned(parts, axis, thirds):
        total = parts[0].astype(f32)
        for other in range(1, dp_size):
            total = total + received(parts[other], "dp", -other).astype(f32)
        each = total.shape[axis] // (seqs * thirds)
        blocks = [
            jnp.concatenate(
                [
                    lax.slice_in_dim(total, (third * seqs + k) * each, (third * seqs + k + 1) * each, axis=axis)
                    for third in range(thirds)
                ],
                axis=axis,
            )
            for k in range(seqs)
        ]
        mine = blocks[0]
        for by in range(1, seqs):
            mine = mine + received(blocks[by].astype(bf16), "zs", -by).astype(f32)
        return mine

    results = None
    upstream_rows = jnp.concatenate(upstream_pieces)
    for_ffn, for_out, for_joined = [], [], []
    for step in range(sections):
        (
            rounded_all,
            qkv,
            mixed,
            lse,
            first_normed,
            first_inverse,
            first_all,
            hidden,
            slope,
            second_normed,
            second_inverse,
        ) = kept[sections - 1 - step]
        last = step + 1 == sections
        upstream = upstream_rows.astype(f32)
        gain_two, shift_two = token_sum(upstream * second_normed), token_sum(upstream)
        grad_second = norm_back(upstream, second_normed, second_inverse, ffn_gain)
        grad_ffn = grad_second.astype(bf16)
        ffn_out_bias_grad = token_sum(grad_ffn)
        grad_ffn_all = everyone(grad_ffn)
        grad_pre = (mm(grad_ffn_all, ffn_out_all, ((1,), (1,))) * slope.astype(f32)).astype(bf16)
        in_bias_sum = token_sum(grad_pre)
        for_ffn.append((hidden, grad_ffn_all, first_all, grad_pre))
        if last:
            ffn_out_parts = chosen(lambda a, b, c, d: parts_of(a, b, 1), for_ffn)
            ffn_in_parts = chosen(lambda a, b, c, d: parts_of(c, d, 0), for_ffn)
            grad_second = after(grad_second, *ffn_out_parts, *ffn_in_parts)
        grad_first = grad_second + returned(grad_pre, in_all, ((1,), (1,)))
        gain_one, shift_one = token_sum(grad_first * first_normed), token_sum(grad_first)
        grad_resid = norm_back(grad_first, first_normed, first_inverse, attn_gain)
        grad_branch = grad_resid.astype(bf16)
        out_bias_grad = token_sum(grad_branch)
        branch_all = everyone(grad_branch)
        grad_mixed = by_position(mm(branch_all, out_all, ((1,), (1,))).astype(bf16))
        for_out.append((mixed, branch_all))
        if last:
            out_parts = chosen(lambda a, b: parts_of(a, b, 1), for_out)
            grad_mixed = after(grad_mixed, *out_parts)
        grads = attend_back(qkv, segment, span, kernel_order, kernel_rows, grad_mixed, lse)
        grad_qkv = jnp.concatenate([by_distance(grad) for grad in grads], axis=1)
        bias_sums = token_sum(grad_qkv)
        for_joined.append((rounded_all, grad_qkv))
        if last:
            joined_parts = chosen(lambda a, b: parts_of(a, b, 0), for_joined)
            grad_resid = after(grad_resid, *joined_parts)
        grad_input = grad_resid + returned(grad_qkv, joined, ((1,), (1,)))
        tw_grad, tb_grad = token_sum(grad_input * time_rows), token_sum(grad_input)
        grad_in = grad_input.astype(bf16)
        slot_sums = jnp.concatenate(
            [
                bias_sums[:heads_all].reshape(seqs, head_cols),
                bias_sums[2 * heads_all :].reshape(seqs, head_cols),
                in_bias_sum.reshape(seqs, unit_cols),
            ],
            axis=1,
        )
        vector_sums = jnp.stack(
            [tw_grad, tb_grad, out_bias_grad, gain_one, shift_one, ffn_out_bias_grad, gain_two, shift_two]
        )
        these = (vector_sums, slot_sums, grad_in)
        if step == 0:
            results = these
        else:
            here = section_at == sections - 1 - step
            results = jax.tree.map(lambda a, b: jnp.where(here, a, b), these, results)
        if not last:
            upstream_rows = passed_along(grad_in, "pipe", -1)
    vector_sums, slot_sums, grad_in = results
    stat_row = jnp.concatenate([stat_terms, jnp.zeros((width - 3,), f32)])[None]
    shared = jnp.concatenate([straightened(vector_sums), stat_row])
    if in_kernels:
        small = jnp.concatenate([shared, jnp.zeros((7, width), f32)])
        padded = -(-slot_sums.shape[1] // 1024) * 1024
        slots = jnp.pad(slot_sums, ((0, 0), (0, padded - slot_sums.shape[1])))
        all_parts = (ffn_out_parts, ffn_in_parts, out_parts, joined_parts)
        by_block = straightened(grad_in).reshape(seqs, rows, width)
        input_pieces, small, slots, *gradients = scatter_all(
            by_block,
            small,
            slots.reshape(seqs, 8, padded // 8),
            [parts[0] for parts in all_parts],
            [parts[1] for parts in all_parts],
            tp_size,
        )
        input_grad = in_positions([input_pieces[(seqs - by) % seqs][None] for by in range(seqs)])
        shared, own_slot = small[:9], slots.reshape(1, padded)[:, : slot_sums.shape[1]]
        ffn_out_grad, ffn_in_grad, out_grad = gradients[:3]
        triple = gradients[3:]
    else:
        input_grad = in_positions(to_positions(grad_in))
        shared = summed_over(summed_over(summed_over(shared, "tp"), "zs"), "dp")
        own_slot = slot_sums[0:1]
        for by in range(1, seqs):
            own_slot = own_slot + received(slot_sums[by : by + 1], "zs", -by)
        own_slot = summed_over(own_slot, "dp")
        ffn_out_grad = owned(ffn_out_parts, 0, 1)
        ffn_in_grad = owned(ffn_in_parts, 1, 1)
        out_grad = owned(out_parts, 0, 1)
        joined_grad = owned(joined_parts, 1, 3)
        triple = [joined_grad[:, i * head_cols : (i + 1) * head_cols] for i in range(3)]
    layer_out = in_positions(layer_pieces, grads[0])
    element_count = float(SEQ_LEN * seqs * dp_size * width)
    stats = jnp.sqrt(shared[8:9, :3] / element_count)
    return (
        layer_out[None],
        input_grad[None],
        shared[0:1],
        shared[1:2],
        triple[0][None],
        own_slot[:, :head_cols],
        triple[1][None],
        triple[2][None],
        own_slot[:, head_cols : 2 * head_cols],
        out_grad[None],
        shared[2:3],
        shared[3:4],
        shared[4:5],
        ffn_in_grad[None],
        own_slot[:, 2 * head_cols :],
        ffn_out_grad[None],
        shared[5:6],
        shared[6:7],
        shared[7:8],
        stats,
    )


def solution(mesh):
    def run(states, *rest):
        sizes = mesh.shape
        seqs = states.shape[1] // sizes["dp"]
        grouped = Mesh(
            mesh.devices.reshape(sizes["pipe"], sizes["dp"], seqs, sizes["tensor"] // seqs),
            ("pipe", "dp", "zs", "tp"),
        )
        return jax.shard_map(
            per_device,
            mesh=grouped,
            in_specs=(
                P(TENSOR, "dp", None),
                P(TENSOR, "dp", None),
                P("dp", None),
                P("dp", None),
                P("pipe", None),
                P("pipe", None),
                P("pipe", None, TENSOR),
                P("pipe", TENSOR),
                P("pipe", None, TENSOR),
                P("pipe", None, TENSOR),
                P("pipe", TENSOR),
                P("pipe", TENSOR, None),
                P("pipe", None),
                P("pipe", None),
                P("pipe", None),
                P("pipe", None, TENSOR),
                P("pipe", TENSOR),
                P("pipe", TENSOR, None),
                P("pipe", None),
                P("pipe", None),
                P("pipe", None),
            ),
            out_specs=(
                P("pipe", TENSOR, "dp", None),
                P("pipe", TENSOR, "dp", None),
                P("pipe", None),
                P("pipe", None),
                P("pipe", "dp", TENSOR),
                P("pipe", TENSOR),
                P("pipe", "dp", TENSOR),
                P("pipe", "dp", TENSOR),
                P("pipe", TENSOR),
                P("pipe", TENSOR, "dp"),
                P("pipe", None),
                P("pipe", None),
                P("pipe", None),
                P("pipe", "dp", TENSOR),
                P("pipe", TENSOR),
                P("pipe", TENSOR, "dp"),
                P("pipe", None),
                P("pipe", None),
                P("pipe", None),
                P("pipe", None),
            ),
            check_vma=False,
        )(states, *rest)

    return run
```

```python
import functools
import math

import jax
import jax.numpy as jnp
from jax import lax
from jax.experimental import pallas as pl
from jax.experimental.pallas import tpu as pltpu
from jax.sharding import Mesh
from jax.sharding import PartitionSpec as P

HDIM = 64
SEQ_LEN = 1152
STEPS = 5000
ITEM_MOST = 525
PAIR = 2 * HDIM
TILE = 128
AHEAD = 2
WIDTHS = (2, 3, 4, 5, 6, 7, 9)
LOG2E = math.log2(math.e)
SCALE = 1.0 / math.sqrt(HDIM)
TENSOR = ("zs", "tp")

epsilon = 1e-05
f32 = jnp.float32
bf16 = jnp.bfloat16


def received(shard, axis, by):
    size = lax.axis_size(axis)
    by = by % size
    if by == 0:
        return shard
    return lax.ppermute(shard, axis, [((i + by) % size, i) for i in range(size)])


def passed_along(shard, axis, by):
    size = lax.axis_size(axis)
    pairs = [(i, i + by) for i in range(size) if 0 <= i + by < size]
    return lax.ppermute(shard, axis, pairs)


def summed_over(values, axis):
    total = values
    for by in range(1, lax.axis_size(axis)):
        total = total + received(values, axis, by)
    return total


def after(value, *others):
    return lax.optimization_barrier((value, *others))[0]


def norm_parts(summed):
    centered = summed - jnp.mean(summed, axis=-1, keepdims=True)
    inverse = lax.rsqrt(jnp.mean(centered * centered, axis=-1, keepdims=True) + epsilon)
    return (centered * inverse, inverse)


def norm_back(upstream, normed, inverse, gain):
    scaled = upstream * gain
    return inverse * (
        scaled
        - jnp.mean(scaled, axis=-1, keepdims=True)
        - normed * jnp.mean(scaled * normed, axis=-1, keepdims=True)
    )


def token_sum(values):
    return jnp.sum(values.astype(f32), axis=0)


def mm(a, b, dims=((1,), (0,))):
    return lax.dot_general(a, b, (dims, ((), ())), preferred_element_type=f32)


def key_spans(item_ends, length):
    tiles = length // TILE
    first = jnp.arange(tiles, dtype=jnp.int32)[:, None] * TILE
    ends = item_ends[None, :]
    start = jnp.max(jnp.where(ends <= first, ends, 0), axis=1) // TILE
    end = jnp.min(jnp.where(ends > first + TILE - 1, ends, length), axis=1)
    need = (end + TILE - 1) // TILE - start
    widths = jnp.array([min(w, tiles) for w in WIDTHS], jnp.int32)
    kind = jnp.sum((widths[None, :] < need[:, None]).astype(jnp.int32), axis=1)
    is_kind = jnp.arange(len(WIDTHS), dtype=jnp.int32)[None, :] == kind[:, None]
    width = jnp.sum(jnp.where(is_kind, widths[None, :], 0), axis=1)
    return jnp.stack([kind, jnp.minimum(start, tiles - width) * TILE]).astype(jnp.int32)


def place(order, source, target, rows, by_position):
    for block in range(source.shape[0] // rows):
        at = pl.ds(pl.multiple_of(order[block] * rows, 16), rows)
        if by_position:
            target[at, :] = source[block * rows : (block + 1) * rows, :]
        else:
            target[block * rows : (block + 1) * rows, :] = source[at, :]


def two_heads(pair):
    first = lax.broadcasted_iota(jnp.int32, pair.shape, 1) < HDIM
    zero = jnp.zeros_like(pair)
    return jnp.concatenate([jnp.where(first, pair, zero), jnp.where(first, zero, pair)], axis=0)


def one_pair(stacked):
    half = stacked.shape[0] // 2
    first = lax.broadcasted_iota(jnp.int32, (half, stacked.shape[1]), 1) < HDIM
    return jnp.where(first, stacked[:half], stacked[half:])


def each_tile(span, length, body):
    tiles = length // TILE

    def step(tile, carry):
        at = pl.ds(pl.multiple_of(tile * TILE, TILE), TILE)

        def branch(width):
            count = min(width, tiles) * TILE
            return lambda: body(at, pl.ds(pl.multiple_of(span[1, tile], TILE), count))

        lax.switch(span[0, tile], [branch(width) for width in WIDTHS])
        return carry

    lax.fori_loop(0, tiles, step, 0)


def attend_kernel(
    rows, order, span, seg_c, seg_r, q_ref, k_ref, v_ref, mixed_ref, lse_ref, q_s, k_s, v_s, mixed_s
):
    for source, target in ((q_ref, q_s), (k_ref, k_s), (v_ref, v_s)):
        place(order, source, target, rows, True)

    def body(at, to):
        same_item = seg_c[at, :] == seg_r[:, to]
        same_item = jnp.concatenate([same_item, same_item], axis=0)
        for pair in range(q_ref.shape[1] // PAIR):
            cols = slice(pair * PAIR, (pair + 1) * PAIR)
            scores = mm(two_heads(q_s[at, cols]), k_s[to, cols], ((1,), (1,))) * (SCALE * LOG2E)
            scores = jnp.where(same_item, scores, -1e30)
            top = jnp.max(scores, axis=1, keepdims=True)
            weights = jnp.exp2(scores - top)
            total = jnp.sum(weights, axis=1, keepdims=True)
            mixed = mm(weights.astype(bf16), v_s[to, cols]) * (1.0 / total)
            mixed_s[at, cols] = one_pair(mixed).astype(bf16)
            sums = top + jnp.log2(total)
            spread = one_pair(jnp.broadcast_to(sums, (2 * TILE, PAIR))).T
            lse_ref[pair, 0:1, at] = spread[0:1]
            lse_ref[pair, 1:2, at] = spread[HDIM : HDIM + 1]

    each_tile(span, q_ref.shape[0], body)
    place(order, mixed_s, mixed_ref, rows, False)


def attend(qkv, segment, span, order, rows):
    length, width = qkv.shape[0], qkv.shape[1] // 3
    pairs = width // PAIR
    small = pl.BlockSpec(memory_space=pltpu.SMEM)
    third = lambda i: pl.BlockSpec((length, width), lambda h: (0, i))
    return pl.pallas_call(
        functools.partial(attend_kernel, rows),
        grid=(1,),
        in_specs=[
            small,
            small,
            pl.BlockSpec((length, 1), lambda h: (0, 0)),
            pl.BlockSpec((1, length), lambda h: (0, 0)),
            third(0),
            third(1),
            third(2),
        ],
        out_specs=[third(0), pl.BlockSpec((pairs, 2, length), lambda h: (0, 0, 0))],
        out_shape=[
            jax.ShapeDtypeStruct((length, width), bf16),
            jax.ShapeDtypeStruct((pairs, 2, length), f32),
        ],
        scratch_shapes=[pltpu.VMEM((length, width), bf16)] * 4,
        compiler_params=pltpu.CompilerParams(vmem_limit_bytes=48 * 1024 * 1024),
        cost_estimate=pl.CostEstimate(flops=0, bytes_accessed=0, transcendentals=0),
    )(order, span, segment[:, None], segment[None, :], qkv, qkv, qkv)


def back_tile(at, to, seg_c, seg_r, lse_ref, q_s, k_s, v_s, up_s, dq_s, dk_s, dv_s):
    same_item = seg_c[to, :] == seg_r[:, at]
    same_item = jnp.concatenate([same_item, same_item], axis=1)
    for pair in range(q_s.shape[1] // PAIR):
        cols = slice(pair * PAIR, (pair + 1) * PAIR)
        keys_all = k_s[to, cols]
        queries, upstream = two_heads(q_s[at, cols]), two_heads(up_s[at, cols])
        lse = jnp.concatenate([lse_ref[pair, 0:1, at], lse_ref[pair, 1:2, at]], axis=1)
        scores = mm(keys_all, queries, ((1,), (1,))) * (SCALE * LOG2E)
        probs = jnp.where(same_item, jnp.exp2(scores - lse), 0.0)
        grad_probs = mm(v_s[to, cols], upstream, ((1,), (1,)))
        weighted = probs * grad_probs
        inner = jnp.sum(weighted, axis=0, keepdims=True)
        grad_scores = (weighted - probs * inner).astype(bf16)
        dv_s[to, cols] += mm(probs.astype(bf16), upstream)
        dk_s[to, cols] += mm(grad_scores, queries)
        dq_s[at, cols] = (one_pair(mm(grad_scores, keys_all, ((0,), (0,)))) * SCALE).astype(bf16)


def attend_back_kernel(
    rows, order, span, seg_c, seg_r, q_ref, k_ref, v_ref, up_ref, lse_ref, dq_ref, dk_ref, dv_ref,
    q_s, k_s, v_s, up_s, dq_s, dk_s, dv_s,
):
    for source, target in ((q_ref, q_s), (k_ref, k_s), (v_ref, v_s), (up_ref, up_s)):
        place(order, source, target, rows, True)
    dk_s[...] = jnp.zeros_like(dk_s)
    dv_s[...] = jnp.zeros_like(dv_s)

    def body(at, to):
        back_tile(at, to, seg_c, seg_r, lse_ref, q_s, k_s, v_s, up_s, dq_s, dk_s, dv_s)

    each_tile(span, q_ref.shape[0], body)
    q_s[...] = (dk_s[...] * SCALE).astype(bf16)
    v_s[...] = dv_s[...].astype(bf16)
    for source, target in ((dq_s, dq_ref), (q_s, dk_ref), (v_s, dv_ref)):
        place(order, source, target, rows, False)


def attend_back(qkv, segment, span, order, rows, grad_mixed, lse):
    length, width = grad_mixed.shape
    pairs = width // PAIR
    small = pl.BlockSpec(memory_space=pltpu.SMEM)
    third = lambda i: pl.BlockSpec((length, width), lambda h: (0, i))
    return pl.pallas_call(
        functools.partial(attend_back_kernel, rows),
        grid=(1,),
        in_specs=[
            small,
            small,
            pl.BlockSpec((length, 1), lambda h: (0, 0)),
            pl.BlockSpec((1, length), lambda h: (0, 0)),
            third(0),
            third(1),
            third(2),
            third(0),
            pl.BlockSpec((pairs, 2, length), lambda h: (0, 0, 0)),
        ],
        out_specs=[third(0)] * 3,
        out_shape=[jax.ShapeDtypeStruct((length, width), bf16)] * 3,
        scratch_shapes=[pltpu.VMEM((length, width), bf16)] * 5 + [pltpu.VMEM((length, width), f32)] * 2,
        compiler_params=pltpu.CompilerParams(vmem_limit_bytes=48 * 1024 * 1024),
        cost_estimate=pl.CostEstimate(flops=0, bytes_accessed=0, transcendentals=0),
    )(order, span, segment[:, None], segment[None, :], qkv, qkv, qkv, grad_mixed, lse)


def gelu_parts(pre):
    size = jnp.abs(pre)
    t = 1.0 / (1.0 + (0.3275911 * math.sqrt(0.5)) * size)
    bell = jnp.exp2((-0.5 * LOG2E) * (pre * pre))
    poly = t * (0.127414796 + t * (-0.142248368 + t * (0.7107068705 + t * (-0.7265760135 + t * 0.5307027145))))
    below = poly * bell
    below = jnp.where(pre >= 0, 1.0 - below, below)
    return pre * below, below + (pre * bell) * (1.0 / math.sqrt(2.0 * math.pi))


def widen_kernel(chunk, x_ref, w_ref, bias_ref, hidden_ref, slope_ref):
    for at in range(0, x_ref.shape[0], chunk):
        rows = slice(at, at + chunk)
        hidden, slope = gelu_parts(mm(x_ref[rows, :], w_ref[...]) + bias_ref[...])
        hidden_ref[rows, :] = hidden.astype(bf16)
        slope_ref[rows, :] = slope.astype(bf16)


def widen(x, weight, bias):
    count, width = x.shape
    units = weight.shape[1]
    step = 256
    return pl.pallas_call(
        functools.partial(widen_kernel, 144),
        grid=(units // step,),
        in_specs=[
            pl.BlockSpec((count, width), lambda i: (0, 0)),
            pl.BlockSpec((width, step), lambda i: (0, i)),
            pl.BlockSpec((1, step), lambda i: (0, i)),
        ],
        out_specs=[pl.BlockSpec((count, step), lambda i: (0, i))] * 2,
        out_shape=[jax.ShapeDtypeStruct((count, units), bf16)] * 2,
        compiler_params=pltpu.CompilerParams(vmem_limit_bytes=48 * 1024 * 1024),
        cost_estimate=pl.CostEstimate(flops=0, bytes_accessed=0, transcendentals=0),
    )(x, weight, bias[None])


def gather_kernel(seqs, dp_size, *refs):
    seq_ref, bias_ref = refs[:2]
    blocks = refs[2:8]
    start_ref, biases_ref, joined_ref, out_ref, in_ref, ffn_out_ref = refs[8:14]
    local_sem, seq_send, seq_get, up_send, up_get, down_send, down_get, side_send, side_get = refs[14:]
    zs, dp = lax.axis_index("zs"), lax.axis_index("dp")
    width, hc = blocks[0].shape
    units = blocks[4].shape[1]
    part = width // dp_size
    half = units // 2
    table = [(0, 0, hc), (1, 0, hc), (2, 0, hc), (3, 0, hc)]
    table += [(4, 0, half), (4, half, half), (5, 0, half), (5, half, half)]
    kinds = range(len(table))

    def home(kind, slot, other):
        array, first, size = table[kind]
        features = slice(other * part, (other + 1) * part)
        if array < 3:
            at = (array * seqs + slot) * hc
            return joined_ref.at[features, at : at + hc]
        if array == 3:
            return out_ref.at[slot * hc : (slot + 1) * hc, features]
        at = slice(slot * units + first, slot * units + first + size)
        return in_ref.at[features, at] if array == 4 else ffn_out_ref.at[at, features]

    def own(kind, other):
        array, first, size = table[kind]
        features = pl.ds(pl.multiple_of(lax.rem(dp + other, dp_size) * part, part), part)
        if array in (3, 5):
            return blocks[array].at[first : first + size, features]
        return blocks[array].at[features, first : first + size]

    def to(axis, at, source, target, send, get):
        return pltpu.make_async_remote_copy(
            src_ref=source,
            dst_ref=target,
            send_sem=send,
            recv_sem=get,
            device_id={axis: at},
            device_id_type=pl.DeviceIdType.MESH,
        )

    def sequence(by):
        at = lax.rem(zs - by + seqs, seqs)
        return to("zs", at, seq_ref.at[at], start_ref.at[by], seq_send.at[by], seq_get.at[by])

    def bias(by):
        at = lax.rem(zs - by + seqs, seqs)
        return to("zs", at, bias_ref, biases_ref.at[by], seq_send.at[seqs + by], seq_get.at[seqs + by])

    def up(kind, hop):
        source = own(kind, 0) if hop == 0 else home(kind, seqs - hop, 0)
        target = home(kind, seqs - hop - 1, 0)
        return to("zs", zs + 1, source, target, up_send.at[kind, hop], up_get.at[kind, hop])

    def down(kind, hop):
        source = own(kind, 0) if hop == 0 else home(kind, hop, 0)
        target = home(kind, hop + 1, 0)
        return to("zs", zs - 1, source, target, down_send.at[kind, hop], down_get.at[kind, hop])

    def side(kind, slot, other):
        at = lax.rem(dp - other + dp_size, dp_size)
        place = side_send.at[kind, slot, other], side_get.at[kind, slot, other]
        return to("dp", at, home(kind, slot, 0), home(kind, slot, other), *place)

    def local(kind, other):
        return pltpu.make_async_copy(own(kind, other), home(kind, 0, other), local_sem.at[kind, other])

    barrier = pltpu.get_barrier_semaphore()
    for axis, at, size in (("zs", zs, seqs), ("dp", dp, dp_size)):
        for by in range(1, size):
            pl.semaphore_signal(
                barrier,
                inc=1,
                device_id={axis: lax.rem(at + by, size)},
                device_id_type=pl.DeviceIdType.MESH,
            )
    pl.semaphore_wait(barrier, seqs + dp_size - 2)

    for by in range(1, seqs):
        sequence(by).start()
        bias(by).start()
    def begin(kind):
        @pl.when(zs < seqs - 1)
        def _():
            up(kind, 0).start()

        @pl.when(zs > 0)
        def _():
            down(kind, 0).start()

    for kind in kinds[:AHEAD]:
        begin(kind)

    own_seq = pltpu.make_async_copy(seq_ref.at[zs], start_ref.at[0], local_sem.at[len(table), 0])
    own_bias = pltpu.make_async_copy(bias_ref, biases_ref.at[0], local_sem.at[len(table), 1])
    own_seq.start()
    own_bias.start()
    for kind in kinds:
        for other in range(dp_size):
            local(kind, other).start()

    def pass_on(kind, hop):
        @pl.when(zs >= hop)
        def _():
            up(kind, hop - 1).wait_recv()
            if hop < seqs - 1:

                @pl.when(zs < seqs - 1)
                def _():
                    up(kind, hop).start()

            for other in range(1, dp_size):
                side(kind, seqs - hop, other).start()

        @pl.when(zs + hop < seqs)
        def _():
            down(kind, hop - 1).wait_recv()
            if hop < seqs - 1:

                @pl.when(zs > 0)
                def _():
                    down(kind, hop).start()

            for other in range(1, dp_size):
                side(kind, hop, other).start()

    for step in range(len(kinds) + seqs - 2):
        for hop in range(1, seqs):
            if 0 <= step - hop + 1 < len(kinds):
                pass_on(step - hop + 1, hop)
        if step + AHEAD < len(kinds):
            begin(step + AHEAD)

    own_seq.wait()
    own_bias.wait()
    for by in range(1, seqs):
        sequence(by).wait()
        bias(by).wait()
    for kind in kinds:
        for other in range(dp_size):
            local(kind, other).wait()
        for slot in range(1, seqs):
            for other in range(1, dp_size):
                side(kind, slot, other).wait()
        for hop in range(seqs - 1):

            @pl.when((zs >= hop) & (zs < seqs - 1))
            def _():
                up(kind, hop).wait_send()

            @pl.when((zs + hop < seqs) & (zs > 0))
            def _():
                down(kind, hop).wait_send()


def gather_all(by_seq, biases, blocks, dp_size):
    seqs, _, width = by_seq.shape
    hc, units = blocks[0].shape[1], blocks[4].shape[1]
    anywhere = pl.BlockSpec(memory_space=pl.ANY)
    low = lambda *shape: jax.ShapeDtypeStruct(shape, bf16)
    dma = pltpu.SemaphoreType.DMA
    kinds = 8
    return pl.pallas_call(
        functools.partial(gather_kernel, seqs, dp_size),
        in_specs=[anywhere] * (2 + len(blocks)),
        out_specs=[anywhere] * 6,
        out_shape=[
            jax.ShapeDtypeStruct(by_seq.shape, bf16),
            jax.ShapeDtypeStruct((seqs,) + biases.shape, f32),
            low(width, 3 * seqs * hc),
            low(seqs * hc, width),
            low(width, seqs * units),
            low(seqs * units, width),
        ],
        scratch_shapes=[
            dma((kinds + 1, max(dp_size, 2))),
            dma((2 * seqs,)),
            dma((2 * seqs,)),
            dma((kinds, seqs - 1)),
            dma((kinds, seqs - 1)),
            dma((kinds, seqs - 1)),
            dma((kinds, seqs - 1)),
            dma((kinds, seqs, dp_size)),
            dma((kinds, seqs, dp_size)),
        ],
        compiler_params=pltpu.CompilerParams(collective_id=0, has_side_effects=True),
    )(by_seq, biases, *blocks)


def scatter_kernel(rows, seqs, dp_size, tp_size, *refs):
    seq_ref, small_ref, slots_ref = refs[:3]
    mine, theirs = list(refs[3:6]), list(refs[6:9])
    qkv_ref, up_ref, lse_ref, seg_c, seg_r, joined_ref, resid_ref, time_ref = refs[9:17]
    tokens_last, tokens_before, gq_before = refs[17:20]
    seq_out, small_out, slots_out = refs[20:23]
    outs = refs[23:29]
    sides, ups, downs = refs[29:33], refs[33:37], refs[37:41]
    small_zs, small_all, slots_zs, slots_dp = refs[41:45]
    seq_send, seq_get, local_sem, small_send, small_get = refs[45:50]
    side_send, side_get, up_send, up_get, down_send, down_get = refs[50:56]
    q_s, k_s, v_s, up_s, dq_s, dk_s, dv_s, gq_s, tokens_s = refs[56:65]
    x_send, x_get, seq_s, small_s, slots_s, joined_mine, joined_theirs = refs[65:72]
    place_sem, x_sem = refs[72:74]
    mine.append(joined_mine)
    theirs.append(joined_theirs)
    first_stage = lax.axis_index("pipe") == 0
    zs, dp, tp = lax.axis_index("zs"), lax.axis_index("dp"), lax.axis_index("tp")
    units = mine[0].shape[0] // seqs
    hc = mine[2].shape[0] // seqs
    half = units // 2
    length, heads_all = q_s.shape
    own_count, width = resid_ref.shape
    part = width // dp_size
    kinds = [(0, 0, 0, half), (0, 0, half, half), (1, 1, 0, half), (1, 1, half, half), (2, 0, 0, hc)]
    kinds += [(3, 1, third * seqs * hc, hc) for third in range(3)]

    def cut(arrays, kind, slot):
        array, axis, first, size = kinds[kind]
        apart = units if array < 2 else hc
        at = slice(first + slot * apart, first + slot * apart + size)
        return arrays[array].at[at, :] if axis == 0 else arrays[array].at[:, at]

    def to(where, source, target, send, get):
        return pltpu.make_async_remote_copy(
            src_ref=source,
            dst_ref=target,
            send_sem=send,
            recv_sem=get,
            device_id=where,
            device_id_type=pl.DeviceIdType.MESH,
        )

    def sequence(by):
        at = lax.rem(zs + by, seqs)
        return to({"zs": at}, seq_s.at[by], seq_out.at[by], seq_send.at[by], seq_get.at[by])

    def side(kind, slot):
        place = side_send.at[kind, slot], side_get.at[kind, slot]
        return to({"dp": 1 - dp}, cut(theirs, kind, slot), cut(sides, kind, slot), *place)

    def up(kind, far):
        place = up_send.at[kind, far], up_get.at[kind, far]
        return to({"zs": zs + 1}, cut(sides, kind, far), cut(ups, kind, far - 1), *place)

    def down(kind, far):
        place = down_send.at[kind, far], down_get.at[kind, far]
        return to({"zs": zs - 1}, cut(sides, kind, seqs - far), cut(downs, kind, far - 1), *place)

    def small(by):
        at = {"zs": lax.rem(zs + by, seqs)}
        return to(at, small_s, small_zs.at[by], small_send.at[0, by], small_get.at[0, by])

    def slots(by):
        at = {"zs": lax.rem(zs + by, seqs)}
        return to(at, slots_s.at[by], slots_zs.at[by], small_send.at[1, by], small_get.at[1, by])

    def small_across(by):
        at = lax.rem(dp * tp_size + tp + by, dp_size * tp_size)
        where = {"dp": lax.div(at, tp_size), "tp": lax.rem(at, tp_size)}
        return to(where, small_all.at[0], small_all.at[by], small_send.at[2, by], small_get.at[2, by])

    def slots_across():
        return to({"dp": 1 - dp}, slots_dp.at[0], slots_dp.at[1], small_send.at[3, 0], small_get.at[3, 0])

    def added(target, *others):
        rows = target.shape[0]
        step = 64

        def body(i, carry):
            at = pl.ds(pl.multiple_of(i * step, step), step)
            total = target[at, :].astype(f32)
            for other in others:
                total = total + other[at, :].astype(f32)
            target[at, :] = total.astype(target.dtype)
            return carry

        lax.fori_loop(0, rows // step, body, 0)

    barrier = pltpu.get_barrier_semaphore()
    greeted = [{"zs": lax.rem(zs + by, seqs)} for by in range(1, seqs)]
    for by in range(1, dp_size * tp_size):
        at = lax.rem(dp * tp_size + tp + by, dp_size * tp_size)
        greeted.append({"dp": lax.div(at, tp_size), "tp": lax.rem(at, tp_size)})
    for where in greeted:
        pl.semaphore_signal(barrier, inc=1, device_id=where, device_id_type=pl.DeviceIdType.MESH)
    pl.semaphore_wait(barrier, len(greeted))

    slot_order = list(range(1, seqs)) + [0]

    def begin(kind):
        for slot in slot_order:
            side(kind, slot).start()

    def placed(block, array):
        member, chip = divmod(block, seqs)
        at = lax.rem(zs + chip, seqs) * tp_size + lax.rem(tp + member, tp_size)
        at = pl.ds(pl.multiple_of(at * rows, 16), rows)
        here = slice(block * rows, (block + 1) * rows)
        if array < 3:
            source = qkv_ref.at[here, array * heads_all : (array + 1) * heads_all]
        else:
            source = up_ref.at[here, :]
        target = (q_s, k_s, v_s, up_s)[array].at[at, :]
        return pltpu.make_async_copy(source, target, place_sem.at[array, block])

    def each_placed(act):
        for array in range(4):
            for block in range(length // rows):
                act(placed(block, array))

    own_tokens = pltpu.make_async_copy(tokens_last, tokens_s, local_sem.at[1])
    old_tokens = pltpu.make_async_copy(tokens_before, tokens_s, local_sem.at[1])
    old_grads = pltpu.make_async_copy(gq_before, gq_s, local_sem.at[2])
    old_seq = pltpu.make_async_copy(seq_ref, seq_s, local_sem.at[3])

    def attention(tiles):
        reach = ITEM_MOST - 1
        for tile in tiles:
            low = max(0, (tile * TILE - reach) // TILE)
            high = min(length, -(-((tile + 1) * TILE + reach) // TILE) * TILE)
            back_tile(
                slice(tile * TILE, (tile + 1) * TILE),
                slice(low * TILE, high),
                seg_c,
                seg_r,
                lse_ref,
                q_s,
                k_s,
                v_s,
                up_s,
                dq_s,
                dk_s,
                dv_s,
            )

    def attention_start():
        @pl.when(first_stage)
        def _():
            own_tokens.start()
            each_placed(lambda copy: copy.start())
            dk_s[...] = jnp.zeros_like(dk_s)
            dv_s[...] = jnp.zeros_like(dv_s)
            each_placed(lambda copy: copy.wait())
            attention(range(length // TILE // 2))

        @pl.when(jnp.logical_not(first_stage))
        def _():
            old_tokens.start()
            old_grads.start()
            old_seq.start()

    def attention_end():
        @pl.when(first_stage)
        def _():
            attention(range(length // TILE // 2, length // TILE))
            q_s[...] = (dk_s[...] * SCALE).astype(bf16)
            v_s[...] = dv_s[...].astype(bf16)
            for third, source in enumerate((dq_s, q_s, v_s)):
                cols = slice(third * heads_all, (third + 1) * heads_all)
                for block in range(length // rows):
                    member, chip = divmod(block, seqs)
                    at = lax.rem(zs + chip, seqs) * tp_size + lax.rem(tp + member, tp_size)
                    at = pl.ds(pl.multiple_of(at * rows, 16), rows)
                    gq_s[block * rows : (block + 1) * rows, cols] = source[at, :]
            own_tokens.wait()

        @pl.when(jnp.logical_not(first_stage))
        def _():
            old_tokens.wait()
            old_grads.wait()
            old_seq.wait()

    def joined_parts():
        step = 256
        for other in reversed(range(dp_size)):
            target = joined_mine if other == 0 else joined_theirs
            for third in range(3):
                cols = slice(third * heads_all, (third + 1) * heads_all)
                for at in range(0, part, step):
                    left = tokens_s[:, other * part + at : other * part + at + step]
                    target[at : at + step, cols] = mm(left, gq_s[:, cols], ((0,), (0,))).astype(bf16)

    def exchange():
        return to({"tp": 1 - tp}, x_send, x_get, x_sem.at[0], x_sem.at[1])

    def input_grads():
        @pl.when(first_stage)
        def _():
            def theirs_rows(i, carry):
                at = pl.multiple_of(i * rows, 16)
                x_send[pl.ds(at, rows), :] = mm(
                    gq_s[pl.ds(own_count + at, rows), :], joined_ref[...], ((1,), (1,))
                ).astype(bf16)
                return carry

            lax.fori_loop(0, seqs, theirs_rows, 0)
            exchange().start()
            for slot in range(seqs):
                cols = slice(slot * hc, (slot + 1) * hc)
                slots_s[slot, 0:1, :] = jnp.sum(gq_s[:, cols].astype(f32), axis=0, keepdims=True)
                cols = slice(2 * heads_all + slot * hc, 2 * heads_all + (slot + 1) * hc)
                slots_s[slot, 1:2, :] = jnp.sum(gq_s[:, cols].astype(f32), axis=0, keepdims=True)
            exchange().wait()

            def own_rows(i, carry):
                at = pl.ds(pl.multiple_of(i * rows, 16), rows)
                total = mm(gq_s[at, :], joined_ref[...], ((1,), (1,)))
                total = total + x_get[at, :].astype(f32) + resid_ref[at, :]
                lowered = total.astype(bf16)
                for other in range(dp_size):
                    cols = pl.ds(pl.multiple_of(lax.rem(dp + other, dp_size) * part, part), part)
                    seq_s[i, :, cols] = lowered[:, other * part : (other + 1) * part]
                timed = jnp.sum(total * time_ref[at, :], axis=0, keepdims=True)
                plain = jnp.sum(total, axis=0, keepdims=True)
                return carry[0] + timed, carry[1] + plain

            zero = jnp.zeros((1, width), f32)
            timed, plain = lax.fori_loop(0, seqs, own_rows, (zero, zero))
            for other in range(dp_size):
                cols = pl.ds(pl.multiple_of(lax.rem(dp + other, dp_size) * part, part), part)
                here = slice(other * part, (other + 1) * part)
                small_s[0:1, cols] = timed[:, here]
                small_s[1:2, cols] = plain[:, here]

    own_seq = pltpu.make_async_copy(seq_s.at[0], seq_out.at[0], local_sem.at[0])

    def send_small():
        for by in range(1, seqs):
            small(by).start()
            slots(by).start()
        for by in range(1, seqs):
            sequence(by).start()
        own_seq.start()

    def add_small():
        total, slot_total = small_s[...], slots_s[0]
        for by in range(1, seqs):
            small(by).wait()
            slots(by).wait()
            total = total + small_zs[by]
            slot_total = slot_total + slots_zs[by]
        small_all[0] = total
        slots_dp[0] = slot_total
        for by in range(1, dp_size * tp_size):
            small_across(by).start()
        slots_across().start()

    small_s[...] = small_ref[...]
    slots_s[...] = slots_ref[...]
    for kind in range(AHEAD):
        begin(kind)
    attention_start()

    def taken(kind):
        for slot in slot_order:
            side(kind, slot).wait()
            added(cut(sides, kind, slot), cut(mine, kind, slot))

    def pass_on(kind, hop):
        @pl.when((zs == hop) & (zs < seqs - 1))
        def _():
            for far in range(seqs - 1 - hop, 0, -1):
                if hop > 0:
                    up(kind, far + 1).wait_recv()
                    added(cut(sides, kind, far), cut(ups, kind, far))
                up(kind, far).start()

        @pl.when((zs == seqs - 1 - hop) & (zs > 0))
        def _():
            for far in range(seqs - 1 - hop, 0, -1):
                if hop > 0:
                    down(kind, far + 1).wait_recv()
                    added(cut(sides, kind, seqs - far), cut(downs, kind, far))
                down(kind, far).start()

    for step in range(len(kinds) + seqs - 2):
        if step < len(kinds):
            taken(step)
            if step + AHEAD < len(kinds):
                begin(step + AHEAD)
        for hop in range(seqs - 1):
            if 0 <= step - hop < len(kinds):
                pass_on(step - hop, hop)
        if step == 0:
            attention_end()
        if step == 1:
            joined_parts()
            input_grads()
            send_small()
        if step == 4:
            add_small()

    total, slot_total = small_all[0], slots_dp[0]
    for by in range(1, dp_size * tp_size):
        small_across(by).wait()
        total = total + small_all[by]
    slots_across().wait()
    small_out[...] = total
    slots_out[...] = slot_total + slots_dp[1]

    for kind, (array, axis, first, size) in enumerate(kinds):
        out = outs[array] if array < 3 else outs[3 + first // (seqs * hc)]
        if array < 2:
            out = out.at[first : first + size, :] if axis == 0 else out.at[:, first : first + size]
        out[...] = cut(sides, kind, 0)[...].astype(f32)

        @pl.when(zs > 0)
        def _():
            up(kind, 1).wait_recv()
            added(out, cut(ups, kind, 0))

        @pl.when(zs < seqs - 1)
        def _():
            down(kind, 1).wait_recv()
            added(out, cut(downs, kind, 0))

        for far in range(1, seqs):

            @pl.when(zs + far < seqs)
            def _():
                up(kind, far).wait_send()

            @pl.when(zs >= far)
            def _():
                down(kind, far).wait_send()

    own_seq.wait()
    for by in range(1, seqs):
        sequence(by).wait()


def scatter_all(rows, by_block, small, slots, mine, theirs, attended, tokens, gq_before, tp_size):
    seqs, _, width = by_block.shape
    units, part = mine[0].shape[0] // seqs, mine[0].shape[1]
    hc = mine[2].shape[0] // seqs
    length, heads_all = tokens[0].shape[0], gq_before.shape[1] // 3
    own_count = length // tp_size
    dp_size = 2
    anywhere = pl.BlockSpec(memory_space=pl.ANY)
    inside = pl.BlockSpec(memory_space=pltpu.VMEM)
    wide = lambda *shape: jax.ShapeDtypeStruct(shape, f32)
    low = lambda *shape: pltpu.VMEM(shape, bf16)
    dma = pltpu.SemaphoreType.DMA
    like = [low(*block.shape) for block in mine] + [low(part, 3 * heads_all)]
    fewer = [low((seqs - 1) * units, part), low(part, (seqs - 1) * units), low((seqs - 1) * hc, part)]
    fewer.append(low(part, 3 * heads_all))
    kinds = 8
    return pl.pallas_call(
        functools.partial(scatter_kernel, rows, seqs, dp_size, tp_size),
        in_specs=[anywhere, inside, inside]
        + [inside] * 3
        + [anywhere] * 3
        + [anywhere, anywhere]
        + [inside] * 6
        + [anywhere] * 3,
        out_specs=[anywhere] + [inside] * 8,
        out_shape=[
            jax.ShapeDtypeStruct(by_block.shape, bf16),
            wide(*small.shape),
            wide(*slots.shape[1:]),
            wide(units, part),
            wide(part, units),
            wide(hc, part),
            wide(part, hc),
            wide(part, hc),
            wide(part, hc),
        ],
        scratch_shapes=like
        + fewer * 2
        + [
            pltpu.VMEM((seqs,) + small.shape, f32),
            pltpu.VMEM((dp_size * tp_size,) + small.shape, f32),
            pltpu.VMEM(slots.shape, f32),
            pltpu.VMEM((2,) + slots.shape[1:], f32),
            dma((seqs,)),
            dma((seqs,)),
            dma((4,)),
            dma((4, max(seqs, dp_size * tp_size))),
            dma((4, max(seqs, dp_size * tp_size))),
        ]
        + [dma((kinds, seqs))] * 6
        + [low(length, heads_all)] * 5
        + [pltpu.VMEM((length, heads_all), f32)] * 2
        + [
            low(length, 3 * heads_all),
            low(length, width),
            low(own_count, width),
            low(own_count, width),
            low(*by_block.shape),
            pltpu.VMEM(small.shape, f32),
            pltpu.VMEM(slots.shape, f32),
            low(part, 3 * heads_all),
            low(part, 3 * heads_all),
            dma((4, length // rows)),
            dma((2,)),
        ],
        compiler_params=pltpu.CompilerParams(
            collective_id=1, has_side_effects=True, vmem_limit_bytes=63 * 1024 * 1024
        ),
    )(by_block, small, slots, *mine, *theirs, *attended, *tokens, gq_before)


def per_device(
    states,
    cotangent,
    lengths,
    timesteps,
    time_weight,
    time_bias,
    query_weight,
    query_bias,
    key_weight,
    value_weight,
    value_bias,
    out_weight,
    out_bias,
    attn_gain,
    attn_shift,
    ffn_in,
    ffn_in_bias,
    ffn_out,
    ffn_out_bias,
    ffn_gain,
    ffn_shift,
):
    rows, seqs, width = states.shape
    own_count = seqs * rows
    sections, section_at = lax.axis_size("pipe"), lax.axis_index("pipe")
    dp_size, dp_at = lax.axis_size("dp"), lax.axis_index("dp")
    zs_at = lax.axis_index("zs")
    tp_size, tp_at = lax.axis_size("tp"), lax.axis_index("tp")
    length = own_count * tp_size
    part = width // dp_size
    head_cols, unit_cols = query_weight.shape[2], ffn_in.shape[2]
    heads_all, units_all = head_cols * seqs, unit_cols * seqs

    def rotated(array, axis=-1):
        axis = axis % array.ndim
        twice = jnp.concatenate([array, array], axis=axis)
        return lax.dynamic_slice_in_dim(twice, dp_at * part, width, axis)

    def straightened(array):
        twice = jnp.concatenate([array, array], axis=-1)
        back = (dp_size - dp_at) % dp_size
        return lax.dynamic_slice_in_dim(twice, back * part, width, array.ndim - 1)

    vectors = rotated(
        jnp.concatenate(
            [time_weight, time_bias, out_bias, attn_gain, attn_shift, ffn_out_bias, ffn_gain, ffn_shift]
        )
    )
    time_weight, time_bias, out_bias, attn_gain = vectors[0], vectors[1], vectors[2], vectors[3]
    attn_shift, ffn_out_bias, ffn_gain, ffn_shift = vectors[4], vectors[5], vectors[6], vectors[7]


    def to_sequence(array):
        by_seq = rotated(jnp.transpose(array, (1, 0, 2)))
        got = []
        for by in range(seqs):
            block = lax.dynamic_index_in_dim(by_seq, (zs_at - by) % seqs, 0, keepdims=False)
            got.append(received(block, "zs", by))
        return got

    def to_positions(array):
        by_block = straightened(array).reshape(seqs, rows, width)
        return [received(by_block[(seqs - by) % seqs], "zs", by)[None] for by in range(seqs)]

    def in_positions(got, *before):
        got = [after(piece, *before) for piece in got]
        twice = jnp.concatenate(got + got)
        by_seq = lax.dynamic_slice_in_dim(twice, (seqs - zs_at) % seqs, seqs, 0)
        return jnp.transpose(by_seq, (1, 0, 2))

    item_ends = jnp.cumsum(lax.dynamic_index_in_dim(lengths, zs_at, 0, keepdims=False))
    own_times = lax.dynamic_index_in_dim(timesteps, zs_at, 0, keepdims=False).astype(f32)
    member = (tp_at + jnp.arange(tp_size, dtype=jnp.int32)) % tp_size
    chips = (zs_at + jnp.arange(seqs, dtype=jnp.int32)) % seqs
    order = (chips[None, :] * tp_size + member[:, None]).reshape(seqs * tp_size).astype(jnp.int32)

    def segment_at(places):
        return jnp.sum((item_ends[None, :] <= places[:, None]).astype(jnp.int32), axis=1)

    segment = segment_at(jnp.arange(length, dtype=jnp.int32))
    span = key_spans(item_ends, length)
    own_places = order[:seqs, None] * rows + jnp.arange(rows, dtype=jnp.int32)[None, :]
    own_segment = segment_at(own_places.reshape(own_count))
    own_pick = own_segment[:, None] == jnp.arange(lengths.shape[1], dtype=jnp.int32)[None, :]
    time_rows = (jnp.sum(jnp.where(own_pick, own_times[None, :], 0.0), axis=1) / STEPS)[:, None]
    aligned = rows % 16 == 0
    kernel_rows = rows if aligned else length
    kernel_order = order if aligned else jnp.zeros((1,), jnp.int32)

    def by_position(array):
        if aligned:
            return array
        blocks = array.reshape(seqs * tp_size, rows, array.shape[1])
        return jnp.take(blocks, jnp.argsort(order), axis=0).reshape(array.shape)

    def by_distance(array):
        if aligned:
            return array
        blocks = array.reshape(seqs * tp_size, rows, array.shape[1])
        return jnp.take(blocks, order, axis=0).reshape(array.shape)


    def over_zs(block, axis, *before):
        mine = lax.dynamic_slice_in_dim(block, dp_at * part, part, axis)
        mine = after(mine, *before)
        return [received(mine, "zs", by) for by in range(1, seqs)]

    def over_dp(pieces):
        return [[received(piece, "dp", other) for other in range(dp_size)] for piece in pieces]

    def assembled(block, axis, pieces, thirds):
        across = 1 - axis
        each = block.shape[across] // thirds
        shape = [0, 0]
        shape[axis], shape[across] = width, block.shape[across] * seqs
        whole = jnp.zeros(shape, block.dtype)

        def put(whole, piece, slot, at):
            for third in range(thirds):
                start = [0, 0]
                start[axis], start[across] = at, (third * seqs + slot) * each
                cut = lax.slice_in_dim(piece, third * each, (third + 1) * each, axis=across)
                whole = lax.dynamic_update_slice(whole, cut, start)
            return whole

        whole = put(whole, rotated(block, axis), 0, 0)
        for slot, row in enumerate(pieces):
            for other, piece in enumerate(row):
                whole = put(whole, piece, slot + 1, other * part)
        return whole

    biases = jnp.concatenate([query_bias[0], value_bias[0], ffn_in_bias[0].astype(f32)])[None]
    in_kernels = sections == 2 and dp_size == 2 and tp_size == 2 and rows % 16 == 0
    in_kernels = in_kernels and head_cols == 128 and part % 256 == 0 and unit_cols % 256 == 0
    if in_kernels:
        by_seq = rotated(jnp.transpose(states, (1, 0, 2)))
        blocks = (query_weight, key_weight, value_weight, out_weight, ffn_in, ffn_out)
        start, bias_slots, joined, out_all, in_all, ffn_out_all = gather_all(
            by_seq, biases, [block[0] for block in blocks], dp_size
        )
        start_rows = start.reshape(own_count, width)
        bias_slots = bias_slots[:, 0]
    else:
        joined_block = jnp.concatenate([query_weight[0], key_weight[0], value_weight[0]], axis=1)
        start_pieces = to_sequence(states)
        start_rows = jnp.concatenate(start_pieces)
        bias_slots = [received(biases, "zs", by)[0] for by in range(seqs)]
        joined_zs = over_zs(joined_block, 0)
        out_zs = over_zs(out_weight[0], 1, *joined_zs, *start_pieces)
        in_zs = over_zs(ffn_in[0], 0, *out_zs)
        ffn_out_zs = over_zs(ffn_out[0], 1, *in_zs)
        joined = assembled(joined_block, 0, over_dp(joined_zs), 3)
        out_all = assembled(out_weight[0], 1, over_dp(out_zs), 1)
        in_all = assembled(ffn_in[0], 0, over_dp(in_zs), 1)
        ffn_out_all = assembled(ffn_out[0], 1, over_dp(ffn_out_zs), 1)
    query_bias_all = jnp.concatenate([b[:head_cols] for b in bias_slots])
    value_bias_all = jnp.concatenate([b[head_cols : 2 * head_cols] for b in bias_slots])
    in_bias_all = jnp.concatenate([b[2 * head_cols :] for b in bias_slots])
    joined_bias = jnp.concatenate([query_bias_all, jnp.zeros_like(query_bias_all), value_bias_all])

    def everyone(own):
        return jnp.concatenate([received(own, "tp", by) for by in range(tp_size)])

    def returned(full, weight, dims):
        total = 0.0
        for by in range(1, tp_size):
            theirs = mm(full[by * own_count : (by + 1) * own_count], weight, dims).astype(bf16)
            total = total + received(theirs, "tp", -by).astype(f32)
        return total + mm(full[:own_count], weight, dims)

    kept = []
    layer_rows, stat_terms = None, None
    inputs = start_rows
    for tick in range(sections):
        residual = inputs.astype(f32) + time_rows * time_weight + time_bias
        rounded_all = everyone(residual.astype(bf16))
        qkv = by_position((mm(rounded_all, joined) + joined_bias).astype(bf16))
        mixed, lse = attend(qkv, segment, span, kernel_order, kernel_rows)
        if tick == 1:
            mixed = after(mixed, *upstream_pieces)
        mixed = by_distance(mixed)
        branch = returned(mixed, out_all, ((1,), (0,))) + out_bias
        first_normed, first_inverse = norm_parts(residual + branch)
        first_out = first_normed * attn_gain + attn_shift
        first_all = everyone(first_out.astype(bf16))
        hidden, slope = widen(first_all, in_all, in_bias_all)
        ffn_branch = returned(hidden, ffn_out_all, ((1,), (0,))) + ffn_out_bias
        second_normed, second_inverse = norm_parts(first_out + ffn_branch)
        layer_y = (second_normed * ffn_gain + ffn_shift).astype(bf16)
        terms = jnp.stack(
            [jnp.sum(residual * residual), jnp.sum(branch * branch), jnp.sum(ffn_branch * ffn_branch)]
        )
        kept.append(
            (
                rounded_all,
                qkv,
                mixed,
                lse,
                first_normed,
                first_inverse,
                first_all,
                hidden,
                slope,
                second_normed,
                second_inverse,
            )
        )
        if tick == 0:
            layer_rows, stat_terms = layer_y, terms
            upstream_pieces = to_sequence(after(cotangent, layer_y))
        else:
            here = section_at == tick
            layer_rows = jnp.where(here, layer_y, layer_rows)
            stat_terms = jnp.where(here, terms, stat_terms)
        if tick + 1 < sections:
            inputs = passed_along(layer_y, "pipe", 1)
    layer_pieces = to_positions(layer_rows)


    def parts_of(left, right, side):
        found = []
        for other in range(dp_size):
            cut = slice(other * part, (other + 1) * part)
            if side == 0:
                found.append(mm(left[:, cut], right, ((0,), (0,))).astype(bf16))
            else:
                found.append(mm(left, right[:, cut], ((0,), (0,))).astype(bf16))
        return found

    def chosen(found_at, operands):
        if sections == 1:
            return found_at(*operands[0])
        return lax.switch(
            sections - 1 - section_at, [functools.partial(found_at, *each) for each in operands]
        )

    def owned(parts, axis, thirds):
        total = parts[0].astype(f32)
        for other in range(1, dp_size):
            total = total + received(parts[other], "dp", -other).astype(f32)
        each = total.shape[axis] // (seqs * thirds)
        blocks = [
            jnp.concatenate(
                [
                    lax.slice_in_dim(total, (third * seqs + k) * each, (third * seqs + k + 1) * each, axis=axis)
                    for third in range(thirds)
                ],
                axis=axis,
            )
            for k in range(seqs)
        ]
        mine = blocks[0]
        for by in range(1, seqs):
            mine = mine + received(blocks[by].astype(bf16), "zs", -by).astype(f32)
        return mine

    results = None
    upstream_rows = jnp.concatenate(upstream_pieces)
    for_ffn, for_out, for_joined = [], [], []
    for step in range(sections):
        (
            rounded_all,
            qkv,
            mixed,
            lse,
            first_normed,
            first_inverse,
            first_all,
            hidden,
            slope,
            second_normed,
            second_inverse,
        ) = kept[sections - 1 - step]
        last = step + 1 == sections
        upstream = upstream_rows.astype(f32)
        gain_two, shift_two = token_sum(upstream * second_normed), token_sum(upstream)
        grad_second = norm_back(upstream, second_normed, second_inverse, ffn_gain)
        grad_ffn = grad_second.astype(bf16)
        ffn_out_bias_grad = token_sum(grad_ffn)
        grad_ffn_all = everyone(grad_ffn)
        grad_pre = (mm(grad_ffn_all, ffn_out_all, ((1,), (1,))) * slope.astype(f32)).astype(bf16)
        in_bias_sum = token_sum(grad_pre)
        for_ffn.append((hidden, grad_ffn_all, first_all, grad_pre))
        if last:
            ffn_out_parts = chosen(lambda a, b, c, d: parts_of(a, b, 1), for_ffn)
            ffn_in_parts = chosen(lambda a, b, c, d: parts_of(c, d, 0), for_ffn)
            grad_second = after(grad_second, *ffn_out_parts, *ffn_in_parts)
        grad_first = grad_second + returned(grad_pre, in_all, ((1,), (1,)))
        gain_one, shift_one = token_sum(grad_first * first_normed), token_sum(grad_first)
        grad_resid = norm_back(grad_first, first_normed, first_inverse, attn_gain)
        grad_branch = grad_resid.astype(bf16)
        out_bias_grad = token_sum(grad_branch)
        branch_all = everyone(grad_branch)
        grad_mixed = by_position(mm(branch_all, out_all, ((1,), (1,))).astype(bf16))
        for_out.append((mixed, branch_all))
        if last:
            out_parts = chosen(lambda a, b: parts_of(a, b, 1), for_out)
            grad_mixed = after(grad_mixed, *out_parts)
        if last and in_kernels:
            attended = (qkv, grad_mixed, lse, segment[:, None], segment[None, :], joined, grad_resid, time_rows)
            tw_grad, tb_grad = jnp.zeros((width,), f32), jnp.zeros((width,), f32)
            bias_sums, grad_in = jnp.zeros((3 * heads_all,), f32), results[2]
        else:
            grads = attend_back(qkv, segment, span, kernel_order, kernel_rows, grad_mixed, lse)
            grad_qkv = jnp.concatenate([by_distance(grad) for grad in grads], axis=1)
            bias_sums = token_sum(grad_qkv)
            for_joined.append((rounded_all, grad_qkv))
            if last:
                joined_parts = chosen(lambda a, b: parts_of(a, b, 0), for_joined)
            grad_input = grad_resid + returned(grad_qkv, joined, ((1,), (1,)))
            tw_grad, tb_grad = token_sum(grad_input * time_rows), token_sum(grad_input)
            grad_in = grad_input.astype(bf16)
        slot_sums = jnp.concatenate(
            [
                bias_sums[:heads_all].reshape(seqs, head_cols),
                bias_sums[2 * heads_all :].reshape(seqs, head_cols),
                in_bias_sum.reshape(seqs, unit_cols),
            ],
            axis=1,
        )
        vector_sums = jnp.stack(
            [tw_grad, tb_grad, out_bias_grad, gain_one, shift_one, ffn_out_bias_grad, gain_two, shift_two]
        )
        these = (vector_sums, slot_sums, grad_in)
        if step == 0:
            results = these
        else:
            here = section_at == sections - 1 - step
            results = jax.tree.map(lambda a, b: jnp.where(here, a, b), these, results)
        if not last:
            upstream_rows = passed_along(grad_in, "pipe", -1)
    vector_sums, slot_sums, grad_in = results
    stat_row = jnp.concatenate([stat_terms, jnp.zeros((width - 3,), f32)])[None]
    shared = jnp.concatenate([straightened(vector_sums), stat_row])
    if in_kernels:
        small = jnp.concatenate([shared, jnp.zeros((7, width), f32)])
        padded = -(-slot_sums.shape[1] // 1024) * 1024
        slots = jnp.pad(slot_sums, ((0, 0), (0, padded - slot_sums.shape[1])))
        all_parts = (ffn_out_parts, ffn_in_parts, out_parts)
        by_block = straightened(grad_in).reshape(seqs, rows, width)
        input_pieces, small, slots, *gradients = scatter_all(
            rows,
            by_block,
            small,
            slots.reshape(seqs, 8, padded // 8),
            [parts[0] for parts in all_parts],
            [parts[1] for parts in all_parts],
            attended,
            (rounded_all, for_joined[0][0]),
            for_joined[0][1],
            tp_size,
        )
        input_grad = in_positions([input_pieces[(seqs - by) % seqs][None] for by in range(seqs)])
        shared, own_slot = small[:9], slots.reshape(1, padded)[:, : slot_sums.shape[1]]
        ffn_out_grad, ffn_in_grad, out_grad = gradients[:3]
        triple = gradients[3:]
    else:
        input_grad = in_positions(to_positions(grad_in))
        shared = summed_over(summed_over(summed_over(shared, "tp"), "zs"), "dp")
        own_slot = slot_sums[0:1]
        for by in range(1, seqs):
            own_slot = own_slot + received(slot_sums[by : by + 1], "zs", -by)
        own_slot = summed_over(own_slot, "dp")
        ffn_out_grad = owned(ffn_out_parts, 0, 1)
        ffn_in_grad = owned(ffn_in_parts, 1, 1)
        out_grad = owned(out_parts, 0, 1)
        joined_grad = owned(joined_parts, 1, 3)
        triple = [joined_grad[:, i * head_cols : (i + 1) * head_cols] for i in range(3)]
    layer_out = in_positions(layer_pieces, grad_mixed)
    element_count = float(SEQ_LEN * seqs * dp_size * width)
    stats = jnp.sqrt(shared[8:9, :3] / element_count)
    return (
        layer_out[None],
        input_grad[None],
        shared[0:1],
        shared[1:2],
        triple[0][None],
        own_slot[:, :head_cols],
        triple[1][None],
        triple[2][None],
        own_slot[:, head_cols : 2 * head_cols],
        out_grad[None],
        shared[2:3],
        shared[3:4],
        shared[4:5],
        ffn_in_grad[None],
        own_slot[:, 2 * head_cols :],
        ffn_out_grad[None],
        shared[5:6],
        shared[6:7],
        shared[7:8],
        stats,
    )


def solution(mesh):
    def run(states, *rest):
        sizes = mesh.shape
        seqs = states.shape[1] // sizes["dp"]
        grouped = Mesh(
            mesh.devices.reshape(sizes["pipe"], sizes["dp"], seqs, sizes["tensor"] // seqs),
            ("pipe", "dp", "zs", "tp"),
        )
        return jax.shard_map(
            per_device,
            mesh=grouped,
            in_specs=(
                P(TENSOR, "dp", None),
                P(TENSOR, "dp", None),
                P("dp", None),
                P("dp", None),
                P("pipe", None),
                P("pipe", None),
                P("pipe", None, TENSOR),
                P("pipe", TENSOR),
                P("pipe", None, TENSOR),
                P("pipe", None, TENSOR),
                P("pipe", TENSOR),
                P("pipe", TENSOR, None),
                P("pipe", None),
                P("pipe", None),
                P("pipe", None),
                P("pipe", None, TENSOR),
                P("pipe", TENSOR),
                P("pipe", TENSOR, None),
                P("pipe", None),
                P("pipe", None),
                P("pipe", None),
            ),
            out_specs=(
                P("pipe", TENSOR, "dp", None),
                P("pipe", TENSOR, "dp", None),
                P("pipe", None),
                P("pipe", None),
                P("pipe", "dp", TENSOR),
                P("pipe", TENSOR),
                P("pipe", "dp", TENSOR),
                P("pipe", "dp", TENSOR),
                P("pipe", TENSOR),
                P("pipe", TENSOR, "dp"),
                P("pipe", None),
                P("pipe", None),
                P("pipe", None),
                P("pipe", "dp", TENSOR),
                P("pipe", TENSOR),
                P("pipe", TENSOR, "dp"),
                P("pipe", None),
                P("pipe", None),
                P("pipe", None),
                P("pipe", None),
            ),
            check_vma=False,
        )(states, *rest)

    return run
```

```python
import functools
import math

import jax
import jax.numpy as jnp
from jax import lax
from jax.experimental import pallas as pl
from jax.experimental.pallas import tpu as pltpu
from jax.sharding import Mesh
from jax.sharding import PartitionSpec as P

HDIM = 64
SEQ_LEN = 1152
STEPS = 5000
ITEM_MOST = 525
PAIR = 2 * HDIM
TILE = 128
AHEAD = 2
WIDTHS = (2, 3, 4, 5, 6, 7, 9)
LOG2E = math.log2(math.e)
SCALE = 1.0 / math.sqrt(HDIM)
TENSOR = ("zs", "tp")

epsilon = 1e-05
f32 = jnp.float32
bf16 = jnp.bfloat16


def received(shard, axis, by):
    size = lax.axis_size(axis)
    by = by % size
    if by == 0:
        return shard
    return lax.ppermute(shard, axis, [((i + by) % size, i) for i in range(size)])


def passed_along(shard, axis, by):
    size = lax.axis_size(axis)
    pairs = [(i, i + by) for i in range(size) if 0 <= i + by < size]
    return lax.ppermute(shard, axis, pairs)


def summed_over(values, axis):
    total = values
    for by in range(1, lax.axis_size(axis)):
        total = total + received(values, axis, by)
    return total


def after(value, *others):
    return lax.optimization_barrier((value, *others))[0]


def norm_parts(summed):
    centered = summed - jnp.mean(summed, axis=-1, keepdims=True)
    inverse = lax.rsqrt(jnp.mean(centered * centered, axis=-1, keepdims=True) + epsilon)
    return (centered * inverse, inverse)


def norm_back(upstream, normed, inverse, gain):
    scaled = upstream * gain
    return inverse * (
        scaled
        - jnp.mean(scaled, axis=-1, keepdims=True)
        - normed * jnp.mean(scaled * normed, axis=-1, keepdims=True)
    )


def token_sum(values):
    return jnp.sum(values.astype(f32), axis=0)


def mm(a, b, dims=((1,), (0,))):
    return lax.dot_general(a, b, (dims, ((), ())), preferred_element_type=f32)


def key_spans(item_ends, length):
    tiles = length // TILE
    first = jnp.arange(tiles, dtype=jnp.int32)[:, None] * TILE
    ends = item_ends[None, :]
    start = jnp.max(jnp.where(ends <= first, ends, 0), axis=1) // TILE
    end = jnp.min(jnp.where(ends > first + TILE - 1, ends, length), axis=1)
    need = (end + TILE - 1) // TILE - start
    widths = jnp.array([min(w, tiles) for w in WIDTHS], jnp.int32)
    kind = jnp.sum((widths[None, :] < need[:, None]).astype(jnp.int32), axis=1)
    is_kind = jnp.arange(len(WIDTHS), dtype=jnp.int32)[None, :] == kind[:, None]
    width = jnp.sum(jnp.where(is_kind, widths[None, :], 0), axis=1)
    return jnp.stack([kind, jnp.minimum(start, tiles - width) * TILE]).astype(jnp.int32)


def place(order, source, target, rows, by_position):
    for block in range(source.shape[0] // rows):
        at = pl.ds(pl.multiple_of(order[block] * rows, 16), rows)
        if by_position:
            target[at, :] = source[block * rows : (block + 1) * rows, :]
        else:
            target[block * rows : (block + 1) * rows, :] = source[at, :]


def two_heads(pair):
    first = lax.broadcasted_iota(jnp.int32, pair.shape, 1) < HDIM
    zero = jnp.zeros_like(pair)
    return jnp.concatenate([jnp.where(first, pair, zero), jnp.where(first, zero, pair)], axis=0)


def one_pair(stacked):
    half = stacked.shape[0] // 2
    first = lax.broadcasted_iota(jnp.int32, (half, stacked.shape[1]), 1) < HDIM
    return jnp.where(first, stacked[:half], stacked[half:])


def each_tile(span, length, body):
    tiles = length // TILE

    def step(tile, carry):
        at = pl.ds(pl.multiple_of(tile * TILE, TILE), TILE)

        def branch(width):
            count = min(width, tiles) * TILE
            return lambda: body(at, pl.ds(pl.multiple_of(span[1, tile], TILE), count))

        lax.switch(span[0, tile], [branch(width) for width in WIDTHS])
        return carry

    lax.fori_loop(0, tiles, step, 0)


def forward_tile(at, to, seg_c, seg_r, lse_ref, q_s, k_s, v_s, mixed_s):
    same_item = seg_c[at, :] == seg_r[:, to]
    same_item = jnp.concatenate([same_item, same_item], axis=0)
    for pair in range(q_s.shape[1] // PAIR):
        cols = slice(pair * PAIR, (pair + 1) * PAIR)
        scores = mm(two_heads(q_s[at, cols]), k_s[to, cols], ((1,), (1,))) * (SCALE * LOG2E)
        scores = jnp.where(same_item, scores, -1e30)
        top = jnp.max(scores, axis=1, keepdims=True)
        weights = jnp.exp2(scores - top)
        total = jnp.sum(weights, axis=1, keepdims=True)
        mixed = mm(weights.astype(bf16), v_s[to, cols]) * (1.0 / total)
        mixed_s[at, cols] = one_pair(mixed).astype(bf16)
        sums = top + jnp.log2(total)
        spread = one_pair(jnp.broadcast_to(sums, (2 * TILE, PAIR))).T
        lse_ref[pair, 0:1, at] = spread[0:1]
        lse_ref[pair, 1:2, at] = spread[HDIM : HDIM + 1]


def banded(tiles, length, body):
    reach = ITEM_MOST - 1
    for tile in tiles:
        low = max(0, (tile * TILE - reach) // TILE)
        high = min(length, -(-((tile + 1) * TILE + reach) // TILE) * TILE)
        body(slice(tile * TILE, (tile + 1) * TILE), slice(low * TILE, high))


def attend_kernel(
    rows, order, span, seg_c, seg_r, q_ref, k_ref, v_ref, mixed_ref, lse_ref, q_s, k_s, v_s, mixed_s
):
    for source, target in ((q_ref, q_s), (k_ref, k_s), (v_ref, v_s)):
        place(order, source, target, rows, True)

    def body(at, to):
        forward_tile(at, to, seg_c, seg_r, lse_ref, q_s, k_s, v_s, mixed_s)

    each_tile(span, q_ref.shape[0], body)
    place(order, mixed_s, mixed_ref, rows, False)


def attend(qkv, segment, span, order, rows):
    length, width = qkv.shape[0], qkv.shape[1] // 3
    pairs = width // PAIR
    small = pl.BlockSpec(memory_space=pltpu.SMEM)
    third = lambda i: pl.BlockSpec((length, width), lambda h: (0, i))
    return pl.pallas_call(
        functools.partial(attend_kernel, rows),
        grid=(1,),
        in_specs=[
            small,
            small,
            pl.BlockSpec((length, 1), lambda h: (0, 0)),
            pl.BlockSpec((1, length), lambda h: (0, 0)),
            third(0),
            third(1),
            third(2),
        ],
        out_specs=[third(0), pl.BlockSpec((pairs, 2, length), lambda h: (0, 0, 0))],
        out_shape=[
            jax.ShapeDtypeStruct((length, width), bf16),
            jax.ShapeDtypeStruct((pairs, 2, length), f32),
        ],
        scratch_shapes=[pltpu.VMEM((length, width), bf16)] * 4,
        compiler_params=pltpu.CompilerParams(vmem_limit_bytes=48 * 1024 * 1024),
        cost_estimate=pl.CostEstimate(flops=0, bytes_accessed=0, transcendentals=0),
    )(order, span, segment[:, None], segment[None, :], qkv, qkv, qkv)


def back_tile(at, to, seg_c, seg_r, lse_ref, q_s, k_s, v_s, up_s, dq_s, dk_s, dv_s):
    same_item = seg_c[to, :] == seg_r[:, at]
    same_item = jnp.concatenate([same_item, same_item], axis=1)
    for pair in range(q_s.shape[1] // PAIR):
        cols = slice(pair * PAIR, (pair + 1) * PAIR)
        keys_all = k_s[to, cols]
        queries, upstream = two_heads(q_s[at, cols]), two_heads(up_s[at, cols])
        lse = jnp.concatenate([lse_ref[pair, 0:1, at], lse_ref[pair, 1:2, at]], axis=1)
        scores = mm(keys_all, queries, ((1,), (1,))) * (SCALE * LOG2E)
        probs = jnp.where(same_item, jnp.exp2(scores - lse), 0.0)
        grad_probs = mm(v_s[to, cols], upstream, ((1,), (1,)))
        weighted = probs * grad_probs
        inner = jnp.sum(weighted, axis=0, keepdims=True)
        grad_scores = (weighted - probs * inner).astype(bf16)
        dv_s[to, cols] += mm(probs.astype(bf16), upstream)
        dk_s[to, cols] += mm(grad_scores, queries)
        dq_s[at, cols] = (one_pair(mm(grad_scores, keys_all, ((0,), (0,)))) * SCALE).astype(bf16)


def attend_back_kernel(
    rows, order, span, seg_c, seg_r, q_ref, k_ref, v_ref, up_ref, lse_ref, dq_ref, dk_ref, dv_ref,
    q_s, k_s, v_s, up_s, dq_s, dk_s, dv_s,
):
    for source, target in ((q_ref, q_s), (k_ref, k_s), (v_ref, v_s), (up_ref, up_s)):
        place(order, source, target, rows, True)
    dk_s[...] = jnp.zeros_like(dk_s)
    dv_s[...] = jnp.zeros_like(dv_s)

    def body(at, to):
        back_tile(at, to, seg_c, seg_r, lse_ref, q_s, k_s, v_s, up_s, dq_s, dk_s, dv_s)

    each_tile(span, q_ref.shape[0], body)
    q_s[...] = (dk_s[...] * SCALE).astype(bf16)
    v_s[...] = dv_s[...].astype(bf16)
    for source, target in ((dq_s, dq_ref), (q_s, dk_ref), (v_s, dv_ref)):
        place(order, source, target, rows, False)


def attend_back(qkv, segment, span, order, rows, grad_mixed, lse):
    length, width = grad_mixed.shape
    pairs = width // PAIR
    small = pl.BlockSpec(memory_space=pltpu.SMEM)
    third = lambda i: pl.BlockSpec((length, width), lambda h: (0, i))
    return pl.pallas_call(
        functools.partial(attend_back_kernel, rows),
        grid=(1,),
        in_specs=[
            small,
            small,
            pl.BlockSpec((length, 1), lambda h: (0, 0)),
            pl.BlockSpec((1, length), lambda h: (0, 0)),
            third(0),
            third(1),
            third(2),
            third(0),
            pl.BlockSpec((pairs, 2, length), lambda h: (0, 0, 0)),
        ],
        out_specs=[third(0)] * 3,
        out_shape=[jax.ShapeDtypeStruct((length, width), bf16)] * 3,
        scratch_shapes=[pltpu.VMEM((length, width), bf16)] * 5 + [pltpu.VMEM((length, width), f32)] * 2,
        compiler_params=pltpu.CompilerParams(vmem_limit_bytes=48 * 1024 * 1024),
        cost_estimate=pl.CostEstimate(flops=0, bytes_accessed=0, transcendentals=0),
    )(order, span, segment[:, None], segment[None, :], qkv, qkv, qkv, grad_mixed, lse)


def gelu_parts(pre):
    size = jnp.abs(pre)
    t = 1.0 / (1.0 + (0.3275911 * math.sqrt(0.5)) * size)
    bell = jnp.exp2((-0.5 * LOG2E) * (pre * pre))
    poly = t * (0.127414796 + t * (-0.142248368 + t * (0.7107068705 + t * (-0.7265760135 + t * 0.5307027145))))
    below = poly * bell
    below = jnp.where(pre >= 0, 1.0 - below, below)
    return pre * below, below + (pre * bell) * (1.0 / math.sqrt(2.0 * math.pi))


def widen_kernel(chunk, x_ref, w_ref, bias_ref, hidden_ref, slope_ref):
    for at in range(0, x_ref.shape[0], chunk):
        rows = slice(at, at + chunk)
        hidden, slope = gelu_parts(mm(x_ref[rows, :], w_ref[...]) + bias_ref[...])
        hidden_ref[rows, :] = hidden.astype(bf16)
        slope_ref[rows, :] = slope.astype(bf16)


def widen(x, weight, bias):
    count, width = x.shape
    units = weight.shape[1]
    step = 256
    return pl.pallas_call(
        functools.partial(widen_kernel, 144),
        grid=(units // step,),
        in_specs=[
            pl.BlockSpec((count, width), lambda i: (0, 0)),
            pl.BlockSpec((width, step), lambda i: (0, i)),
            pl.BlockSpec((1, step), lambda i: (0, i)),
        ],
        out_specs=[pl.BlockSpec((count, step), lambda i: (0, i))] * 2,
        out_shape=[jax.ShapeDtypeStruct((count, units), bf16)] * 2,
        compiler_params=pltpu.CompilerParams(vmem_limit_bytes=48 * 1024 * 1024),
        cost_estimate=pl.CostEstimate(flops=0, bytes_accessed=0, transcendentals=0),
    )(x, weight, bias[None])


def gather_kernel(seqs, dp_size, tp_size, *refs):
    seq_ref, bias_ref = refs[:2]
    blocks = refs[2:8]
    time_ref, time_weight, time_bias, seg_c, seg_r = refs[8:13]
    start_ref, biases_ref, joined_ref, out_ref, in_ref, ffn_out_ref = refs[13:19]
    tokens_ref, qkv_ref, mixed_ref, lse_ref = refs[19:23]
    local_sem, seq_send, seq_get, up_send, up_get, down_send, down_get, side_send, side_get = refs[23:32]
    start_s, joined_s, q_s, k_s, v_s, mixed_s, x_sem, load_sem = refs[32:]
    zs, dp, tp = lax.axis_index("zs"), lax.axis_index("dp"), lax.axis_index("tp")
    rows = seq_ref.shape[1]
    own_count = seqs * rows
    length, heads_all = mixed_ref.shape
    width, hc = blocks[0].shape
    units = blocks[4].shape[1]
    part = width // dp_size
    half = units // 2
    table = [(0, 0, hc), (1, 0, hc), (2, 0, hc), (3, 0, hc)]
    table += [(4, 0, half), (4, half, half), (5, 0, half), (5, half, half)]
    kinds = range(len(table))

    def home(kind, slot, other):
        array, first, size = table[kind]
        features = slice(other * part, (other + 1) * part)
        if array < 3:
            at = (array * seqs + slot) * hc
            return joined_ref.at[features, at : at + hc]
        if array == 3:
            return out_ref.at[slot * hc : (slot + 1) * hc, features]
        at = slice(slot * units + first, slot * units + first + size)
        return in_ref.at[features, at] if array == 4 else ffn_out_ref.at[at, features]

    def own(kind, other):
        array, first, size = table[kind]
        features = pl.ds(pl.multiple_of(lax.rem(dp + other, dp_size) * part, part), part)
        if array in (3, 5):
            return blocks[array].at[first : first + size, features]
        return blocks[array].at[features, first : first + size]

    def to(axis, at, source, target, send, get):
        return pltpu.make_async_remote_copy(
            src_ref=source,
            dst_ref=target,
            send_sem=send,
            recv_sem=get,
            device_id={axis: at},
            device_id_type=pl.DeviceIdType.MESH,
        )

    def sequence(by):
        at = lax.rem(zs - by + seqs, seqs)
        return to("zs", at, seq_ref.at[at], start_ref.at[by], seq_send.at[by], seq_get.at[by])

    def bias(by):
        at = lax.rem(zs - by + seqs, seqs)
        return to("zs", at, bias_ref, biases_ref.at[by], seq_send.at[seqs + by], seq_get.at[seqs + by])

    def up(kind, hop):
        source = own(kind, 0) if hop == 0 else home(kind, seqs - hop, 0)
        target = home(kind, seqs - hop - 1, 0)
        return to("zs", zs + 1, source, target, up_send.at[kind, hop], up_get.at[kind, hop])

    def down(kind, hop):
        source = own(kind, 0) if hop == 0 else home(kind, hop, 0)
        target = home(kind, hop + 1, 0)
        return to("zs", zs - 1, source, target, down_send.at[kind, hop], down_get.at[kind, hop])

    def side(kind, slot, other):
        at = lax.rem(dp - other + dp_size, dp_size)
        place = side_send.at[kind, slot, other], side_get.at[kind, slot, other]
        return to("dp", at, home(kind, slot, 0), home(kind, slot, other), *place)

    def local(kind, other):
        return pltpu.make_async_copy(own(kind, other), home(kind, 0, other), local_sem.at[kind, other])

    barrier = pltpu.get_barrier_semaphore()
    for axis, at, size in (("zs", zs, seqs), ("dp", dp, dp_size), ("tp", tp, tp_size)):
        for by in range(1, size):
            pl.semaphore_signal(
                barrier,
                inc=1,
                device_id={axis: lax.rem(at + by, size)},
                device_id_type=pl.DeviceIdType.MESH,
            )
    pl.semaphore_wait(barrier, seqs + dp_size + tp_size - 3)

    for by in range(1, seqs):
        sequence(by).start()
        bias(by).start()
    def begin(kind):
        @pl.when(zs < seqs - 1)
        def _():
            up(kind, 0).start()

        @pl.when(zs > 0)
        def _():
            down(kind, 0).start()

    for kind in kinds[:AHEAD]:
        begin(kind)

    own_seq = pltpu.make_async_copy(seq_ref.at[zs], start_ref.at[0], local_sem.at[len(table), 0])
    own_bias = pltpu.make_async_copy(bias_ref, biases_ref.at[0], local_sem.at[len(table), 1])
    own_seq.start()
    own_bias.start()
    for kind in kinds:
        for other in range(dp_size):
            local(kind, other).start()

    def pass_on(kind, hop):
        @pl.when(zs >= hop)
        def _():
            up(kind, hop - 1).wait_recv()
            if hop < seqs - 1:

                @pl.when(zs < seqs - 1)
                def _():
                    up(kind, hop).start()

            for other in range(1, dp_size):
                side(kind, seqs - hop, other).start()

        @pl.when(zs + hop < seqs)
        def _():
            down(kind, hop - 1).wait_recv()
            if hop < seqs - 1:

                @pl.when(zs > 0)
                def _():
                    down(kind, hop).start()

            for other in range(1, dp_size):
                side(kind, hop, other).start()

    def exchange():
        here, there = tokens_ref.at[:own_count, :], tokens_ref.at[own_count:, :]
        return to("tp", 1 - tp, here, there, x_sem.at[0], x_sem.at[1])

    def placed(block):
        member, chip = divmod(block, seqs)
        at = lax.rem(zs + chip, seqs) * tp_size + lax.rem(tp + member, tp_size)
        return pl.ds(pl.multiple_of(at * rows, 16), rows)

    load_start = pltpu.make_async_copy(start_ref, start_s, load_sem.at[0])
    load_joined = pltpu.make_async_copy(joined_ref, joined_s, load_sem.at[1])

    def tokens():
        own_seq.wait()
        for by in range(1, seqs):
            sequence(by).wait()
        load_start.start()
        load_start.wait()
        for block in range(seqs):
            at = slice(block * rows, (block + 1) * rows)
            residual = start_s[block].astype(f32) + time_ref[at, :] * time_weight[...] + time_bias[...]
            tokens_ref[at, :] = residual.astype(bf16)
        exchange().start()

    def joined_there():
        for kind in range(3):
            for other in range(dp_size):
                local(kind, other).wait()
            for slot in range(1, seqs):
                for other in range(1, dp_size):
                    side(kind, slot, other).wait()
        load_joined.start()
        own_bias.wait()
        for by in range(1, seqs):
            bias(by).wait()
        exchange().wait()
        load_joined.wait()

    def project(member):
        here = slice(member * own_count, (member + 1) * own_count)
        for third, target in enumerate((q_s, k_s, v_s)):
            cols = slice(third * heads_all, (third + 1) * heads_all)
            found = mm(tokens_ref[here, :], joined_s[:, cols])
            if third != 1:
                at = slice(third // 2 * hc, third // 2 * hc + hc)
                found = found + jnp.concatenate([biases_ref[slot, :, at] for slot in range(seqs)], axis=1)
            found = found.astype(bf16)
            qkv_ref[here, cols] = found
            for chip in range(seqs):
                target[placed(member * seqs + chip), :] = found[chip * rows : (chip + 1) * rows]

    def attention(tiles):
        def body(at, to):
            forward_tile(at, to, seg_c, seg_r, lse_ref, q_s, k_s, v_s, mixed_s)

        banded(tiles, length, body)

    def mixed_out():
        for block in range(seqs * tp_size):
            mixed_ref[block * rows : (block + 1) * rows, :] = mixed_s[placed(block), :]

    tiles = length // TILE
    for step in range(len(kinds) + seqs - 2):
        for hop in range(1, seqs):
            if 0 <= step - hop + 1 < len(kinds):
                pass_on(step - hop + 1, hop)
        if step + AHEAD < len(kinds):
            begin(step + AHEAD)
        if step == 2:
            tokens()
        if step == seqs:
            joined_there()
            for member in range(tp_size):
                project(member)
        if step == seqs + 1:
            attention(range(tiles // 3))
        if step == seqs + 2:
            attention(range(tiles // 3, 2 * tiles // 3))
        if step == seqs + 3:
            attention(range(2 * tiles // 3, tiles))
            mixed_out()

    for kind in kinds:
        if kind >= 3:
            for other in range(dp_size):
                local(kind, other).wait()
            for slot in range(1, seqs):
                for other in range(1, dp_size):
                    side(kind, slot, other).wait()
        for hop in range(seqs - 1):

            @pl.when((zs >= hop) & (zs < seqs - 1))
            def _():
                up(kind, hop).wait_send()

            @pl.when((zs + hop < seqs) & (zs > 0))
            def _():
                down(kind, hop).wait_send()


def gather_all(by_seq, biases, blocks, tokenwise, dp_size, tp_size):
    seqs, rows, width = by_seq.shape
    hc, units = blocks[0].shape[1], blocks[4].shape[1]
    length, heads_all = seqs * rows * tp_size, seqs * hc
    anywhere = pl.BlockSpec(memory_space=pl.ANY)
    inside = pl.BlockSpec(memory_space=pltpu.VMEM)
    low = lambda *shape: jax.ShapeDtypeStruct(shape, bf16)
    held = lambda *shape: pltpu.VMEM(shape, bf16)
    dma = pltpu.SemaphoreType.DMA
    kinds = 8
    return pl.pallas_call(
        functools.partial(gather_kernel, seqs, dp_size, tp_size),
        in_specs=[anywhere] * (2 + len(blocks)) + [inside] * 5,
        out_specs=[anywhere, inside] + [anywhere] * 4 + [inside] * 4,
        out_shape=[
            jax.ShapeDtypeStruct(by_seq.shape, bf16),
            jax.ShapeDtypeStruct((seqs,) + biases.shape, f32),
            low(width, 3 * heads_all),
            low(heads_all, width),
            low(width, seqs * units),
            low(seqs * units, width),
            low(length, width),
            low(length, 3 * heads_all),
            low(length, heads_all),
            jax.ShapeDtypeStruct((heads_all // PAIR, 2, length), f32),
        ],
        scratch_shapes=[
            dma((kinds + 1, max(dp_size, 2))),
            dma((2 * seqs,)),
            dma((2 * seqs,)),
            dma((kinds, seqs - 1)),
            dma((kinds, seqs - 1)),
            dma((kinds, seqs - 1)),
            dma((kinds, seqs - 1)),
            dma((kinds, seqs, dp_size)),
            dma((kinds, seqs, dp_size)),
            held(*by_seq.shape),
            held(width, 3 * heads_all),
            held(length, heads_all),
            held(length, heads_all),
            held(length, heads_all),
            held(length, heads_all),
            dma((2,)),
            dma((2,)),
        ],
        compiler_params=pltpu.CompilerParams(
            collective_id=0, has_side_effects=True, vmem_limit_bytes=56 * 1024 * 1024
        ),
    )(by_seq, biases, *blocks, *tokenwise)


def scatter_kernel(rows, seqs, dp_size, tp_size, *refs):
    seq_ref, small_ref, slots_ref = refs[:3]
    operands_before, operands_last = refs[3:9], refs[9:15]
    qkv_ref, up_ref, lse_ref, seg_c, seg_r, joined_ref, resid_ref, time_ref = refs[15:23]
    tokens_last, tokens_before, gq_before = refs[23:26]
    seq_out, small_out, slots_out = refs[26:29]
    outs = refs[29:35]
    sides, ups, downs = refs[35:39], refs[39:43], refs[43:47]
    small_zs, small_all, slots_zs, slots_dp = refs[47:51]
    seq_send, seq_get, local_sem, small_send, small_get = refs[51:56]
    side_send, side_get, up_send, up_get, down_send, down_get = refs[56:62]
    wide_s, dq_s, dk_s, dv_s, gq_s, tokens_s = refs[62:68]
    x_send, x_get, seq_s, small_s, slots_s = refs[68:73]
    mine, theirs = refs[73:77], refs[77:81]
    place_sem, x_sem, load_sem = refs[81:84]
    joined_mine, joined_theirs = mine[3], theirs[3]
    heads_all = dq_s.shape[1]
    q_s, k_s, v_s, up_s = [wide_s.at[:, i * heads_all : (i + 1) * heads_all] for i in range(4)]
    first_stage = lax.axis_index("pipe") == 0
    zs, dp, tp = lax.axis_index("zs"), lax.axis_index("dp"), lax.axis_index("tp")
    units = mine[0].shape[0] // seqs
    hc = mine[2].shape[0] // seqs
    half = units // 2
    length = dq_s.shape[0]
    own_count, width = resid_ref.shape
    part = width // dp_size
    kinds = [(0, 0, 0, half), (0, 0, half, half), (1, 1, 0, half), (1, 1, half, half), (2, 0, 0, hc)]
    kinds += [(3, 1, third * seqs * hc, hc) for third in range(3)]

    def cut(arrays, kind, slot):
        array, axis, first, size = kinds[kind]
        apart = units if array < 2 else hc
        at = slice(first + slot * apart, first + slot * apart + size)
        return arrays[array].at[at, :] if axis == 0 else arrays[array].at[:, at]

    def to(where, source, target, send, get):
        return pltpu.make_async_remote_copy(
            src_ref=source,
            dst_ref=target,
            send_sem=send,
            recv_sem=get,
            device_id=where,
            device_id_type=pl.DeviceIdType.MESH,
        )

    def sequence(by):
        at = lax.rem(zs + by, seqs)
        return to({"zs": at}, seq_s.at[by], seq_out.at[zs], seq_send.at[by], seq_get.at[by])

    def side(kind, slot):
        place = side_send.at[kind, slot], side_get.at[kind, slot]
        return to({"dp": 1 - dp}, cut(theirs, kind, slot), cut(sides, kind, slot), *place)

    def up(kind, far):
        place = up_send.at[kind, far], up_get.at[kind, far]
        return to({"zs": zs + 1}, cut(sides, kind, far), cut(ups, kind, far - 1), *place)

    def down(kind, far):
        place = down_send.at[kind, far], down_get.at[kind, far]
        return to({"zs": zs - 1}, cut(sides, kind, seqs - far), cut(downs, kind, far - 1), *place)

    def small(by):
        at = {"zs": lax.rem(zs + by, seqs)}
        return to(at, small_s, small_zs.at[by], small_send.at[0, by], small_get.at[0, by])

    def slots(by):
        at = {"zs": lax.rem(zs + by, seqs)}
        return to(at, slots_s.at[by], slots_zs.at[by], small_send.at[1, by], small_get.at[1, by])

    def small_across(by):
        at = lax.rem(dp * tp_size + tp + by, dp_size * tp_size)
        where = {"dp": lax.div(at, tp_size), "tp": lax.rem(at, tp_size)}
        return to(where, small_all.at[0], small_all.at[by], small_send.at[2, by], small_get.at[2, by])

    def slots_across():
        return to({"dp": 1 - dp}, slots_dp.at[0], slots_dp.at[1], small_send.at[3, 0], small_get.at[3, 0])

    def added(target, *others):
        rows = target.shape[0]
        step = 64

        def body(i, carry):
            at = pl.ds(pl.multiple_of(i * step, step), step)
            total = target[at, :].astype(f32)
            for other in others:
                total = total + other[at, :].astype(f32)
            target[at, :] = total.astype(target.dtype)
            return carry

        lax.fori_loop(0, rows // step, body, 0)

    barrier = pltpu.get_barrier_semaphore()
    greeted = [{"zs": lax.rem(zs + by, seqs)} for by in range(1, seqs)]
    for by in range(1, dp_size * tp_size):
        at = lax.rem(dp * tp_size + tp + by, dp_size * tp_size)
        greeted.append({"dp": lax.div(at, tp_size), "tp": lax.rem(at, tp_size)})
    for where in greeted:
        pl.semaphore_signal(barrier, inc=1, device_id=where, device_id_type=pl.DeviceIdType.MESH)
    pl.semaphore_wait(barrier, len(greeted))

    slot_order = list(range(1, seqs)) + [0]

    def begin(kind):
        for slot in slot_order:
            side(kind, slot).start()

    def placed(block, array):
        member, chip = divmod(block, seqs)
        at = lax.rem(zs + chip, seqs) * tp_size + lax.rem(tp + member, tp_size)
        at = pl.ds(pl.multiple_of(at * rows, 16), rows)
        here = slice(block * rows, (block + 1) * rows)
        if array < 3:
            source = qkv_ref.at[here, array * heads_all : (array + 1) * heads_all]
        else:
            source = up_ref.at[here, :]
        target = (q_s, k_s, v_s, up_s)[array].at[at, :]
        return pltpu.make_async_copy(source, target, place_sem.at[array, block])

    def each_placed(act):
        for array in range(4):
            for block in range(length // rows):
                act(placed(block, array))

    own_tokens = pltpu.make_async_copy(tokens_last, tokens_s, local_sem.at[1])
    old_tokens = pltpu.make_async_copy(tokens_before, tokens_s, local_sem.at[1])
    old_grads = pltpu.make_async_copy(gq_before, gq_s, local_sem.at[2])
    old_seq = pltpu.make_async_copy(seq_ref, seq_s, local_sem.at[3])

    def attention(tiles):
        def body(at, to):
            back_tile(at, to, seg_c, seg_r, lse_ref, q_s, k_s, v_s, up_s, dq_s, dk_s, dv_s)

        banded(tiles, length, body)

    def attention_start():
        @pl.when(first_stage)
        def _():
            own_tokens.start()
            each_placed(lambda copy: copy.start())
            dk_s[...] = jnp.zeros_like(dk_s)
            dv_s[...] = jnp.zeros_like(dv_s)
            each_placed(lambda copy: copy.wait())
            attention(range(length // TILE // 2))

        @pl.when(jnp.logical_not(first_stage))
        def _():
            old_tokens.start()
            old_grads.start()
            old_seq.start()

    def attention_end():
        @pl.when(first_stage)
        def _():
            attention(range(length // TILE // 2, length // TILE))
            q_s[...] = (dk_s[...] * SCALE).astype(bf16)
            v_s[...] = dv_s[...].astype(bf16)
            for third, source in enumerate((dq_s, q_s, v_s)):
                cols = slice(third * heads_all, (third + 1) * heads_all)
                for block in range(length // rows):
                    member, chip = divmod(block, seqs)
                    at = lax.rem(zs + chip, seqs) * tp_size + lax.rem(tp + member, tp_size)
                    at = pl.ds(pl.multiple_of(at * rows, 16), rows)
                    gq_s[block * rows : (block + 1) * rows, cols] = source[at, :]
            own_tokens.wait()

        @pl.when(jnp.logical_not(first_stage))
        def _():
            old_tokens.wait()
            old_grads.wait()
            old_seq.wait()

    def joined_parts():
        step = 256
        for other in reversed(range(dp_size)):
            target = joined_mine if other == 0 else joined_theirs
            for third in range(3):
                cols = slice(third * heads_all, (third + 1) * heads_all)
                for at in range(0, part, step):
                    left = tokens_s[:, other * part + at : other * part + at + step]
                    target[at : at + step, cols] = mm(left, gq_s[:, cols], ((0,), (0,))).astype(bf16)

    def exchange():
        return to({"tp": 1 - tp}, x_send, x_get, x_sem.at[0], x_sem.at[1])

    def input_grads():
        @pl.when(first_stage)
        def _():
            def theirs_rows(i, carry):
                at = pl.multiple_of(i * rows, 16)
                x_send[pl.ds(at, rows), :] = mm(
                    gq_s[pl.ds(own_count + at, rows), :], joined_ref[...], ((1,), (1,))
                ).astype(bf16)
                return carry

            lax.fori_loop(0, seqs, theirs_rows, 0)
            exchange().start()
            for slot in range(seqs):
                cols = slice(slot * hc, (slot + 1) * hc)
                slots_s[slot, 0:1, :] = jnp.sum(gq_s[:, cols].astype(f32), axis=0, keepdims=True)
                cols = slice(2 * heads_all + slot * hc, 2 * heads_all + (slot + 1) * hc)
                slots_s[slot, 1:2, :] = jnp.sum(gq_s[:, cols].astype(f32), axis=0, keepdims=True)
            exchange().wait()

            def own_rows(i, carry):
                at = pl.ds(pl.multiple_of(i * rows, 16), rows)
                total = mm(gq_s[at, :], joined_ref[...], ((1,), (1,)))
                total = total + x_get[at, :].astype(f32) + resid_ref[at, :]
                lowered = total.astype(bf16)
                for other in range(dp_size):
                    cols = pl.ds(pl.multiple_of(lax.rem(dp + other, dp_size) * part, part), part)
                    seq_s[i, :, cols] = lowered[:, other * part : (other + 1) * part]
                timed = jnp.sum(total * time_ref[at, :], axis=0, keepdims=True)
                plain = jnp.sum(total, axis=0, keepdims=True)
                return carry[0] + timed, carry[1] + plain

            zero = jnp.zeros((1, width), f32)
            timed, plain = lax.fori_loop(0, seqs, own_rows, (zero, zero))
            for other in range(dp_size):
                cols = pl.ds(pl.multiple_of(lax.rem(dp + other, dp_size) * part, part), part)
                here = slice(other * part, (other + 1) * part)
                small_s[0:1, cols] = timed[:, here]
                small_s[1:2, cols] = plain[:, here]

    own_seq = pltpu.make_async_copy(seq_s.at[0], seq_out.at[zs], local_sem.at[0])

    def send_small():
        for by in range(1, seqs):
            small(by).start()
            slots(by).start()
        for by in range(1, seqs):
            sequence(by).start()
        own_seq.start()

    def add_small():
        total, slot_total = small_s[...], slots_s[0]
        for by in range(1, seqs):
            small(by).wait()
            slots(by).wait()
            total = total + small_zs[by]
            slot_total = slot_total + slots_zs[by]
        small_all[0] = total
        slots_dp[0] = slot_total
        for by in range(1, dp_size * tp_size):
            small_across(by).start()
        slots_across().start()

    small_s[...] = small_ref[...]
    slots_s[...] = slots_ref[...]
    def load(index, target):
        def copies(operands):
            return pltpu.make_async_copy(operands[index], target, load_sem.at[index])

        @pl.when(first_stage)
        def _():
            copies(operands_last).start()

        @pl.when(jnp.logical_not(first_stage))
        def _():
            copies(operands_before).start()

        return copies(operands_last)

    def product(kind, other):
        array, axis, first, size = kinds[kind]
        target = (mine if other == 0 else theirs)[array]
        features = slice(other * part, (other + 1) * part)
        for slot in range(seqs):
            apart = units if array < 2 else hc
            at = slice(first + slot * apart, first + slot * apart + size)
            if axis == 0:
                left = dq_s if array == 2 else wide_s
                target[at, :] = mm(left[:, at], tokens_s[:, features], ((0,), (0,))).astype(bf16)
            else:
                found = mm(tokens_s[:, features], wide_s[:, at], ((0,), (0,)))
                target[:, at] = found.astype(bf16)

    hidden, grads = load(0, wide_s), load(1, tokens_s)
    hidden.wait()
    grads.wait()
    for kind in (0, 1):
        for other in reversed(range(dp_size)):
            product(kind, other)
            if other == 1:
                begin(kind)
    inputs, grads = load(2, tokens_s), load(3, wide_s)
    inputs.wait()
    grads.wait()
    for kind in (2, 3):
        for other in range(dp_size):
            product(kind, other)
    mixed, grads = load(4, dq_s), load(5, tokens_s)
    mixed.wait()
    grads.wait()
    for other in range(dp_size):
        product(4, other)
    attention_start()

    def taken(kind):
        for slot in slot_order:
            side(kind, slot).wait()
            added(cut(sides, kind, slot), cut(mine, kind, slot))

    def pass_on(kind, hop):
        @pl.when((zs == hop) & (zs < seqs - 1))
        def _():
            for far in range(seqs - 1 - hop, 0, -1):
                if hop > 0:
                    up(kind, far + 1).wait_recv()
                    added(cut(sides, kind, far), cut(ups, kind, far))
                up(kind, far).start()

        @pl.when((zs == seqs - 1 - hop) & (zs > 0))
        def _():
            for far in range(seqs - 1 - hop, 0, -1):
                if hop > 0:
                    down(kind, far + 1).wait_recv()
                    added(cut(sides, kind, seqs - far), cut(downs, kind, far))
                down(kind, far).start()

    for step in range(len(kinds) + seqs - 2):
        if step < len(kinds):
            taken(step)
            if step + AHEAD < len(kinds):
                begin(step + AHEAD)
        for hop in range(seqs - 1):
            if 0 <= step - hop < len(kinds):
                pass_on(step - hop, hop)
        if step == 0:
            attention_end()
        if step == 1:
            joined_parts()
            input_grads()
            send_small()
        if step == 4:
            add_small()

    total, slot_total = small_all[0], slots_dp[0]
    for by in range(1, dp_size * tp_size):
        small_across(by).wait()
        total = total + small_all[by]
    slots_across().wait()
    small_out[...] = total
    slots_out[...] = slot_total + slots_dp[1]

    for kind, (array, axis, first, size) in enumerate(kinds):
        out = outs[array] if array < 3 else outs[3 + first // (seqs * hc)]
        if array < 2:
            out = out.at[first : first + size, :] if axis == 0 else out.at[:, first : first + size]
        out[...] = cut(sides, kind, 0)[...].astype(f32)

        @pl.when(zs > 0)
        def _():
            up(kind, 1).wait_recv()
            added(out, cut(ups, kind, 0))

        @pl.when(zs < seqs - 1)
        def _():
            down(kind, 1).wait_recv()
            added(out, cut(downs, kind, 0))

        for far in range(1, seqs):

            @pl.when(zs + far < seqs)
            def _():
                up(kind, far).wait_send()

            @pl.when(zs >= far)
            def _():
                down(kind, far).wait_send()

    own_seq.wait()
    for by in range(1, seqs):
        sequence(by).wait()


def scatter_all(rows, by_block, small, slots, operands, attended, tokens, gq_before, tp_size):
    seqs, _, width = by_block.shape
    dp_size = 2
    units, part = operands[0].shape[1] // seqs, width // dp_size
    length, heads_all = tokens[0].shape[0], gq_before.shape[1] // 3
    hc = heads_all // seqs
    own_count = length // tp_size
    anywhere = pl.BlockSpec(memory_space=pl.ANY)
    inside = pl.BlockSpec(memory_space=pltpu.VMEM)
    wide = lambda *shape: jax.ShapeDtypeStruct(shape, f32)
    low = lambda *shape: pltpu.VMEM(shape, bf16)
    dma = pltpu.SemaphoreType.DMA
    like = [low(seqs * units, part), low(part, seqs * units), low(heads_all, part), low(part, 3 * heads_all)]
    fewer = [low((seqs - 1) * units, part), low(part, (seqs - 1) * units), low((seqs - 1) * hc, part)]
    fewer.append(low(part, 3 * heads_all))
    kinds = 8
    return pl.pallas_call(
        functools.partial(scatter_kernel, rows, seqs, dp_size, tp_size),
        in_specs=[anywhere, inside, inside]
        + [anywhere] * 12
        + [anywhere, anywhere]
        + [inside] * 6
        + [anywhere] * 3,
        out_specs=[anywhere] + [inside] * 8,
        out_shape=[
            jax.ShapeDtypeStruct(by_block.shape, bf16),
            wide(*small.shape),
            wide(*slots.shape[1:]),
            wide(units, part),
            wide(part, units),
            wide(hc, part),
            wide(part, hc),
            wide(part, hc),
            wide(part, hc),
        ],
        scratch_shapes=like
        + fewer * 2
        + [
            pltpu.VMEM((seqs,) + small.shape, f32),
            pltpu.VMEM((dp_size * tp_size,) + small.shape, f32),
            pltpu.VMEM(slots.shape, f32),
            pltpu.VMEM((2,) + slots.shape[1:], f32),
            dma((seqs,)),
            dma((seqs,)),
            dma((4,)),
            dma((4, max(seqs, dp_size * tp_size))),
            dma((4, max(seqs, dp_size * tp_size))),
        ]
        + [dma((kinds, seqs))] * 6
        + [low(length, 4 * heads_all), low(length, heads_all)]
        + [pltpu.VMEM((length, heads_all), f32)] * 2
        + [
            low(length, 3 * heads_all),
            low(length, width),
            low(own_count, width),
            low(own_count, width),
            low(*by_block.shape),
            pltpu.VMEM(small.shape, f32),
            pltpu.VMEM(slots.shape, f32),
        ]
        + like * 2
        + [dma((4, length // rows)), dma((2,)), dma((6,))],
        compiler_params=pltpu.CompilerParams(
            collective_id=1, has_side_effects=True, vmem_limit_bytes=63 * 1024 * 1024
        ),
    )(by_block, small, slots, *operands, *attended, *tokens, gq_before)


def per_device(
    states,
    cotangent,
    lengths,
    timesteps,
    time_weight,
    time_bias,
    query_weight,
    query_bias,
    key_weight,
    value_weight,
    value_bias,
    out_weight,
    out_bias,
    attn_gain,
    attn_shift,
    ffn_in,
    ffn_in_bias,
    ffn_out,
    ffn_out_bias,
    ffn_gain,
    ffn_shift,
):
    rows, seqs, width = states.shape
    own_count = seqs * rows
    sections, section_at = lax.axis_size("pipe"), lax.axis_index("pipe")
    dp_size, dp_at = lax.axis_size("dp"), lax.axis_index("dp")
    zs_at = lax.axis_index("zs")
    tp_size, tp_at = lax.axis_size("tp"), lax.axis_index("tp")
    length = own_count * tp_size
    part = width // dp_size
    head_cols, unit_cols = query_weight.shape[2], ffn_in.shape[2]
    heads_all, units_all = head_cols * seqs, unit_cols * seqs

    def rotated(array, axis=-1):
        axis = axis % array.ndim
        twice = jnp.concatenate([array, array], axis=axis)
        return lax.dynamic_slice_in_dim(twice, dp_at * part, width, axis)

    def straightened(array):
        twice = jnp.concatenate([array, array], axis=-1)
        back = (dp_size - dp_at) % dp_size
        return lax.dynamic_slice_in_dim(twice, back * part, width, array.ndim - 1)

    vectors = rotated(
        jnp.concatenate(
            [time_weight, time_bias, out_bias, attn_gain, attn_shift, ffn_out_bias, ffn_gain, ffn_shift]
        )
    )
    time_weight, time_bias, out_bias, attn_gain = vectors[0], vectors[1], vectors[2], vectors[3]
    attn_shift, ffn_out_bias, ffn_gain, ffn_shift = vectors[4], vectors[5], vectors[6], vectors[7]


    def to_sequence(array):
        by_seq = rotated(jnp.transpose(array, (1, 0, 2)))
        got = []
        for by in range(seqs):
            block = lax.dynamic_index_in_dim(by_seq, (zs_at - by) % seqs, 0, keepdims=False)
            got.append(received(block, "zs", by))
        return got

    def to_positions(array):
        by_block = straightened(array).reshape(seqs, rows, width)
        return [received(by_block[(seqs - by) % seqs], "zs", by)[None] for by in range(seqs)]

    def in_positions(got, *before):
        got = [after(piece, *before)[0] for piece in got]
        by_seq = []
        for at in range(seqs):
            found = got[0]
            for by in range(1, seqs):
                found = jnp.where((zs_at + by) % seqs == at, got[by], found)
            by_seq.append(found)
        return jnp.stack(by_seq, axis=1)

    item_ends = jnp.cumsum(lax.dynamic_index_in_dim(lengths, zs_at, 0, keepdims=False))
    own_times = lax.dynamic_index_in_dim(timesteps, zs_at, 0, keepdims=False).astype(f32)
    member = (tp_at + jnp.arange(tp_size, dtype=jnp.int32)) % tp_size
    chips = (zs_at + jnp.arange(seqs, dtype=jnp.int32)) % seqs
    order = (chips[None, :] * tp_size + member[:, None]).reshape(seqs * tp_size).astype(jnp.int32)

    def segment_at(places):
        return jnp.sum((item_ends[None, :] <= places[:, None]).astype(jnp.int32), axis=1)

    segment = segment_at(jnp.arange(length, dtype=jnp.int32))
    span = key_spans(item_ends, length)
    own_places = order[:seqs, None] * rows + jnp.arange(rows, dtype=jnp.int32)[None, :]
    own_segment = segment_at(own_places.reshape(own_count))
    own_pick = own_segment[:, None] == jnp.arange(lengths.shape[1], dtype=jnp.int32)[None, :]
    time_rows = (jnp.sum(jnp.where(own_pick, own_times[None, :], 0.0), axis=1) / STEPS)[:, None]
    aligned = rows % 16 == 0
    kernel_rows = rows if aligned else length
    kernel_order = order if aligned else jnp.zeros((1,), jnp.int32)

    def by_position(array):
        if aligned:
            return array
        blocks = array.reshape(seqs * tp_size, rows, array.shape[1])
        return jnp.take(blocks, jnp.argsort(order), axis=0).reshape(array.shape)

    def by_distance(array):
        if aligned:
            return array
        blocks = array.reshape(seqs * tp_size, rows, array.shape[1])
        return jnp.take(blocks, order, axis=0).reshape(array.shape)


    def over_zs(block, axis, *before):
        mine = lax.dynamic_slice_in_dim(block, dp_at * part, part, axis)
        mine = after(mine, *before)
        return [received(mine, "zs", by) for by in range(1, seqs)]

    def over_dp(pieces):
        return [[received(piece, "dp", other) for other in range(dp_size)] for piece in pieces]

    def assembled(block, axis, pieces, thirds):
        across = 1 - axis
        each = block.shape[across] // thirds
        shape = [0, 0]
        shape[axis], shape[across] = width, block.shape[across] * seqs
        whole = jnp.zeros(shape, block.dtype)

        def put(whole, piece, slot, at):
            for third in range(thirds):
                start = [0, 0]
                start[axis], start[across] = at, (third * seqs + slot) * each
                cut = lax.slice_in_dim(piece, third * each, (third + 1) * each, axis=across)
                whole = lax.dynamic_update_slice(whole, cut, start)
            return whole

        whole = put(whole, rotated(block, axis), 0, 0)
        for slot, row in enumerate(pieces):
            for other, piece in enumerate(row):
                whole = put(whole, piece, slot + 1, other * part)
        return whole

    biases = jnp.concatenate([query_bias[0], value_bias[0], ffn_in_bias[0].astype(f32)])[None]
    in_kernels = sections == 2 and dp_size == 2 and tp_size == 2 and rows % 16 == 0
    in_kernels = in_kernels and head_cols == 128 and part % 256 == 0 and unit_cols % 256 == 0
    if in_kernels:
        by_seq = rotated(jnp.transpose(states, (1, 0, 2)))
        blocks = (query_weight, key_weight, value_weight, out_weight, ffn_in, ffn_out)
        tokenwise = (time_rows, time_weight[None], time_bias[None], segment[:, None], segment[None, :])
        start, bias_slots, joined, out_all, in_all, ffn_out_all, *attended_first = gather_all(
            by_seq, biases, [block[0] for block in blocks], tokenwise, dp_size, tp_size
        )
        start_rows = start.reshape(own_count, width)
        bias_slots = bias_slots[:, 0]
    else:
        joined_block = jnp.concatenate([query_weight[0], key_weight[0], value_weight[0]], axis=1)
        start_pieces = to_sequence(states)
        start_rows = jnp.concatenate(start_pieces)
        bias_slots = [received(biases, "zs", by)[0] for by in range(seqs)]
        joined_zs = over_zs(joined_block, 0)
        out_zs = over_zs(out_weight[0], 1, *joined_zs, *start_pieces)
        in_zs = over_zs(ffn_in[0], 0, *out_zs)
        ffn_out_zs = over_zs(ffn_out[0], 1, *in_zs)
        joined = assembled(joined_block, 0, over_dp(joined_zs), 3)
        out_all = assembled(out_weight[0], 1, over_dp(out_zs), 1)
        in_all = assembled(ffn_in[0], 0, over_dp(in_zs), 1)
        ffn_out_all = assembled(ffn_out[0], 1, over_dp(ffn_out_zs), 1)
    query_bias_all = jnp.concatenate([b[:head_cols] for b in bias_slots])
    value_bias_all = jnp.concatenate([b[head_cols : 2 * head_cols] for b in bias_slots])
    in_bias_all = jnp.concatenate([b[2 * head_cols :] for b in bias_slots])
    joined_bias = jnp.concatenate([query_bias_all, jnp.zeros_like(query_bias_all), value_bias_all])

    def everyone(own):
        return jnp.concatenate([received(own, "tp", by) for by in range(tp_size)])

    def returned(full, weight, dims):
        total = 0.0
        for by in range(1, tp_size):
            theirs = mm(full[by * own_count : (by + 1) * own_count], weight, dims).astype(bf16)
            total = total + received(theirs, "tp", -by).astype(f32)
        return total + mm(full[:own_count], weight, dims)

    kept = []
    layer_rows, stat_terms = None, None
    inputs = start_rows
    for tick in range(sections):
        residual = inputs.astype(f32) + time_rows * time_weight + time_bias
        if tick == 0 and in_kernels:
            rounded_all, qkv, mixed, lse = attended_first
        else:
            rounded_all = everyone(residual.astype(bf16))
            qkv = by_position((mm(rounded_all, joined) + joined_bias).astype(bf16))
            mixed, lse = attend(qkv, segment, span, kernel_order, kernel_rows)
        if tick == 1:
            mixed = after(mixed, *upstream_pieces)
        mixed = by_distance(mixed)
        branch = returned(mixed, out_all, ((1,), (0,))) + out_bias
        first_normed, first_inverse = norm_parts(residual + branch)
        first_out = first_normed * attn_gain + attn_shift
        first_all = everyone(first_out.astype(bf16))
        hidden, slope = widen(first_all, in_all, in_bias_all)
        ffn_branch = returned(hidden, ffn_out_all, ((1,), (0,))) + ffn_out_bias
        second_normed, second_inverse = norm_parts(first_out + ffn_branch)
        layer_y = (second_normed * ffn_gain + ffn_shift).astype(bf16)
        terms = jnp.stack(
            [jnp.sum(residual * residual), jnp.sum(branch * branch), jnp.sum(ffn_branch * ffn_branch)]
        )
        kept.append(
            (
                rounded_all,
                qkv,
                mixed,
                lse,
                first_normed,
                first_inverse,
                first_all,
                hidden,
                slope,
                second_normed,
                second_inverse,
            )
        )
        if tick == 0:
            layer_rows, stat_terms = layer_y, terms
            upstream_pieces = to_sequence(after(cotangent, layer_y))
        else:
            here = section_at == tick
            layer_rows = jnp.where(here, layer_y, layer_rows)
            stat_terms = jnp.where(here, terms, stat_terms)
        if tick + 1 < sections:
            inputs = passed_along(layer_y, "pipe", 1)
    layer_pieces = to_positions(layer_rows)


    def parts_of(left, right, side):
        found = []
        for other in range(dp_size):
            cut = slice(other * part, (other + 1) * part)
            if side == 0:
                found.append(mm(left[:, cut], right, ((0,), (0,))).astype(bf16))
            else:
                found.append(mm(left, right[:, cut], ((0,), (0,))).astype(bf16))
        return found

    def chosen(found_at, operands):
        if sections == 1:
            return found_at(*operands[0])
        return lax.switch(
            sections - 1 - section_at, [functools.partial(found_at, *each) for each in operands]
        )

    def owned(parts, axis, thirds):
        total = parts[0].astype(f32)
        for other in range(1, dp_size):
            total = total + received(parts[other], "dp", -other).astype(f32)
        each = total.shape[axis] // (seqs * thirds)
        blocks = [
            jnp.concatenate(
                [
                    lax.slice_in_dim(total, (third * seqs + k) * each, (third * seqs + k + 1) * each, axis=axis)
                    for third in range(thirds)
                ],
                axis=axis,
            )
            for k in range(seqs)
        ]
        mine = blocks[0]
        for by in range(1, seqs):
            mine = mine + received(blocks[by].astype(bf16), "zs", -by).astype(f32)
        return mine

    results = None
    upstream_rows = jnp.concatenate(upstream_pieces)
    for_ffn, for_out, for_joined = [], [], []
    for step in range(sections):
        (
            rounded_all,
            qkv,
            mixed,
            lse,
            first_normed,
            first_inverse,
            first_all,
            hidden,
            slope,
            second_normed,
            second_inverse,
        ) = kept[sections - 1 - step]
        last = step + 1 == sections
        upstream = upstream_rows.astype(f32)
        gain_two, shift_two = token_sum(upstream * second_normed), token_sum(upstream)
        grad_second = norm_back(upstream, second_normed, second_inverse, ffn_gain)
        grad_ffn = grad_second.astype(bf16)
        ffn_out_bias_grad = token_sum(grad_ffn)
        grad_ffn_all = everyone(grad_ffn)
        grad_pre = (mm(grad_ffn_all, ffn_out_all, ((1,), (1,))) * slope.astype(f32)).astype(bf16)
        in_bias_sum = token_sum(grad_pre)
        for_ffn.append((hidden, grad_ffn_all, first_all, grad_pre))
        if last and not in_kernels:
            ffn_out_parts = chosen(lambda a, b, c, d: parts_of(a, b, 1), for_ffn)
            ffn_in_parts = chosen(lambda a, b, c, d: parts_of(c, d, 0), for_ffn)
            grad_second = after(grad_second, *ffn_out_parts, *ffn_in_parts)
        grad_first = grad_second + returned(grad_pre, in_all, ((1,), (1,)))
        gain_one, shift_one = token_sum(grad_first * first_normed), token_sum(grad_first)
        grad_resid = norm_back(grad_first, first_normed, first_inverse, attn_gain)
        grad_branch = grad_resid.astype(bf16)
        out_bias_grad = token_sum(grad_branch)
        branch_all = everyone(grad_branch)
        grad_mixed = by_position(mm(branch_all, out_all, ((1,), (1,))).astype(bf16))
        for_out.append((mixed, branch_all))
        if last and not in_kernels:
            out_parts = chosen(lambda a, b: parts_of(a, b, 1), for_out)
            grad_mixed = after(grad_mixed, *out_parts)
        if last and in_kernels:
            attended = (qkv, grad_mixed, lse, segment[:, None], segment[None, :], joined, grad_resid, time_rows)
            tw_grad, tb_grad = jnp.zeros((width,), f32), jnp.zeros((width,), f32)
            bias_sums, grad_in_before = jnp.zeros((3 * heads_all,), f32), results[2]
            grad_in = jnp.zeros((), bf16)
            results = (results[0], results[1], grad_in)
        else:
            grads = attend_back(qkv, segment, span, kernel_order, kernel_rows, grad_mixed, lse)
            grad_qkv = jnp.concatenate([by_distance(grad) for grad in grads], axis=1)
            bias_sums = token_sum(grad_qkv)
            for_joined.append((rounded_all, grad_qkv))
            if last:
                joined_parts = chosen(lambda a, b: parts_of(a, b, 0), for_joined)
            grad_input = grad_resid + returned(grad_qkv, joined, ((1,), (1,)))
            tw_grad, tb_grad = token_sum(grad_input * time_rows), token_sum(grad_input)
            grad_in = grad_input.astype(bf16)
        slot_sums = jnp.concatenate(
            [
                bias_sums[:heads_all].reshape(seqs, head_cols),
                bias_sums[2 * heads_all :].reshape(seqs, head_cols),
                in_bias_sum.reshape(seqs, unit_cols),
            ],
            axis=1,
        )
        vector_sums = jnp.stack(
            [tw_grad, tb_grad, out_bias_grad, gain_one, shift_one, ffn_out_bias_grad, gain_two, shift_two]
        )
        these = (vector_sums, slot_sums, grad_in)
        if step == 0:
            results = these
        else:
            here = section_at == sections - 1 - step
            results = jax.tree.map(lambda a, b: jnp.where(here, a, b), these, results)
        if not last:
            upstream_rows = passed_along(grad_in, "pipe", -1)
    vector_sums, slot_sums, grad_in = results
    stat_row = jnp.concatenate([stat_terms, jnp.zeros((width - 3,), f32)])[None]
    shared = jnp.concatenate([straightened(vector_sums), stat_row])
    if in_kernels:
        small = jnp.concatenate([shared, jnp.zeros((7, width), f32)])
        padded = -(-slot_sums.shape[1] // 1024) * 1024
        slots = jnp.pad(slot_sums, ((0, 0), (0, padded - slot_sums.shape[1])))
        by_block = straightened(grad_in_before).reshape(seqs, rows, width)
        input_pieces, small, slots, *gradients = scatter_all(
            rows,
            by_block,
            small,
            slots.reshape(seqs, 8, padded // 8),
            [operand for each in zip(for_ffn, for_out) for pair in each for operand in pair],
            attended,
            (rounded_all, for_joined[0][0]),
            for_joined[0][1],
            tp_size,
        )
        input_grad = jnp.transpose(input_pieces, (1, 0, 2))
        shared, own_slot = small[:9], slots.reshape(1, padded)[:, : slot_sums.shape[1]]
        ffn_out_grad, ffn_in_grad, out_grad = gradients[:3]
        triple = gradients[3:]
    else:
        input_grad = in_positions(to_positions(grad_in))
        shared = summed_over(summed_over(summed_over(shared, "tp"), "zs"), "dp")
        own_slot = slot_sums[0:1]
        for by in range(1, seqs):
            own_slot = own_slot + received(slot_sums[by : by + 1], "zs", -by)
        own_slot = summed_over(own_slot, "dp")
        ffn_out_grad = owned(ffn_out_parts, 0, 1)
        ffn_in_grad = owned(ffn_in_parts, 1, 1)
        out_grad = owned(out_parts, 0, 1)
        joined_grad = owned(joined_parts, 1, 3)
        triple = [joined_grad[:, i * head_cols : (i + 1) * head_cols] for i in range(3)]
    layer_out = in_positions(layer_pieces, grad_mixed)
    element_count = float(SEQ_LEN * seqs * dp_size * width)
    stats = jnp.sqrt(shared[8:9, :3] / element_count)
    return (
        layer_out[None],
        input_grad[None],
        shared[0:1],
        shared[1:2],
        triple[0][None],
        own_slot[:, :head_cols],
        triple[1][None],
        triple[2][None],
        own_slot[:, head_cols : 2 * head_cols],
        out_grad[None],
        shared[2:3],
        shared[3:4],
        shared[4:5],
        ffn_in_grad[None],
        own_slot[:, 2 * head_cols :],
        ffn_out_grad[None],
        shared[5:6],
        shared[6:7],
        shared[7:8],
        stats,
    )


def solution(mesh):
    def run(states, *rest):
        sizes = mesh.shape
        seqs = states.shape[1] // sizes["dp"]
        grouped = Mesh(
            mesh.devices.reshape(sizes["pipe"], sizes["dp"], seqs, sizes["tensor"] // seqs),
            ("pipe", "dp", "zs", "tp"),
        )
        return jax.shard_map(
            per_device,
            mesh=grouped,
            in_specs=(
                P(TENSOR, "dp", None),
                P(TENSOR, "dp", None),
                P("dp", None),
                P("dp", None),
                P("pipe", None),
                P("pipe", None),
                P("pipe", None, TENSOR),
                P("pipe", TENSOR),
                P("pipe", None, TENSOR),
                P("pipe", None, TENSOR),
                P("pipe", TENSOR),
                P("pipe", TENSOR, None),
                P("pipe", None),
                P("pipe", None),
                P("pipe", None),
                P("pipe", None, TENSOR),
                P("pipe", TENSOR),
                P("pipe", TENSOR, None),
                P("pipe", None),
                P("pipe", None),
                P("pipe", None),
            ),
            out_specs=(
                P("pipe", TENSOR, "dp", None),
                P("pipe", TENSOR, "dp", None),
                P("pipe", None),
                P("pipe", None),
                P("pipe", "dp", TENSOR),
                P("pipe", TENSOR),
                P("pipe", "dp", TENSOR),
                P("pipe", "dp", TENSOR),
                P("pipe", TENSOR),
                P("pipe", TENSOR, "dp"),
                P("pipe", None),
                P("pipe", None),
                P("pipe", None),
                P("pipe", "dp", TENSOR),
                P("pipe", TENSOR),
                P("pipe", TENSOR, "dp"),
                P("pipe", None),
                P("pipe", None),
                P("pipe", None),
                P("pipe", None),
            ),
            check_vma=False,
        )(states, *rest)

    return run
```

```python
import functools
import math

import jax
import jax.numpy as jnp
from jax import lax
from jax.experimental import pallas as pl
from jax.experimental.pallas import tpu as pltpu
from jax.sharding import Mesh
from jax.sharding import PartitionSpec as P

HDIM = 64
SEQ_LEN = 1152
STEPS = 5000
ITEM_MOST = 525
PAIR = 2 * HDIM
TILE = 128
AHEAD = 2
WIDTHS = (2, 3, 4, 5, 6, 7, 9)
LOG2E = math.log2(math.e)
SCALE = 1.0 / math.sqrt(HDIM)
TENSOR = ("zs", "tp")

epsilon = 1e-05
f32 = jnp.float32
bf16 = jnp.bfloat16


def received(shard, axis, by):
    size = lax.axis_size(axis)
    by = by % size
    if by == 0:
        return shard
    return lax.ppermute(shard, axis, [((i + by) % size, i) for i in range(size)])


def passed_along(shard, axis, by):
    size = lax.axis_size(axis)
    pairs = [(i, i + by) for i in range(size) if 0 <= i + by < size]
    return lax.ppermute(shard, axis, pairs)


def summed_over(values, axis):
    total = values
    for by in range(1, lax.axis_size(axis)):
        total = total + received(values, axis, by)
    return total


def after(value, *others):
    return lax.optimization_barrier((value, *others))[0]


def norm_parts(summed):
    centered = summed - jnp.mean(summed, axis=-1, keepdims=True)
    inverse = lax.rsqrt(jnp.mean(centered * centered, axis=-1, keepdims=True) + epsilon)
    return (centered * inverse, inverse)


def norm_back(upstream, normed, inverse, gain):
    scaled = upstream * gain
    return inverse * (
        scaled
        - jnp.mean(scaled, axis=-1, keepdims=True)
        - normed * jnp.mean(scaled * normed, axis=-1, keepdims=True)
    )


def token_sum(values):
    return jnp.sum(values.astype(f32), axis=0)


def mm(a, b, dims=((1,), (0,))):
    return lax.dot_general(a, b, (dims, ((), ())), preferred_element_type=f32)


def key_spans(item_ends, length):
    tiles = length // TILE
    first = jnp.arange(tiles, dtype=jnp.int32)[:, None] * TILE
    ends = item_ends[None, :]
    start = jnp.max(jnp.where(ends <= first, ends, 0), axis=1) // TILE
    end = jnp.min(jnp.where(ends > first + TILE - 1, ends, length), axis=1)
    need = (end + TILE - 1) // TILE - start
    widths = jnp.array([min(w, tiles) for w in WIDTHS], jnp.int32)
    kind = jnp.sum((widths[None, :] < need[:, None]).astype(jnp.int32), axis=1)
    is_kind = jnp.arange(len(WIDTHS), dtype=jnp.int32)[None, :] == kind[:, None]
    width = jnp.sum(jnp.where(is_kind, widths[None, :], 0), axis=1)
    return jnp.stack([kind, jnp.minimum(start, tiles - width) * TILE]).astype(jnp.int32)


def place(order, source, target, rows, by_position):
    for block in range(source.shape[0] // rows):
        at = pl.ds(pl.multiple_of(order[block] * rows, 16), rows)
        if by_position:
            target[at, :] = source[block * rows : (block + 1) * rows, :]
        else:
            target[block * rows : (block + 1) * rows, :] = source[at, :]


def two_heads(pair):
    first = lax.broadcasted_iota(jnp.int32, pair.shape, 1) < HDIM
    zero = jnp.zeros_like(pair)
    return jnp.concatenate([jnp.where(first, pair, zero), jnp.where(first, zero, pair)], axis=0)


def one_pair(stacked):
    half = stacked.shape[0] // 2
    first = lax.broadcasted_iota(jnp.int32, (half, stacked.shape[1]), 1) < HDIM
    return jnp.where(first, stacked[:half], stacked[half:])


def each_tile(span, length, body):
    tiles = length // TILE

    def step(tile, carry):
        at = pl.ds(pl.multiple_of(tile * TILE, TILE), TILE)

        def branch(width):
            count = min(width, tiles) * TILE
            return lambda: body(at, pl.ds(pl.multiple_of(span[1, tile], TILE), count))

        lax.switch(span[0, tile], [branch(width) for width in WIDTHS])
        return carry

    lax.fori_loop(0, tiles, step, 0)


def forward_tile(at, to, seg_c, seg_r, lse_ref, q_s, k_s, v_s, mixed_s):
    same_item = seg_c[at, :] == seg_r[:, to]
    same_item = jnp.concatenate([same_item, same_item], axis=0)
    for pair in range(q_s.shape[1] // PAIR):
        cols = slice(pair * PAIR, (pair + 1) * PAIR)
        scores = mm(two_heads(q_s[at, cols]), k_s[to, cols], ((1,), (1,))) * (SCALE * LOG2E)
        scores = jnp.where(same_item, scores, -1e30)
        top = jnp.max(scores, axis=1, keepdims=True)
        weights = jnp.exp2(scores - top)
        total = jnp.sum(weights, axis=1, keepdims=True)
        mixed = mm(weights.astype(bf16), v_s[to, cols]) * (1.0 / total)
        mixed_s[at, cols] = one_pair(mixed).astype(bf16)
        sums = top + jnp.log2(total)
        spread = one_pair(jnp.broadcast_to(sums, (2 * TILE, PAIR))).T
        lse_ref[pair, 0:1, at] = spread[0:1]
        lse_ref[pair, 1:2, at] = spread[HDIM : HDIM + 1]


def banded(tiles, length, body):
    reach = ITEM_MOST - 1
    for tile in tiles:
        low = max(0, (tile * TILE - reach) // TILE)
        high = min(length, -(-((tile + 1) * TILE + reach) // TILE) * TILE)
        body(slice(tile * TILE, (tile + 1) * TILE), slice(low * TILE, high))


def attend_kernel(
    rows, order, span, seg_c, seg_r, q_ref, k_ref, v_ref, mixed_ref, lse_ref, q_s, k_s, v_s, mixed_s
):
    for source, target in ((q_ref, q_s), (k_ref, k_s), (v_ref, v_s)):
        place(order, source, target, rows, True)

    def body(at, to):
        forward_tile(at, to, seg_c, seg_r, lse_ref, q_s, k_s, v_s, mixed_s)

    each_tile(span, q_ref.shape[0], body)
    place(order, mixed_s, mixed_ref, rows, False)


def attend(qkv, segment, span, order, rows):
    length, width = qkv.shape[0], qkv.shape[1] // 3
    pairs = width // PAIR
    small = pl.BlockSpec(memory_space=pltpu.SMEM)
    third = lambda i: pl.BlockSpec((length, width), lambda h: (0, i))
    return pl.pallas_call(
        functools.partial(attend_kernel, rows),
        grid=(1,),
        in_specs=[
            small,
            small,
            pl.BlockSpec((length, 1), lambda h: (0, 0)),
            pl.BlockSpec((1, length), lambda h: (0, 0)),
            third(0),
            third(1),
            third(2),
        ],
        out_specs=[third(0), pl.BlockSpec((pairs, 2, length), lambda h: (0, 0, 0))],
        out_shape=[
            jax.ShapeDtypeStruct((length, width), bf16),
            jax.ShapeDtypeStruct((pairs, 2, length), f32),
        ],
        scratch_shapes=[pltpu.VMEM((length, width), bf16)] * 4,
        compiler_params=pltpu.CompilerParams(vmem_limit_bytes=48 * 1024 * 1024),
        cost_estimate=pl.CostEstimate(flops=0, bytes_accessed=0, transcendentals=0),
    )(order, span, segment[:, None], segment[None, :], qkv, qkv, qkv)


def back_tile(at, to, seg_c, seg_r, lse_ref, q_s, k_s, v_s, up_s, dq_s, dk_s, dv_s):
    same_item = seg_c[to, 0:1] == seg_r[:, at]
    same_item = jnp.concatenate([same_item, same_item], axis=1)
    for pair in range(q_s.shape[1] // PAIR):
        cols = slice(pair * PAIR, (pair + 1) * PAIR)
        keys_all = k_s[to, cols]
        queries, upstream = two_heads(q_s[at, cols]), two_heads(up_s[at, cols])
        lse = jnp.concatenate([lse_ref[pair, 0:1, at], lse_ref[pair, 1:2, at]], axis=1)
        scores = mm(keys_all, queries, ((1,), (1,))) * (SCALE * LOG2E)
        probs = jnp.where(same_item, jnp.exp2(scores - lse), 0.0)
        grad_probs = mm(v_s[to, cols], upstream, ((1,), (1,)))
        weighted = probs * grad_probs
        inner = jnp.sum(weighted, axis=0, keepdims=True)
        grad_scores = (weighted - probs * inner).astype(bf16)
        dv_s[to, cols] += mm(probs.astype(bf16), upstream)
        dk_s[to, cols] += mm(grad_scores, queries)
        dq_s[at, cols] = (one_pair(mm(grad_scores, keys_all, ((0,), (0,)))) * SCALE).astype(bf16)


def attend_back_kernel(
    rows, order, span, seg_c, seg_r, q_ref, k_ref, v_ref, up_ref, lse_ref, dq_ref, dk_ref, dv_ref,
    q_s, k_s, v_s, up_s, dq_s, dk_s, dv_s,
):
    for source, target in ((q_ref, q_s), (k_ref, k_s), (v_ref, v_s), (up_ref, up_s)):
        place(order, source, target, rows, True)
    dk_s[...] = jnp.zeros_like(dk_s)
    dv_s[...] = jnp.zeros_like(dv_s)

    def body(at, to):
        back_tile(at, to, seg_c, seg_r, lse_ref, q_s, k_s, v_s, up_s, dq_s, dk_s, dv_s)

    each_tile(span, q_ref.shape[0], body)
    q_s[...] = (dk_s[...] * SCALE).astype(bf16)
    v_s[...] = dv_s[...].astype(bf16)
    for source, target in ((dq_s, dq_ref), (q_s, dk_ref), (v_s, dv_ref)):
        place(order, source, target, rows, False)


def attend_back(qkv, segment, span, order, rows, grad_mixed, lse):
    length, width = grad_mixed.shape
    pairs = width // PAIR
    small = pl.BlockSpec(memory_space=pltpu.SMEM)
    third = lambda i: pl.BlockSpec((length, width), lambda h: (0, i))
    return pl.pallas_call(
        functools.partial(attend_back_kernel, rows),
        grid=(1,),
        in_specs=[
            small,
            small,
            pl.BlockSpec((length, 1), lambda h: (0, 0)),
            pl.BlockSpec((1, length), lambda h: (0, 0)),
            third(0),
            third(1),
            third(2),
            third(0),
            pl.BlockSpec((pairs, 2, length), lambda h: (0, 0, 0)),
        ],
        out_specs=[third(0)] * 3,
        out_shape=[jax.ShapeDtypeStruct((length, width), bf16)] * 3,
        scratch_shapes=[pltpu.VMEM((length, width), bf16)] * 5 + [pltpu.VMEM((length, width), f32)] * 2,
        compiler_params=pltpu.CompilerParams(vmem_limit_bytes=48 * 1024 * 1024),
        cost_estimate=pl.CostEstimate(flops=0, bytes_accessed=0, transcendentals=0),
    )(order, span, segment[:, None], segment[None, :], qkv, qkv, qkv, grad_mixed, lse)


def gelu_parts(pre):
    size = jnp.abs(pre)
    t = 1.0 / (1.0 + (0.3275911 * math.sqrt(0.5)) * size)
    bell = jnp.exp2((-0.5 * LOG2E) * (pre * pre))
    poly = t * (0.127414796 + t * (-0.142248368 + t * (0.7107068705 + t * (-0.7265760135 + t * 0.5307027145))))
    below = poly * bell
    below = jnp.where(pre >= 0, 1.0 - below, below)
    return pre * below, below + (pre * bell) * (1.0 / math.sqrt(2.0 * math.pi))


def widen_kernel(chunk, x_ref, w_ref, bias_ref, hidden_ref, slope_ref):
    for at in range(0, x_ref.shape[0], chunk):
        rows = slice(at, at + chunk)
        hidden, slope = gelu_parts(mm(x_ref[rows, :], w_ref[...]) + bias_ref[...])
        hidden_ref[rows, :] = hidden.astype(bf16)
        slope_ref[rows, :] = slope.astype(bf16)


def widen(x, weight, bias):
    count, width = x.shape
    units = weight.shape[1]
    step = 256
    return pl.pallas_call(
        functools.partial(widen_kernel, 144),
        grid=(units // step,),
        in_specs=[
            pl.BlockSpec((count, width), lambda i: (0, 0)),
            pl.BlockSpec((width, step), lambda i: (0, i)),
            pl.BlockSpec((1, step), lambda i: (0, i)),
        ],
        out_specs=[pl.BlockSpec((count, step), lambda i: (0, i))] * 2,
        out_shape=[jax.ShapeDtypeStruct((count, units), bf16)] * 2,
        compiler_params=pltpu.CompilerParams(vmem_limit_bytes=48 * 1024 * 1024),
        cost_estimate=pl.CostEstimate(flops=0, bytes_accessed=0, transcendentals=0),
    )(x, weight, bias[None])


def gather_kernel(seqs, dp_size, tp_size, *refs):
    seq_ref, bias_ref = refs[:2]
    blocks = refs[2:8]
    time_ref, time_weight, time_bias, seg_c, seg_r = refs[8:13]
    start_ref, biases_ref, joined_ref, out_ref, in_ref, ffn_out_ref = refs[13:19]
    tokens_ref, qkv_ref, mixed_ref, lse_ref = refs[19:23]
    local_sem, seq_send, seq_get, up_send, up_get, down_send, down_get, side_send, side_get = refs[23:32]
    start_s, joined_s, q_s, k_s, v_s, mixed_s, x_sem, load_sem = refs[32:]
    zs, dp, tp = lax.axis_index("zs"), lax.axis_index("dp"), lax.axis_index("tp")
    rows = seq_ref.shape[1]
    own_count = seqs * rows
    length, heads_all = mixed_ref.shape
    width, hc = blocks[0].shape
    units = blocks[4].shape[1]
    part = width // dp_size
    half = units // 2
    table = [(0, 0, hc), (1, 0, hc), (2, 0, hc), (3, 0, hc)]
    table += [(4, 0, half), (4, half, half), (5, 0, half), (5, half, half)]
    kinds = range(len(table))

    def home(kind, slot, other):
        array, first, size = table[kind]
        features = slice(other * part, (other + 1) * part)
        if array < 3:
            at = (array * seqs + slot) * hc
            return joined_ref.at[features, at : at + hc]
        if array == 3:
            return out_ref.at[slot * hc : (slot + 1) * hc, features]
        at = slice(slot * units + first, slot * units + first + size)
        return in_ref.at[features, at] if array == 4 else ffn_out_ref.at[at, features]

    def own(kind, other):
        array, first, size = table[kind]
        features = pl.ds(pl.multiple_of(lax.rem(dp + other, dp_size) * part, part), part)
        if array in (3, 5):
            return blocks[array].at[first : first + size, features]
        return blocks[array].at[features, first : first + size]

    def to(axis, at, source, target, send, get):
        return pltpu.make_async_remote_copy(
            src_ref=source,
            dst_ref=target,
            send_sem=send,
            recv_sem=get,
            device_id={axis: at},
            device_id_type=pl.DeviceIdType.MESH,
        )

    def sequence(by):
        at = lax.rem(zs - by + seqs, seqs)
        return to("zs", at, seq_ref.at[at], start_ref.at[by], seq_send.at[by], seq_get.at[by])

    def bias(by):
        at = lax.rem(zs - by + seqs, seqs)
        return to("zs", at, bias_ref, biases_ref.at[by], seq_send.at[seqs + by], seq_get.at[seqs + by])

    def up(kind, hop):
        source = own(kind, 0) if hop == 0 else home(kind, seqs - hop, 0)
        target = home(kind, seqs - hop - 1, 0)
        return to("zs", zs + 1, source, target, up_send.at[kind, hop], up_get.at[kind, hop])

    def down(kind, hop):
        source = own(kind, 0) if hop == 0 else home(kind, hop, 0)
        target = home(kind, hop + 1, 0)
        return to("zs", zs - 1, source, target, down_send.at[kind, hop], down_get.at[kind, hop])

    def side(kind, slot, other):
        at = lax.rem(dp - other + dp_size, dp_size)
        place = side_send.at[kind, slot, other], side_get.at[kind, slot, other]
        return to("dp", at, home(kind, slot, 0), home(kind, slot, other), *place)

    def local(kind, other):
        return pltpu.make_async_copy(own(kind, other), home(kind, 0, other), local_sem.at[kind, other])

    barrier = pltpu.get_barrier_semaphore()
    for axis, at, size in (("zs", zs, seqs), ("dp", dp, dp_size), ("tp", tp, tp_size)):
        for by in range(1, size):
            pl.semaphore_signal(
                barrier,
                inc=1,
                device_id={axis: lax.rem(at + by, size)},
                device_id_type=pl.DeviceIdType.MESH,
            )
    pl.semaphore_wait(barrier, seqs + dp_size + tp_size - 3)

    for by in range(1, seqs):
        sequence(by).start()
        bias(by).start()
    def begin(kind):
        @pl.when(zs < seqs - 1)
        def _():
            up(kind, 0).start()

        @pl.when(zs > 0)
        def _():
            down(kind, 0).start()

    for kind in kinds[:AHEAD]:
        begin(kind)

    own_seq = pltpu.make_async_copy(seq_ref.at[zs], start_ref.at[0], local_sem.at[len(table), 0])
    own_bias = pltpu.make_async_copy(bias_ref, biases_ref.at[0], local_sem.at[len(table), 1])
    own_seq.start()
    own_bias.start()
    for kind in kinds:
        for other in range(dp_size):
            local(kind, other).start()

    def pass_on(kind, hop):
        @pl.when(zs >= hop)
        def _():
            up(kind, hop - 1).wait_recv()
            if hop < seqs - 1:

                @pl.when(zs < seqs - 1)
                def _():
                    up(kind, hop).start()

            for other in range(1, dp_size):
                side(kind, seqs - hop, other).start()

        @pl.when(zs + hop < seqs)
        def _():
            down(kind, hop - 1).wait_recv()
            if hop < seqs - 1:

                @pl.when(zs > 0)
                def _():
                    down(kind, hop).start()

            for other in range(1, dp_size):
                side(kind, hop, other).start()

    def exchange():
        here, there = tokens_ref.at[:own_count, :], tokens_ref.at[own_count:, :]
        return to("tp", 1 - tp, here, there, x_sem.at[0], x_sem.at[1])

    def placed(block):
        member, chip = divmod(block, seqs)
        at = lax.rem(zs + chip, seqs) * tp_size + lax.rem(tp + member, tp_size)
        return pl.ds(pl.multiple_of(at * rows, 16), rows)

    load_start = pltpu.make_async_copy(start_ref, start_s, load_sem.at[0])
    load_joined = pltpu.make_async_copy(joined_ref, joined_s, load_sem.at[1])

    def tokens():
        own_seq.wait()
        for by in range(1, seqs):
            sequence(by).wait()
        load_start.start()
        load_start.wait()
        for block in range(seqs):
            at = slice(block * rows, (block + 1) * rows)
            residual = start_s[block].astype(f32) + time_ref[at, :] * time_weight[...] + time_bias[...]
            tokens_ref[at, :] = residual.astype(bf16)
        exchange().start()

    def joined_there():
        for kind in range(3):
            for other in range(dp_size):
                local(kind, other).wait()
            for slot in range(1, seqs):
                for other in range(1, dp_size):
                    side(kind, slot, other).wait()
        load_joined.start()
        own_bias.wait()
        for by in range(1, seqs):
            bias(by).wait()
        exchange().wait()
        load_joined.wait()

    def project(member):
        here = slice(member * own_count, (member + 1) * own_count)
        for third, target in enumerate((q_s, k_s, v_s)):
            cols = slice(third * heads_all, (third + 1) * heads_all)
            found = mm(tokens_ref[here, :], joined_s[:, cols])
            if third != 1:
                at = slice(third // 2 * hc, third // 2 * hc + hc)
                found = found + jnp.concatenate([biases_ref[slot, :, at] for slot in range(seqs)], axis=1)
            found = found.astype(bf16)
            qkv_ref[here, cols] = found
            for chip in range(seqs):
                target[placed(member * seqs + chip), :] = found[chip * rows : (chip + 1) * rows]

    def attention(tiles):
        def body(at, to):
            forward_tile(at, to, seg_c, seg_r, lse_ref, q_s, k_s, v_s, mixed_s)

        banded(tiles, length, body)

    def mixed_out():
        for block in range(seqs * tp_size):
            mixed_ref[block * rows : (block + 1) * rows, :] = mixed_s[placed(block), :]

    tiles = length // TILE
    for step in range(len(kinds) + seqs - 2):
        for hop in range(1, seqs):
            if 0 <= step - hop + 1 < len(kinds):
                pass_on(step - hop + 1, hop)
        if step + AHEAD < len(kinds):
            begin(step + AHEAD)
        if step == 2:
            tokens()
        if step == seqs:
            joined_there()
            for member in range(tp_size):
                project(member)
        if step == seqs + 1:
            attention(range(tiles // 3))
        if step == seqs + 2:
            attention(range(tiles // 3, 2 * tiles // 3))
        if step == seqs + 3:
            attention(range(2 * tiles // 3, tiles))
            mixed_out()

    for kind in kinds:
        if kind >= 3:
            for other in range(dp_size):
                local(kind, other).wait()
            for slot in range(1, seqs):
                for other in range(1, dp_size):
                    side(kind, slot, other).wait()
        for hop in range(seqs - 1):

            @pl.when((zs >= hop) & (zs < seqs - 1))
            def _():
                up(kind, hop).wait_send()

            @pl.when((zs + hop < seqs) & (zs > 0))
            def _():
                down(kind, hop).wait_send()


def gather_all(by_seq, biases, blocks, tokenwise, dp_size, tp_size):
    seqs, rows, width = by_seq.shape
    hc, units = blocks[0].shape[1], blocks[4].shape[1]
    length, heads_all = seqs * rows * tp_size, seqs * hc
    anywhere = pl.BlockSpec(memory_space=pl.ANY)
    inside = pl.BlockSpec(memory_space=pltpu.VMEM)
    low = lambda *shape: jax.ShapeDtypeStruct(shape, bf16)
    held = lambda *shape: pltpu.VMEM(shape, bf16)
    dma = pltpu.SemaphoreType.DMA
    kinds = 8
    return pl.pallas_call(
        functools.partial(gather_kernel, seqs, dp_size, tp_size),
        in_specs=[anywhere] * (2 + len(blocks)) + [inside] * 5,
        out_specs=[anywhere, inside] + [anywhere] * 4 + [inside] * 4,
        out_shape=[
            jax.ShapeDtypeStruct(by_seq.shape, bf16),
            jax.ShapeDtypeStruct((seqs,) + biases.shape, f32),
            low(width, 3 * heads_all),
            low(heads_all, width),
            low(width, seqs * units),
            low(seqs * units, width),
            low(length, width),
            low(length, 3 * heads_all),
            low(length, heads_all),
            jax.ShapeDtypeStruct((heads_all // PAIR, 2, length), f32),
        ],
        scratch_shapes=[
            dma((kinds + 1, max(dp_size, 2))),
            dma((2 * seqs,)),
            dma((2 * seqs,)),
            dma((kinds, seqs - 1)),
            dma((kinds, seqs - 1)),
            dma((kinds, seqs - 1)),
            dma((kinds, seqs - 1)),
            dma((kinds, seqs, dp_size)),
            dma((kinds, seqs, dp_size)),
            held(*by_seq.shape),
            held(width, 3 * heads_all),
            held(length, heads_all),
            held(length, heads_all),
            held(length, heads_all),
            held(length, heads_all),
            dma((2,)),
            dma((2,)),
        ],
        compiler_params=pltpu.CompilerParams(
            collective_id=0, has_side_effects=True, vmem_limit_bytes=56 * 1024 * 1024
        ),
    )(by_seq, biases, *blocks, *tokenwise)


def scatter_kernel(rows, seqs, dp_size, tp_size, *refs):
    seq_ref, small_ref, slots_ref = refs[:3]
    operands_before, operands_last = refs[3:9], refs[9:13]
    qkv_ref, lse_ref, column_ref, seg_r, joined_ref = refs[13:18]
    tokens_last, tokens_before, gq_before = refs[18:21]
    ffn_out_ref, slope_ref, in_ref, out_ref, second_ref, normed_ref, gain_ref = refs[21:28]
    seq_out, small_out, slots_out = refs[28:31]
    outs = refs[31:37]
    sides, ups, downs = refs[37:41], refs[41:45], refs[45:49]
    small_zs, small_all, slots_zs, slots_dp = refs[49:53]
    seq_send, seq_get, local_sem, small_send, small_get = refs[53:58]
    side_send, side_get, up_send, up_get, down_send, down_get = refs[58:64]
    wide_s, dq_s, dk_s, dv_s, gq_s, tokens_s = refs[64:70]
    x_send, x_get, seq_s, small_s, slots_s = refs[70:75]
    mine, theirs = refs[75:79], refs[79:83]
    place_sem, x_sem, load_sem, resid_ref, branch_s, more_sem = refs[83:89]
    joined_mine, joined_theirs = mine[3], theirs[3]
    heads_all = dq_s.shape[1]
    q_s, k_s, v_s, up_s = [wide_s.at[:, i * heads_all : (i + 1) * heads_all] for i in range(4)]
    first_stage = lax.axis_index("pipe") == 0
    zs, dp, tp = lax.axis_index("zs"), lax.axis_index("dp"), lax.axis_index("tp")
    units = mine[0].shape[0] // seqs
    hc = mine[2].shape[0] // seqs
    half = units // 2
    length = dq_s.shape[0]
    own_count, width = resid_ref.shape
    seg_c = column_ref
    part = width // dp_size
    kinds = [(0, 0, 0, half), (0, 0, half, half), (1, 1, 0, half), (1, 1, half, half), (2, 0, 0, hc)]
    kinds += [(3, 1, third * seqs * hc, hc) for third in range(3)]

    def cut(arrays, kind, slot):
        array, axis, first, size = kinds[kind]
        apart = units if array < 2 else hc
        at = slice(first + slot * apart, first + slot * apart + size)
        return arrays[array].at[at, :] if axis == 0 else arrays[array].at[:, at]

    def to(where, source, target, send, get):
        return pltpu.make_async_remote_copy(
            src_ref=source,
            dst_ref=target,
            send_sem=send,
            recv_sem=get,
            device_id=where,
            device_id_type=pl.DeviceIdType.MESH,
        )

    def sequence(by):
        at = lax.rem(zs + by, seqs)
        return to({"zs": at}, seq_s.at[by], seq_out.at[zs], seq_send.at[by], seq_get.at[by])

    def side(kind, slot):
        place = side_send.at[kind, slot], side_get.at[kind, slot]
        return to({"dp": 1 - dp}, cut(theirs, kind, slot), cut(sides, kind, slot), *place)

    def up(kind, far):
        place = up_send.at[kind, far], up_get.at[kind, far]
        return to({"zs": zs + 1}, cut(sides, kind, far), cut(ups, kind, far - 1), *place)

    def down(kind, far):
        place = down_send.at[kind, far], down_get.at[kind, far]
        return to({"zs": zs - 1}, cut(sides, kind, seqs - far), cut(downs, kind, far - 1), *place)

    def small(by):
        at = {"zs": lax.rem(zs + by, seqs)}
        return to(at, small_s, small_zs.at[by], small_send.at[0, by], small_get.at[0, by])

    def slots(by):
        at = {"zs": lax.rem(zs + by, seqs)}
        return to(at, slots_s.at[by], slots_zs.at[by], small_send.at[1, by], small_get.at[1, by])

    def small_across(by):
        at = lax.rem(dp * tp_size + tp + by, dp_size * tp_size)
        where = {"dp": lax.div(at, tp_size), "tp": lax.rem(at, tp_size)}
        return to(where, small_all.at[0], small_all.at[by], small_send.at[2, by], small_get.at[2, by])

    def slots_across():
        return to({"dp": 1 - dp}, slots_dp.at[0], slots_dp.at[1], small_send.at[3, 0], small_get.at[3, 0])

    def added(target, *others):
        rows = target.shape[0]
        step = 64

        def body(i, carry):
            at = pl.ds(pl.multiple_of(i * step, step), step)
            total = target[at, :].astype(f32)
            for other in others:
                total = total + other[at, :].astype(f32)
            target[at, :] = total.astype(target.dtype)
            return carry

        lax.fori_loop(0, rows // step, body, 0)

    barrier = pltpu.get_barrier_semaphore()
    greeted = [{"zs": lax.rem(zs + by, seqs)} for by in range(1, seqs)]
    for by in range(1, dp_size * tp_size):
        at = lax.rem(dp * tp_size + tp + by, dp_size * tp_size)
        greeted.append({"dp": lax.div(at, tp_size), "tp": lax.rem(at, tp_size)})
    for where in greeted:
        pl.semaphore_signal(barrier, inc=1, device_id=where, device_id_type=pl.DeviceIdType.MESH)
    pl.semaphore_wait(barrier, len(greeted))

    slot_order = list(range(1, seqs)) + [0]

    def begin(kind):
        for slot in slot_order:
            side(kind, slot).start()

    def placed(block, array):
        member, chip = divmod(block, seqs)
        at = lax.rem(zs + chip, seqs) * tp_size + lax.rem(tp + member, tp_size)
        at = pl.ds(pl.multiple_of(at * rows, 16), rows)
        here = slice(block * rows, (block + 1) * rows)
        source = qkv_ref.at[here, array * heads_all : (array + 1) * heads_all]
        target = (q_s, k_s, v_s)[array].at[at, :]
        return pltpu.make_async_copy(source, target, place_sem.at[array, block])

    def each_placed(act):
        for array in range(3):
            for block in range(length // rows):
                act(placed(block, array))

    own_tokens = pltpu.make_async_copy(tokens_last, tokens_s, local_sem.at[1])
    old_tokens = pltpu.make_async_copy(tokens_before, tokens_s, local_sem.at[1])
    old_grads = pltpu.make_async_copy(gq_before, gq_s, local_sem.at[2])
    old_seq = pltpu.make_async_copy(seq_ref, seq_s, local_sem.at[3])

    def attention(tiles):
        def body(at, to):
            back_tile(at, to, seg_c, seg_r, lse_ref, q_s, k_s, v_s, up_s, dq_s, dk_s, dv_s)

        banded(tiles, length, body)

    def attention_start():
        @pl.when(first_stage)
        def _():
            own_tokens.start()
            each_placed(lambda copy: copy.start())
            dk_s[...] = jnp.zeros_like(dk_s)
            dv_s[...] = jnp.zeros_like(dv_s)
            each_placed(lambda copy: copy.wait())
            attention(range(length // TILE // 2))

        @pl.when(jnp.logical_not(first_stage))
        def _():
            old_tokens.start()
            old_grads.start()
            old_seq.start()

    def attention_end():
        @pl.when(first_stage)
        def _():
            attention(range(length // TILE // 2, length // TILE))
            q_s[...] = (dk_s[...] * SCALE).astype(bf16)
            v_s[...] = dv_s[...].astype(bf16)
            for third, source in enumerate((dq_s, q_s, v_s)):
                cols = slice(third * heads_all, (third + 1) * heads_all)
                for block in range(length // rows):
                    member, chip = divmod(block, seqs)
                    at = lax.rem(zs + chip, seqs) * tp_size + lax.rem(tp + member, tp_size)
                    at = pl.ds(pl.multiple_of(at * rows, 16), rows)
                    gq_s[block * rows : (block + 1) * rows, cols] = source[at, :]
            own_tokens.wait()

        @pl.when(jnp.logical_not(first_stage))
        def _():
            old_tokens.wait()
            old_grads.wait()
            old_seq.wait()

    def joined_parts():
        step = 256
        for other in reversed(range(dp_size)):
            target = joined_mine if other == 0 else joined_theirs
            for third in range(3):
                cols = slice(third * heads_all, (third + 1) * heads_all)
                for at in range(0, part, step):
                    left = tokens_s[:, other * part + at : other * part + at + step]
                    target[at : at + step, cols] = mm(left, gq_s[:, cols], ((0,), (0,))).astype(bf16)

    def exchange(time):
        return to({"tp": 1 - tp}, x_send, x_get, x_sem.at[0, time], x_sem.at[1, time])

    def branch_exchange():
        here, there = branch_s.at[:own_count, :], branch_s.at[own_count:, :]
        return to({"tp": 1 - tp}, here, there, x_sem.at[0, 2], x_sem.at[1, 2])

    def fetched(*pairs):
        copies = [pltpu.make_async_copy(*pair, more_sem.at[i]) for i, pair in enumerate(pairs)]
        for copy in copies:
            copy.start()
        for copy in copies:
            copy.wait()

    def keep_sums(first, sums):
        for other in range(dp_size):
            cols = pl.ds(pl.multiple_of(lax.rem(dp + other, dp_size) * part, part), part)
            for i, values in enumerate(sums):
                small_s[first + i : first + i + 1, cols] = values[:, other * part : (other + 1) * part]

    members = [slice(member * own_count, (member + 1) * own_count) for member in range(tp_size)]

    def hidden_grads():
        for slot in range(seqs):
            at = slice(slot * units, (slot + 1) * units)
            fetched((ffn_out_ref.at[at, :], branch_s.at[:units, :]), (slope_ref.at[:, at], dq_s))
            total = jnp.zeros((1, units), f32)
            for here in members:
                found = mm(tokens_s[here, :], branch_s[:units, :], ((1,), (1,)))
                found = (found * dq_s[here, :].astype(f32)).astype(bf16)
                wide_s[here, at] = found
                total = total + jnp.sum(found.astype(f32), axis=0, keepdims=True)
            for i in range(units // 128):
                slots_s[slot, 2 + i : 3 + i, :] = total[:, i * 128 : (i + 1) * 128]

    def first_grads():
        half = seqs * units // 2
        low, high = mine[3].at[:, :half], theirs[3].at[:, :half]
        for other in range(dp_size):
            at = slice(other * part, (other + 1) * part)
            fetched((in_ref.at[at, :half], low), (in_ref.at[at, half:], high))

            def found(here):
                total = mm(wide_s[here, :half], low[...], ((1,), (1,)))
                return total + mm(wide_s[here, half:], high[...], ((1,), (1,)))

            x_send[:, at] = found(members[1]).astype(bf16)
            resid_ref[:, at] = found(members[0])
        exchange(0).start()

    def norm_grads():
        pairs = []
        for source, target in ((second_ref, dk_s), (normed_ref, dv_s)):
            for i, here in enumerate(members):
                pairs.append((source.at[:, i * heads_all : (i + 1) * heads_all], target.at[here, :]))
        fetched(*pairs)
        exchange(0).wait()

        def block(i, carry):
            at = pl.ds(pl.multiple_of(i * rows, 16), rows)
            late = pl.ds(pl.multiple_of(own_count + i * rows, 16), rows)
            grads = resid_ref[at, :] + x_get[at, :].astype(f32)
            grads = grads + jnp.concatenate([dk_s[at, :], dk_s[late, :]], axis=1)
            normed = jnp.concatenate([dv_s[at, :], dv_s[late, :]], axis=1)
            found = norm_back(grads, normed, column_ref[at, 2:3], gain_ref[...])
            lowered = found.astype(bf16)
            resid_ref[at, :] = found
            branch_s[at, :] = lowered
            terms = (lowered.astype(f32), grads * normed, grads)
            return tuple(c + jnp.sum(term, axis=0, keepdims=True) for c, term in zip(carry, terms))

        zero = jnp.zeros((1, width), f32)
        keep_sums(2, lax.fori_loop(0, seqs, block, (zero, zero, zero)))
        branch_exchange().start()
        fetched((operands_last[3], dq_s), (out_ref, x_send.at[:heads_all, :]))
        branch_exchange().wait()

    def mixed_grads():
        for member, here in enumerate(members):
            found = mm(branch_s[here, :], x_send[:heads_all, :], ((1,), (1,))).astype(bf16)
            for chip in range(seqs):
                at = lax.rem(zs + chip, seqs) * tp_size + lax.rem(tp + member, tp_size)
                at = pl.ds(pl.multiple_of(at * rows, 16), rows)
                up_s[at, :] = found[chip * rows : (chip + 1) * rows]

    def input_grads():
        @pl.when(first_stage)
        def _():
            def theirs_rows(i, carry):
                at = pl.multiple_of(i * rows, 16)
                x_send[pl.ds(at, rows), :] = mm(
                    gq_s[pl.ds(own_count + at, rows), :], joined_ref[...], ((1,), (1,))
                ).astype(bf16)
                return carry

            lax.fori_loop(0, seqs, theirs_rows, 0)
            exchange(1).start()
            for slot in range(seqs):
                cols = slice(slot * hc, (slot + 1) * hc)
                slots_s[slot, 0:1, :] = jnp.sum(gq_s[:, cols].astype(f32), axis=0, keepdims=True)
                cols = slice(2 * heads_all + slot * hc, 2 * heads_all + (slot + 1) * hc)
                slots_s[slot, 1:2, :] = jnp.sum(gq_s[:, cols].astype(f32), axis=0, keepdims=True)
            exchange(1).wait()

            def own_rows(i, carry):
                at = pl.ds(pl.multiple_of(i * rows, 16), rows)
                total = mm(gq_s[at, :], joined_ref[...], ((1,), (1,)))
                total = total + x_get[at, :].astype(f32) + resid_ref[at, :]
                lowered = total.astype(bf16)
                for other in range(dp_size):
                    cols = pl.ds(pl.multiple_of(lax.rem(dp + other, dp_size) * part, part), part)
                    seq_s[i, :, cols] = lowered[:, other * part : (other + 1) * part]
                timed = jnp.sum(total * column_ref[at, 1:2], axis=0, keepdims=True)
                plain = jnp.sum(total, axis=0, keepdims=True)
                return carry[0] + timed, carry[1] + plain

            zero = jnp.zeros((1, width), f32)
            timed, plain = lax.fori_loop(0, seqs, own_rows, (zero, zero))
            keep_sums(0, (timed, plain))

    own_seq = pltpu.make_async_copy(seq_s.at[0], seq_out.at[zs], local_sem.at[0])

    def send_small():
        for by in range(1, seqs):
            small(by).start()
            slots(by).start()
        for by in range(1, seqs):
            sequence(by).start()
        own_seq.start()

    def add_small():
        total, slot_total = small_s[...], slots_s[0]
        for by in range(1, seqs):
            small(by).wait()
            slots(by).wait()
            total = total + small_zs[by]
            slot_total = slot_total + slots_zs[by]
        small_all[0] = total
        slots_dp[0] = slot_total
        for by in range(1, dp_size * tp_size):
            small_across(by).start()
        slots_across().start()

    small_s[...] = small_ref[...]
    slots_s[...] = slots_ref[...]
    def taken(kind):
        for slot in slot_order:
            side(kind, slot).wait()
            added(cut(sides, kind, slot), cut(mine, kind, slot))

    def pass_on(kind, hop):
        @pl.when((zs == hop) & (zs < seqs - 1))
        def _():
            for far in range(seqs - 1 - hop, 0, -1):
                if hop > 0:
                    up(kind, far + 1).wait_recv()
                    added(cut(sides, kind, far), cut(ups, kind, far))
                up(kind, far).start()

        @pl.when((zs == seqs - 1 - hop) & (zs > 0))
        def _():
            for far in range(seqs - 1 - hop, 0, -1):
                if hop > 0:
                    down(kind, far + 1).wait_recv()
                    added(cut(sides, kind, seqs - far), cut(downs, kind, far))
                down(kind, far).start()

    def load(index, target):
        def copies(operands):
            return pltpu.make_async_copy(operands[index], target, load_sem.at[index])


        @pl.when(first_stage)
        def _():
            copies(operands_last).start()

        @pl.when(jnp.logical_not(first_stage))
        def _():
            copies(operands_before).start()

        return copies(operands_last)

    def product(kind, other):
        array, axis, first, size = kinds[kind]
        target = (mine if other == 0 else theirs)[array]
        features = slice(other * part, (other + 1) * part)
        for slot in range(seqs):
            apart = units if array < 2 else hc
            at = slice(first + slot * apart, first + slot * apart + size)
            if axis == 0:
                left = dq_s if array == 2 else wide_s
                right = branch_s if array == 2 else tokens_s
                target[at, :] = mm(left[:, at], right[:, features], ((0,), (0,))).astype(bf16)
            else:
                found = mm(tokens_s[:, features], wide_s[:, at], ((0,), (0,)))
                target[:, at] = found.astype(bf16)

    def old(index, target):
        return pltpu.make_async_copy(operands_before[index], target, load_sem.at[index])

    def relay(step):
        if step < len(kinds):
            taken(step)
        for hop in range(seqs - 1):
            if 0 <= step - hop < len(kinds):
                pass_on(step - hop, hop)

    hidden, grads = load(0, wide_s), load(1, tokens_s)
    hidden.wait()
    grads.wait()
    for kind in (0, 1):
        for other in reversed(range(dp_size)):
            product(kind, other)
            if other == 1:
                begin(kind)

    @pl.when(first_stage)
    def _():
        hidden_grads()

    @pl.when(jnp.logical_not(first_stage))
    def _():
        old(3, wide_s).start()
        old(3, wide_s).wait()

    load(2, tokens_s).wait()
    for kind in (2, 3):
        for other in reversed(range(dp_size)):
            product(kind, other)
        begin(kind)

    @pl.when(first_stage)
    def _():
        first_grads()

    relay(0)

    @pl.when(first_stage)
    def _():
        norm_grads()

    @pl.when(jnp.logical_not(first_stage))
    def _():
        old(4, dq_s).start()
        old(5, branch_s).start()
        old(4, dq_s).wait()
        old(5, branch_s).wait()

    for other in reversed(range(dp_size)):
        product(4, other)
    begin(4)

    @pl.when(first_stage)
    def _():
        mixed_grads()

    relay(1)
    attention_start()
    relay(2)
    attention_end()
    relay(3)
    joined_parts()
    for kind in range(5, len(kinds)):
        begin(kind)
    input_grads()
    send_small()
    for step in range(4, len(kinds) + seqs - 2):
        relay(step)
        if step == 6:
            add_small()

    total, slot_total = small_all[0], slots_dp[0]
    for by in range(1, dp_size * tp_size):
        small_across(by).wait()
        total = total + small_all[by]
    slots_across().wait()
    small_out[...] = total
    slots_out[...] = slot_total + slots_dp[1]

    for kind, (array, axis, first, size) in enumerate(kinds):
        out = outs[array] if array < 3 else outs[3 + first // (seqs * hc)]
        if array < 2:
            out = out.at[first : first + size, :] if axis == 0 else out.at[:, first : first + size]
        out[...] = cut(sides, kind, 0)[...].astype(f32)

        @pl.when(zs > 0)
        def _():
            up(kind, 1).wait_recv()
            added(out, cut(ups, kind, 0))

        @pl.when(zs < seqs - 1)
        def _():
            down(kind, 1).wait_recv()
            added(out, cut(downs, kind, 0))

        for far in range(1, seqs):

            @pl.when(zs + far < seqs)
            def _():
                up(kind, far).wait_send()

            @pl.when(zs >= far)
            def _():
                down(kind, far).wait_send()

    own_seq.wait()
    for by in range(1, seqs):
        sequence(by).wait()


def scatter_all(rows, by_block, small, slots, operands, attended, tokens, gq_before, onward, tp_size):
    seqs, _, width = by_block.shape
    dp_size = 2
    units, part = operands[0].shape[1] // seqs, width // dp_size
    length, heads_all = tokens[0].shape[0], gq_before.shape[1] // 3
    hc = heads_all // seqs
    own_count = length // tp_size
    anywhere = pl.BlockSpec(memory_space=pl.ANY)
    inside = pl.BlockSpec(memory_space=pltpu.VMEM)
    wide = lambda *shape: jax.ShapeDtypeStruct(shape, f32)
    low = lambda *shape: pltpu.VMEM(shape, bf16)
    dma = pltpu.SemaphoreType.DMA
    like = [low(seqs * units, part), low(part, seqs * units), low(heads_all, part), low(part, 3 * heads_all)]
    fewer = [low((seqs - 1) * units, part), low(part, (seqs - 1) * units), low((seqs - 1) * hc, part)]
    fewer.append(low(part, 3 * heads_all))
    kinds = 8
    return pl.pallas_call(
        functools.partial(scatter_kernel, rows, seqs, dp_size, tp_size),
        in_specs=[anywhere, inside, inside]
        + [anywhere] * 11
        + [inside] * 4
        + [anywhere] * 9
        + [inside],
        out_specs=[anywhere] + [inside] * 8,
        out_shape=[
            jax.ShapeDtypeStruct(by_block.shape, bf16),
            wide(*small.shape),
            wide(*slots.shape[1:]),
            wide(units, part),
            wide(part, units),
            wide(hc, part),
            wide(part, hc),
            wide(part, hc),
            wide(part, hc),
        ],
        scratch_shapes=like
        + fewer * 2
        + [
            pltpu.VMEM((seqs,) + small.shape, f32),
            pltpu.VMEM((dp_size * tp_size,) + small.shape, f32),
            pltpu.VMEM(slots.shape, f32),
            pltpu.VMEM((2,) + slots.shape[1:], f32),
            dma((seqs,)),
            dma((seqs,)),
            dma((4,)),
            dma((4, max(seqs, dp_size * tp_size))),
            dma((4, max(seqs, dp_size * tp_size))),
        ]
        + [dma((kinds, seqs))] * 6
        + [low(length, 4 * heads_all), low(length, heads_all)]
        + [pltpu.VMEM((length, heads_all), f32)] * 2
        + [
            low(length, 3 * heads_all),
            low(length, width),
            low(own_count, width),
            low(own_count, width),
            low(*by_block.shape),
            pltpu.VMEM(small.shape, f32),
            pltpu.VMEM(slots.shape, f32),
        ]
        + like * 2
        + [
            dma((3, length // rows)),
            dma((2, 3)),
            dma((6,)),
            pltpu.VMEM((own_count, width), f32),
            low(length, width),
            dma((4,)),
        ],
        compiler_params=pltpu.CompilerParams(
            collective_id=1, has_side_effects=True, vmem_limit_bytes=63 * 1024 * 1024
        ),
    )(by_block, small, slots, *operands, *attended, *tokens, gq_before, *onward)


def per_device(
    states,
    cotangent,
    lengths,
    timesteps,
    time_weight,
    time_bias,
    query_weight,
    query_bias,
    key_weight,
    value_weight,
    value_bias,
    out_weight,
    out_bias,
    attn_gain,
    attn_shift,
    ffn_in,
    ffn_in_bias,
    ffn_out,
    ffn_out_bias,
    ffn_gain,
    ffn_shift,
):
    rows, seqs, width = states.shape
    own_count = seqs * rows
    sections, section_at = lax.axis_size("pipe"), lax.axis_index("pipe")
    dp_size, dp_at = lax.axis_size("dp"), lax.axis_index("dp")
    zs_at = lax.axis_index("zs")
    tp_size, tp_at = lax.axis_size("tp"), lax.axis_index("tp")
    length = own_count * tp_size
    part = width // dp_size
    head_cols, unit_cols = query_weight.shape[2], ffn_in.shape[2]
    heads_all, units_all = head_cols * seqs, unit_cols * seqs

    def rotated(array, axis=-1):
        axis = axis % array.ndim
        twice = jnp.concatenate([array, array], axis=axis)
        return lax.dynamic_slice_in_dim(twice, dp_at * part, width, axis)

    def straightened(array):
        twice = jnp.concatenate([array, array], axis=-1)
        back = (dp_size - dp_at) % dp_size
        return lax.dynamic_slice_in_dim(twice, back * part, width, array.ndim - 1)

    vectors = rotated(
        jnp.concatenate(
            [time_weight, time_bias, out_bias, attn_gain, attn_shift, ffn_out_bias, ffn_gain, ffn_shift]
        )
    )
    time_weight, time_bias, out_bias, attn_gain = vectors[0], vectors[1], vectors[2], vectors[3]
    attn_shift, ffn_out_bias, ffn_gain, ffn_shift = vectors[4], vectors[5], vectors[6], vectors[7]


    def to_sequence(array):
        by_seq = rotated(jnp.transpose(array, (1, 0, 2)))
        got = []
        for by in range(seqs):
            block = lax.dynamic_index_in_dim(by_seq, (zs_at - by) % seqs, 0, keepdims=False)
            got.append(received(block, "zs", by))
        return got

    def to_positions(array):
        by_block = straightened(array).reshape(seqs, rows, width)
        return [received(by_block[(seqs - by) % seqs], "zs", by)[None] for by in range(seqs)]

    def in_positions(got, *before):
        got = [after(piece, *before)[0] for piece in got]
        by_seq = []
        for at in range(seqs):
            found = got[0]
            for by in range(1, seqs):
                found = jnp.where((zs_at + by) % seqs == at, got[by], found)
            by_seq.append(found)
        return jnp.stack(by_seq, axis=1)

    item_ends = jnp.cumsum(lax.dynamic_index_in_dim(lengths, zs_at, 0, keepdims=False))
    own_times = lax.dynamic_index_in_dim(timesteps, zs_at, 0, keepdims=False).astype(f32)
    member = (tp_at + jnp.arange(tp_size, dtype=jnp.int32)) % tp_size
    chips = (zs_at + jnp.arange(seqs, dtype=jnp.int32)) % seqs
    order = (chips[None, :] * tp_size + member[:, None]).reshape(seqs * tp_size).astype(jnp.int32)

    def segment_at(places):
        return jnp.sum((item_ends[None, :] <= places[:, None]).astype(jnp.int32), axis=1)

    segment = segment_at(jnp.arange(length, dtype=jnp.int32))
    span = key_spans(item_ends, length)
    own_places = order[:seqs, None] * rows + jnp.arange(rows, dtype=jnp.int32)[None, :]
    own_segment = segment_at(own_places.reshape(own_count))
    own_pick = own_segment[:, None] == jnp.arange(lengths.shape[1], dtype=jnp.int32)[None, :]
    time_rows = (jnp.sum(jnp.where(own_pick, own_times[None, :], 0.0), axis=1) / STEPS)[:, None]
    aligned = rows % 16 == 0
    kernel_rows = rows if aligned else length
    kernel_order = order if aligned else jnp.zeros((1,), jnp.int32)

    def by_position(array):
        if aligned:
            return array
        blocks = array.reshape(seqs * tp_size, rows, array.shape[1])
        return jnp.take(blocks, jnp.argsort(order), axis=0).reshape(array.shape)

    def by_distance(array):
        if aligned:
            return array
        blocks = array.reshape(seqs * tp_size, rows, array.shape[1])
        return jnp.take(blocks, order, axis=0).reshape(array.shape)


    def over_zs(block, axis, *before):
        mine = lax.dynamic_slice_in_dim(block, dp_at * part, part, axis)
        mine = after(mine, *before)
        return [received(mine, "zs", by) for by in range(1, seqs)]

    def over_dp(pieces):
        return [[received(piece, "dp", other) for other in range(dp_size)] for piece in pieces]

    def assembled(block, axis, pieces, thirds):
        across = 1 - axis
        each = block.shape[across] // thirds
        shape = [0, 0]
        shape[axis], shape[across] = width, block.shape[across] * seqs
        whole = jnp.zeros(shape, block.dtype)

        def put(whole, piece, slot, at):
            for third in range(thirds):
                start = [0, 0]
                start[axis], start[across] = at, (third * seqs + slot) * each
                cut = lax.slice_in_dim(piece, third * each, (third + 1) * each, axis=across)
                whole = lax.dynamic_update_slice(whole, cut, start)
            return whole

        whole = put(whole, rotated(block, axis), 0, 0)
        for slot, row in enumerate(pieces):
            for other, piece in enumerate(row):
                whole = put(whole, piece, slot + 1, other * part)
        return whole

    biases = jnp.concatenate([query_bias[0], value_bias[0], ffn_in_bias[0].astype(f32)])[None]
    in_kernels = sections == 2 and dp_size == 2 and tp_size == 2 and rows % 16 == 0
    in_kernels = in_kernels and head_cols == 128 and part % 256 == 0 and unit_cols % 256 == 0
    in_kernels = in_kernels and heads_all == unit_cols == part
    if in_kernels:
        by_seq = rotated(jnp.transpose(states, (1, 0, 2)))
        blocks = (query_weight, key_weight, value_weight, out_weight, ffn_in, ffn_out)
        tokenwise = (time_rows, time_weight[None], time_bias[None], segment[:, None], segment[None, :])
        start, bias_slots, joined, out_all, in_all, ffn_out_all, *attended_first = gather_all(
            by_seq, biases, [block[0] for block in blocks], tokenwise, dp_size, tp_size
        )
        start_rows = start.reshape(own_count, width)
        bias_slots = bias_slots[:, 0]
    else:
        joined_block = jnp.concatenate([query_weight[0], key_weight[0], value_weight[0]], axis=1)
        start_pieces = to_sequence(states)
        start_rows = jnp.concatenate(start_pieces)
        bias_slots = [received(biases, "zs", by)[0] for by in range(seqs)]
        joined_zs = over_zs(joined_block, 0)
        out_zs = over_zs(out_weight[0], 1, *joined_zs, *start_pieces)
        in_zs = over_zs(ffn_in[0], 0, *out_zs)
        ffn_out_zs = over_zs(ffn_out[0], 1, *in_zs)
        joined = assembled(joined_block, 0, over_dp(joined_zs), 3)
        out_all = assembled(out_weight[0], 1, over_dp(out_zs), 1)
        in_all = assembled(ffn_in[0], 0, over_dp(in_zs), 1)
        ffn_out_all = assembled(ffn_out[0], 1, over_dp(ffn_out_zs), 1)
    query_bias_all = jnp.concatenate([b[:head_cols] for b in bias_slots])
    value_bias_all = jnp.concatenate([b[head_cols : 2 * head_cols] for b in bias_slots])
    in_bias_all = jnp.concatenate([b[2 * head_cols :] for b in bias_slots])
    joined_bias = jnp.concatenate([query_bias_all, jnp.zeros_like(query_bias_all), value_bias_all])

    def everyone(own):
        return jnp.concatenate([received(own, "tp", by) for by in range(tp_size)])

    def returned(full, weight, dims):
        total = 0.0
        for by in range(1, tp_size):
            theirs = mm(full[by * own_count : (by + 1) * own_count], weight, dims).astype(bf16)
            total = total + received(theirs, "tp", -by).astype(f32)
        return total + mm(full[:own_count], weight, dims)

    kept = []
    layer_rows, stat_terms = None, None
    inputs = start_rows
    for tick in range(sections):
        residual = inputs.astype(f32) + time_rows * time_weight + time_bias
        if tick == 0 and in_kernels:
            rounded_all, qkv, mixed, lse = attended_first
        else:
            rounded_all = everyone(residual.astype(bf16))
            qkv = by_position((mm(rounded_all, joined) + joined_bias).astype(bf16))
            mixed, lse = attend(qkv, segment, span, kernel_order, kernel_rows)
        if tick == 1:
            mixed = after(mixed, *upstream_pieces)
        mixed = by_distance(mixed)
        branch = returned(mixed, out_all, ((1,), (0,))) + out_bias
        first_normed, first_inverse = norm_parts(residual + branch)
        first_out = first_normed * attn_gain + attn_shift
        first_all = everyone(first_out.astype(bf16))
        hidden, slope = widen(first_all, in_all, in_bias_all)
        ffn_branch = returned(hidden, ffn_out_all, ((1,), (0,))) + ffn_out_bias
        second_normed, second_inverse = norm_parts(first_out + ffn_branch)
        layer_y = (second_normed * ffn_gain + ffn_shift).astype(bf16)
        terms = jnp.stack(
            [jnp.sum(residual * residual), jnp.sum(branch * branch), jnp.sum(ffn_branch * ffn_branch)]
        )
        kept.append(
            (
                rounded_all,
                qkv,
                mixed,
                lse,
                first_normed,
                first_inverse,
                first_all,
                hidden,
                slope,
                second_normed,
                second_inverse,
            )
        )
        if tick == 0:
            layer_rows, stat_terms = layer_y, terms
            upstream_pieces = to_sequence(after(cotangent, layer_y))
        else:
            here = section_at == tick
            layer_rows = jnp.where(here, layer_y, layer_rows)
            stat_terms = jnp.where(here, terms, stat_terms)
        if tick + 1 < sections:
            inputs = passed_along(layer_y, "pipe", 1)
    layer_pieces = to_positions(layer_rows)


    def parts_of(left, right, side):
        found = []
        for other in range(dp_size):
            cut = slice(other * part, (other + 1) * part)
            if side == 0:
                found.append(mm(left[:, cut], right, ((0,), (0,))).astype(bf16))
            else:
                found.append(mm(left, right[:, cut], ((0,), (0,))).astype(bf16))
        return found

    def chosen(found_at, operands):
        if sections == 1:
            return found_at(*operands[0])
        return lax.switch(
            sections - 1 - section_at, [functools.partial(found_at, *each) for each in operands]
        )

    def owned(parts, axis, thirds):
        total = parts[0].astype(f32)
        for other in range(1, dp_size):
            total = total + received(parts[other], "dp", -other).astype(f32)
        each = total.shape[axis] // (seqs * thirds)
        blocks = [
            jnp.concatenate(
                [
                    lax.slice_in_dim(total, (third * seqs + k) * each, (third * seqs + k + 1) * each, axis=axis)
                    for third in range(thirds)
                ],
                axis=axis,
            )
            for k in range(seqs)
        ]
        mine = blocks[0]
        for by in range(1, seqs):
            mine = mine + received(blocks[by].astype(bf16), "zs", -by).astype(f32)
        return mine

    results = None
    upstream_rows = jnp.concatenate(upstream_pieces)
    for_ffn, for_out, for_joined = [], [], []
    for step in range(sections):
        (
            rounded_all,
            qkv,
            mixed,
            lse,
            first_normed,
            first_inverse,
            first_all,
            hidden,
            slope,
            second_normed,
            second_inverse,
        ) = kept[sections - 1 - step]
        last = step + 1 == sections
        upstream = upstream_rows.astype(f32)
        gain_two, shift_two = token_sum(upstream * second_normed), token_sum(upstream)
        grad_second = norm_back(upstream, second_normed, second_inverse, ffn_gain)
        grad_ffn = grad_second.astype(bf16)
        ffn_out_bias_grad = token_sum(grad_ffn)
        grad_ffn_all = everyone(grad_ffn)
        if last and in_kernels:
            by_token = jnp.concatenate([time_rows, first_inverse], axis=1)
            by_token = jnp.pad(by_token, ((0, length - own_count), (0, 0)))
            columns = jnp.concatenate([segment.astype(f32)[:, None], by_token], axis=1)
            attended = (qkv, lse, columns, segment.astype(f32)[None, :], joined)
            onward = (
                ffn_out_all,
                slope,
                in_all,
                out_all,
                grad_second,
                first_normed,
                attn_gain[None],
            )
            (before,), (before_out,) = for_ffn, for_out
            operands = (*before, *before_out, hidden, grad_ffn_all, first_all, mixed)
            nothing = jnp.zeros((width,), f32)
            tw_grad, tb_grad, out_bias_grad, gain_one, shift_one = [nothing] * 5
            in_bias_sum, bias_sums = jnp.zeros((units_all,), f32), jnp.zeros((3 * heads_all,), f32)
            grad_in_before, grad_in = results[2], jnp.zeros((), bf16)
            results = (results[0], results[1], grad_in)
        else:
            grad_pre = (mm(grad_ffn_all, ffn_out_all, ((1,), (1,))) * slope.astype(f32)).astype(bf16)
            in_bias_sum = token_sum(grad_pre)
            for_ffn.append((hidden, grad_ffn_all, first_all, grad_pre))
            if last:
                ffn_out_parts = chosen(lambda a, b, c, d: parts_of(a, b, 1), for_ffn)
                ffn_in_parts = chosen(lambda a, b, c, d: parts_of(c, d, 0), for_ffn)
                grad_second = after(grad_second, *ffn_out_parts, *ffn_in_parts)
            grad_first = grad_second + returned(grad_pre, in_all, ((1,), (1,)))
            gain_one, shift_one = token_sum(grad_first * first_normed), token_sum(grad_first)
            grad_resid = norm_back(grad_first, first_normed, first_inverse, attn_gain)
            grad_branch = grad_resid.astype(bf16)
            out_bias_grad = token_sum(grad_branch)
            branch_all = everyone(grad_branch)
            grad_mixed = by_position(mm(branch_all, out_all, ((1,), (1,))).astype(bf16))
            for_out.append((mixed, branch_all))
            if last:
                out_parts = chosen(lambda a, b: parts_of(a, b, 1), for_out)
                grad_mixed = after(grad_mixed, *out_parts)
            grads = attend_back(qkv, segment, span, kernel_order, kernel_rows, grad_mixed, lse)
            grad_qkv = jnp.concatenate([by_distance(grad) for grad in grads], axis=1)
            bias_sums = token_sum(grad_qkv)
            for_joined.append((rounded_all, grad_qkv))
            if last:
                joined_parts = chosen(lambda a, b: parts_of(a, b, 0), for_joined)
            grad_input = grad_resid + returned(grad_qkv, joined, ((1,), (1,)))
            tw_grad, tb_grad = token_sum(grad_input * time_rows), token_sum(grad_input)
            grad_in = grad_input.astype(bf16)
        slot_sums = jnp.concatenate(
            [
                bias_sums[:heads_all].reshape(seqs, head_cols),
                bias_sums[2 * heads_all :].reshape(seqs, head_cols),
                in_bias_sum.reshape(seqs, unit_cols),
            ],
            axis=1,
        )
        vector_sums = jnp.stack(
            [tw_grad, tb_grad, out_bias_grad, gain_one, shift_one, ffn_out_bias_grad, gain_two, shift_two]
        )
        these = (vector_sums, slot_sums, grad_in)
        if step == 0:
            results = these
        else:
            here = section_at == sections - 1 - step
            results = jax.tree.map(lambda a, b: jnp.where(here, a, b), these, results)
        if not last:
            upstream_rows = passed_along(grad_in, "pipe", -1)
    vector_sums, slot_sums, grad_in = results
    stat_row = jnp.concatenate([stat_terms, jnp.zeros((width - 3,), f32)])[None]
    shared = jnp.concatenate([straightened(vector_sums), stat_row])
    if in_kernels:
        small = jnp.concatenate([shared, jnp.zeros((7, width), f32)])
        padded = -(-slot_sums.shape[1] // 1024) * 1024
        slots = jnp.pad(slot_sums, ((0, 0), (0, padded - slot_sums.shape[1])))
        by_block = straightened(grad_in_before).reshape(seqs, rows, width)
        input_pieces, small, slots, *gradients = scatter_all(
            rows,
            by_block,
            small,
            slots.reshape(seqs, 8, padded // 8),
            operands,
            attended,
            (rounded_all, for_joined[0][0]),
            for_joined[0][1],
            onward,
            tp_size,
        )
        input_grad = jnp.transpose(input_pieces, (1, 0, 2))
        shared, own_slot = small[:9], slots.reshape(1, padded)[:, : slot_sums.shape[1]]
        ffn_out_grad, ffn_in_grad, out_grad = gradients[:3]
        triple = gradients[3:]
    else:
        input_grad = in_positions(to_positions(grad_in))
        shared = summed_over(summed_over(summed_over(shared, "tp"), "zs"), "dp")
        own_slot = slot_sums[0:1]
        for by in range(1, seqs):
            own_slot = own_slot + received(slot_sums[by : by + 1], "zs", -by)
        own_slot = summed_over(own_slot, "dp")
        ffn_out_grad = owned(ffn_out_parts, 0, 1)
        ffn_in_grad = owned(ffn_in_parts, 1, 1)
        out_grad = owned(out_parts, 0, 1)
        joined_grad = owned(joined_parts, 1, 3)
        triple = [joined_grad[:, i * head_cols : (i + 1) * head_cols] for i in range(3)]
    layer_out = in_positions(layer_pieces, grad_ffn_all)
    element_count = float(SEQ_LEN * seqs * dp_size * width)
    stats = jnp.sqrt(shared[8:9, :3] / element_count)
    return (
        layer_out[None],
        input_grad[None],
        shared[0:1],
        shared[1:2],
        triple[0][None],
        own_slot[:, :head_cols],
        triple[1][None],
        triple[2][None],
        own_slot[:, head_cols : 2 * head_cols],
        out_grad[None],
        shared[2:3],
        shared[3:4],
        shared[4:5],
        ffn_in_grad[None],
        own_slot[:, 2 * head_cols :],
        ffn_out_grad[None],
        shared[5:6],
        shared[6:7],
        shared[7:8],
        stats,
    )


def solution(mesh):
    def run(states, *rest):
        sizes = mesh.shape
        seqs = states.shape[1] // sizes["dp"]
        grouped = Mesh(
            mesh.devices.reshape(sizes["pipe"], sizes["dp"], seqs, sizes["tensor"] // seqs),
            ("pipe", "dp", "zs", "tp"),
        )
        return jax.shard_map(
            per_device,
            mesh=grouped,
            in_specs=(
                P(TENSOR, "dp", None),
                P(TENSOR, "dp", None),
                P("dp", None),
                P("dp", None),
                P("pipe", None),
                P("pipe", None),
                P("pipe", None, TENSOR),
                P("pipe", TENSOR),
                P("pipe", None, TENSOR),
                P("pipe", None, TENSOR),
                P("pipe", TENSOR),
                P("pipe", TENSOR, None),
                P("pipe", None),
                P("pipe", None),
                P("pipe", None),
                P("pipe", None, TENSOR),
                P("pipe", TENSOR),
                P("pipe", TENSOR, None),
                P("pipe", None),
                P("pipe", None),
                P("pipe", None),
            ),
            out_specs=(
                P("pipe", TENSOR, "dp", None),
                P("pipe", TENSOR, "dp", None),
                P("pipe", None),
                P("pipe", None),
                P("pipe", "dp", TENSOR),
                P("pipe", TENSOR),
                P("pipe", "dp", TENSOR),
                P("pipe", "dp", TENSOR),
                P("pipe", TENSOR),
                P("pipe", TENSOR, "dp"),
                P("pipe", None),
                P("pipe", None),
                P("pipe", None),
                P("pipe", "dp", TENSOR),
                P("pipe", TENSOR),
                P("pipe", TENSOR, "dp"),
                P("pipe", None),
                P("pipe", None),
                P("pipe", None),
                P("pipe", None),
            ),
            check_vma=False,
        )(states, *rest)

    return run
```

```python
import functools
import math

import jax
import jax.numpy as jnp
from jax import lax
from jax.experimental import pallas as pl
from jax.experimental.pallas import tpu as pltpu
from jax.sharding import Mesh
from jax.sharding import PartitionSpec as P

HDIM = 64
SEQ_LEN = 1152
STEPS = 5000
ITEM_MOST = 525
PAIR = 2 * HDIM
TILE = 128
AHEAD = 2
WIDTHS = (2, 3, 4, 5, 6, 7, 9)
LOG2E = math.log2(math.e)
SCALE = 1.0 / math.sqrt(HDIM)
TENSOR = ("zs", "tp")

epsilon = 1e-05
f32 = jnp.float32
bf16 = jnp.bfloat16


def received(shard, axis, by):
    size = lax.axis_size(axis)
    by = by % size
    if by == 0:
        return shard
    return lax.ppermute(shard, axis, [((i + by) % size, i) for i in range(size)])


def passed_along(shard, axis, by):
    size = lax.axis_size(axis)
    pairs = [(i, i + by) for i in range(size) if 0 <= i + by < size]
    return lax.ppermute(shard, axis, pairs)


def summed_over(values, axis):
    total = values
    for by in range(1, lax.axis_size(axis)):
        total = total + received(values, axis, by)
    return total


def after(value, *others):
    return lax.optimization_barrier((value, *others))[0]


def norm_parts(summed):
    centered = summed - jnp.mean(summed, axis=-1, keepdims=True)
    inverse = lax.rsqrt(jnp.mean(centered * centered, axis=-1, keepdims=True) + epsilon)
    return (centered * inverse, inverse)


def norm_back(upstream, normed, inverse, gain):
    scaled = upstream * gain
    return inverse * (
        scaled
        - jnp.mean(scaled, axis=-1, keepdims=True)
        - normed * jnp.mean(scaled * normed, axis=-1, keepdims=True)
    )


def token_sum(values):
    return jnp.sum(values.astype(f32), axis=0)


def mm(a, b, dims=((1,), (0,))):
    return lax.dot_general(a, b, (dims, ((), ())), preferred_element_type=f32)


def key_spans(item_ends, length):
    tiles = length // TILE
    first = jnp.arange(tiles, dtype=jnp.int32)[:, None] * TILE
    ends = item_ends[None, :]
    start = jnp.max(jnp.where(ends <= first, ends, 0), axis=1) // TILE
    end = jnp.min(jnp.where(ends > first + TILE - 1, ends, length), axis=1)
    need = (end + TILE - 1) // TILE - start
    widths = jnp.array([min(w, tiles) for w in WIDTHS], jnp.int32)
    kind = jnp.sum((widths[None, :] < need[:, None]).astype(jnp.int32), axis=1)
    is_kind = jnp.arange(len(WIDTHS), dtype=jnp.int32)[None, :] == kind[:, None]
    width = jnp.sum(jnp.where(is_kind, widths[None, :], 0), axis=1)
    return jnp.stack([kind, jnp.minimum(start, tiles - width) * TILE]).astype(jnp.int32)


def place(order, source, target, rows, by_position):
    for block in range(source.shape[0] // rows):
        at = pl.ds(pl.multiple_of(order[block] * rows, 16), rows)
        if by_position:
            target[at, :] = source[block * rows : (block + 1) * rows, :]
        else:
            target[block * rows : (block + 1) * rows, :] = source[at, :]


def two_heads(pair):
    first = lax.broadcasted_iota(jnp.int32, pair.shape, 1) < HDIM
    zero = jnp.zeros_like(pair)
    return jnp.concatenate([jnp.where(first, pair, zero), jnp.where(first, zero, pair)], axis=0)


def one_pair(stacked):
    half = stacked.shape[0] // 2
    first = lax.broadcasted_iota(jnp.int32, (half, stacked.shape[1]), 1) < HDIM
    return jnp.where(first, stacked[:half], stacked[half:])


def each_tile(span, length, body):
    tiles = length // TILE

    def step(tile, carry):
        at = pl.ds(pl.multiple_of(tile * TILE, TILE), TILE)

        def branch(width):
            count = min(width, tiles) * TILE
            return lambda: body(at, pl.ds(pl.multiple_of(span[1, tile], TILE), count))

        lax.switch(span[0, tile], [branch(width) for width in WIDTHS])
        return carry

    lax.fori_loop(0, tiles, step, 0)


def forward_tile(at, to, seg_c, seg_r, lse_ref, q_s, k_s, v_s, mixed_s):
    same_item = seg_c[at, :] == seg_r[:, to]
    same_item = jnp.concatenate([same_item, same_item], axis=0)
    for pair in range(q_s.shape[1] // PAIR):
        cols = slice(pair * PAIR, (pair + 1) * PAIR)
        scores = mm(two_heads(q_s[at, cols]), k_s[to, cols], ((1,), (1,))) * (SCALE * LOG2E)
        scores = jnp.where(same_item, scores, -1e30)
        top = jnp.max(scores, axis=1, keepdims=True)
        weights = jnp.exp2(scores - top)
        total = jnp.sum(weights, axis=1, keepdims=True)
        mixed = mm(weights.astype(bf16), v_s[to, cols]) * (1.0 / total)
        mixed_s[at, cols] = one_pair(mixed).astype(bf16)
        sums = top + jnp.log2(total)
        spread = one_pair(jnp.broadcast_to(sums, (2 * TILE, PAIR))).T
        lse_ref[pair, 0:1, at] = spread[0:1]
        lse_ref[pair, 1:2, at] = spread[HDIM : HDIM + 1]


def banded(tiles, length, body):
    reach = ITEM_MOST - 1
    for tile in tiles:
        low = max(0, (tile * TILE - reach) // TILE)
        high = min(length, -(-((tile + 1) * TILE + reach) // TILE) * TILE)
        body(slice(tile * TILE, (tile + 1) * TILE), slice(low * TILE, high))


def attend_kernel(
    rows, order, span, seg_c, seg_r, q_ref, k_ref, v_ref, mixed_ref, lse_ref, q_s, k_s, v_s, mixed_s
):
    for source, target in ((q_ref, q_s), (k_ref, k_s), (v_ref, v_s)):
        place(order, source, target, rows, True)

    def body(at, to):
        forward_tile(at, to, seg_c, seg_r, lse_ref, q_s, k_s, v_s, mixed_s)

    each_tile(span, q_ref.shape[0], body)
    place(order, mixed_s, mixed_ref, rows, False)


def attend(qkv, segment, span, order, rows):
    length, width = qkv.shape[0], qkv.shape[1] // 3
    pairs = width // PAIR
    small = pl.BlockSpec(memory_space=pltpu.SMEM)
    third = lambda i: pl.BlockSpec((length, width), lambda h: (0, i))
    return pl.pallas_call(
        functools.partial(attend_kernel, rows),
        grid=(1,),
        in_specs=[
            small,
            small,
            pl.BlockSpec((length, 1), lambda h: (0, 0)),
            pl.BlockSpec((1, length), lambda h: (0, 0)),
            third(0),
            third(1),
            third(2),
        ],
        out_specs=[third(0), pl.BlockSpec((pairs, 2, length), lambda h: (0, 0, 0))],
        out_shape=[
            jax.ShapeDtypeStruct((length, width), bf16),
            jax.ShapeDtypeStruct((pairs, 2, length), f32),
        ],
        scratch_shapes=[pltpu.VMEM((length, width), bf16)] * 4,
        compiler_params=pltpu.CompilerParams(vmem_limit_bytes=48 * 1024 * 1024),
        cost_estimate=pl.CostEstimate(flops=0, bytes_accessed=0, transcendentals=0),
    )(order, span, segment[:, None], segment[None, :], qkv, qkv, qkv)


def back_tile(at, to, seg_c, seg_r, lse_ref, q_s, k_s, v_s, up_s, dq_s, dk_s, dv_s):
    same_item = seg_c[to, 0:1] == seg_r[:, at]
    same_item = jnp.concatenate([same_item, same_item], axis=1)
    for pair in range(q_s.shape[1] // PAIR):
        cols = slice(pair * PAIR, (pair + 1) * PAIR)
        keys_all = k_s[to, cols]
        queries, upstream = two_heads(q_s[at, cols]), two_heads(up_s[at, cols])
        lse = jnp.concatenate([lse_ref[pair, 0:1, at], lse_ref[pair, 1:2, at]], axis=1)
        scores = mm(keys_all, queries, ((1,), (1,))) * (SCALE * LOG2E)
        probs = jnp.where(same_item, jnp.exp2(scores - lse), 0.0)
        grad_probs = mm(v_s[to, cols], upstream, ((1,), (1,)))
        weighted = probs * grad_probs
        inner = jnp.sum(weighted, axis=0, keepdims=True)
        grad_scores = (weighted - probs * inner).astype(bf16)
        dv_s[to, cols] += mm(probs.astype(bf16), upstream)
        dk_s[to, cols] += mm(grad_scores, queries)
        dq_s[at, cols] = (one_pair(mm(grad_scores, keys_all, ((0,), (0,)))) * SCALE).astype(bf16)


def attend_back_kernel(
    rows, order, span, seg_c, seg_r, q_ref, k_ref, v_ref, up_ref, lse_ref, dq_ref, dk_ref, dv_ref,
    q_s, k_s, v_s, up_s, dq_s, dk_s, dv_s,
):
    for source, target in ((q_ref, q_s), (k_ref, k_s), (v_ref, v_s), (up_ref, up_s)):
        place(order, source, target, rows, True)
    dk_s[...] = jnp.zeros_like(dk_s)
    dv_s[...] = jnp.zeros_like(dv_s)

    def body(at, to):
        back_tile(at, to, seg_c, seg_r, lse_ref, q_s, k_s, v_s, up_s, dq_s, dk_s, dv_s)

    each_tile(span, q_ref.shape[0], body)
    q_s[...] = (dk_s[...] * SCALE).astype(bf16)
    v_s[...] = dv_s[...].astype(bf16)
    for source, target in ((dq_s, dq_ref), (q_s, dk_ref), (v_s, dv_ref)):
        place(order, source, target, rows, False)


def attend_back(qkv, segment, span, order, rows, grad_mixed, lse):
    length, width = grad_mixed.shape
    pairs = width // PAIR
    small = pl.BlockSpec(memory_space=pltpu.SMEM)
    third = lambda i: pl.BlockSpec((length, width), lambda h: (0, i))
    return pl.pallas_call(
        functools.partial(attend_back_kernel, rows),
        grid=(1,),
        in_specs=[
            small,
            small,
            pl.BlockSpec((length, 1), lambda h: (0, 0)),
            pl.BlockSpec((1, length), lambda h: (0, 0)),
            third(0),
            third(1),
            third(2),
            third(0),
            pl.BlockSpec((pairs, 2, length), lambda h: (0, 0, 0)),
        ],
        out_specs=[third(0)] * 3,
        out_shape=[jax.ShapeDtypeStruct((length, width), bf16)] * 3,
        scratch_shapes=[pltpu.VMEM((length, width), bf16)] * 5 + [pltpu.VMEM((length, width), f32)] * 2,
        compiler_params=pltpu.CompilerParams(vmem_limit_bytes=48 * 1024 * 1024),
        cost_estimate=pl.CostEstimate(flops=0, bytes_accessed=0, transcendentals=0),
    )(order, span, segment[:, None], segment[None, :], qkv, qkv, qkv, grad_mixed, lse)


def gelu_parts(pre):
    size = jnp.abs(pre)
    t = 1.0 / (1.0 + (0.3275911 * math.sqrt(0.5)) * size)
    bell = jnp.exp2((-0.5 * LOG2E) * (pre * pre))
    poly = t * (0.127414796 + t * (-0.142248368 + t * (0.7107068705 + t * (-0.7265760135 + t * 0.5307027145))))
    below = poly * bell
    below = jnp.where(pre >= 0, 1.0 - below, below)
    return pre * below, below + (pre * bell) * (1.0 / math.sqrt(2.0 * math.pi))


def widen_kernel(chunk, x_ref, w_ref, bias_ref, hidden_ref, slope_ref):
    for at in range(0, x_ref.shape[0], chunk):
        rows = slice(at, at + chunk)
        hidden, slope = gelu_parts(mm(x_ref[rows, :], w_ref[...]) + bias_ref[...])
        hidden_ref[rows, :] = hidden.astype(bf16)
        slope_ref[rows, :] = slope.astype(bf16)


def widen(x, weight, bias):
    count, width = x.shape
    units = weight.shape[1]
    step = 256
    return pl.pallas_call(
        functools.partial(widen_kernel, 144),
        grid=(units // step,),
        in_specs=[
            pl.BlockSpec((count, width), lambda i: (0, 0)),
            pl.BlockSpec((width, step), lambda i: (0, i)),
            pl.BlockSpec((1, step), lambda i: (0, i)),
        ],
        out_specs=[pl.BlockSpec((count, step), lambda i: (0, i))] * 2,
        out_shape=[jax.ShapeDtypeStruct((count, units), bf16)] * 2,
        compiler_params=pltpu.CompilerParams(vmem_limit_bytes=48 * 1024 * 1024),
        cost_estimate=pl.CostEstimate(flops=0, bytes_accessed=0, transcendentals=0),
    )(x, weight, bias[None])


def gather_kernel(seqs, dp_size, tp_size, *refs):
    seq_ref, bias_ref = refs[:2]
    blocks = refs[2:8]
    time_ref, time_weight, time_bias, seg_c, seg_r = refs[8:13]
    start_ref, biases_ref, joined_ref, out_ref, in_ref, ffn_out_ref = refs[13:19]
    tokens_ref, qkv_ref, mixed_ref, lse_ref = refs[19:23]
    local_sem, seq_send, seq_get, up_send, up_get, down_send, down_get, side_send, side_get = refs[23:32]
    start_s, joined_s, q_s, k_s, v_s, mixed_s, x_sem, load_sem = refs[32:]
    zs, dp, tp = lax.axis_index("zs"), lax.axis_index("dp"), lax.axis_index("tp")
    rows = seq_ref.shape[1]
    own_count = seqs * rows
    length, heads_all = mixed_ref.shape
    width, hc = blocks[0].shape
    units = blocks[4].shape[1]
    part = width // dp_size
    half = units // 2
    table = [(0, 0, hc), (1, 0, hc), (2, 0, hc), (3, 0, hc)]
    table += [(4, 0, half), (4, half, half), (5, 0, half), (5, half, half)]
    kinds = range(len(table))

    def home(kind, slot, other):
        array, first, size = table[kind]
        features = slice(other * part, (other + 1) * part)
        if array < 3:
            at = (array * seqs + slot) * hc
            return joined_ref.at[features, at : at + hc]
        if array == 3:
            return out_ref.at[slot * hc : (slot + 1) * hc, features]
        at = slice(slot * units + first, slot * units + first + size)
        return in_ref.at[features, at] if array == 4 else ffn_out_ref.at[at, features]

    def own(kind, other):
        array, first, size = table[kind]
        features = pl.ds(pl.multiple_of(lax.rem(dp + other, dp_size) * part, part), part)
        if array in (3, 5):
            return blocks[array].at[first : first + size, features]
        return blocks[array].at[features, first : first + size]

    def to(axis, at, source, target, send, get):
        return pltpu.make_async_remote_copy(
            src_ref=source,
            dst_ref=target,
            send_sem=send,
            recv_sem=get,
            device_id={axis: at},
            device_id_type=pl.DeviceIdType.MESH,
        )

    def sequence(by):
        at = lax.rem(zs - by + seqs, seqs)
        return to("zs", at, seq_ref.at[at], start_ref.at[by], seq_send.at[by], seq_get.at[by])

    def bias(by):
        at = lax.rem(zs - by + seqs, seqs)
        return to("zs", at, bias_ref, biases_ref.at[by], seq_send.at[seqs + by], seq_get.at[seqs + by])

    def up(kind, hop):
        source = own(kind, 0) if hop == 0 else home(kind, seqs - hop, 0)
        target = home(kind, seqs - hop - 1, 0)
        return to("zs", zs + 1, source, target, up_send.at[kind, hop], up_get.at[kind, hop])

    def down(kind, hop):
        source = own(kind, 0) if hop == 0 else home(kind, hop, 0)
        target = home(kind, hop + 1, 0)
        return to("zs", zs - 1, source, target, down_send.at[kind, hop], down_get.at[kind, hop])

    def side(kind, slot, other):
        at = lax.rem(dp - other + dp_size, dp_size)
        place = side_send.at[kind, slot, other], side_get.at[kind, slot, other]
        return to("dp", at, home(kind, slot, 0), home(kind, slot, other), *place)

    def local(kind, other):
        return pltpu.make_async_copy(own(kind, other), home(kind, 0, other), local_sem.at[kind, other])

    barrier = pltpu.get_barrier_semaphore()
    for axis, at, size in (("zs", zs, seqs), ("dp", dp, dp_size), ("tp", tp, tp_size)):
        for by in range(1, size):
            pl.semaphore_signal(
                barrier,
                inc=1,
                device_id={axis: lax.rem(at + by, size)},
                device_id_type=pl.DeviceIdType.MESH,
            )
    pl.semaphore_wait(barrier, seqs + dp_size + tp_size - 3)

    for by in range(1, seqs):
        sequence(by).start()
        bias(by).start()
    def begin(kind):
        @pl.when(zs < seqs - 1)
        def _():
            up(kind, 0).start()

        @pl.when(zs > 0)
        def _():
            down(kind, 0).start()

    for kind in kinds[:AHEAD]:
        begin(kind)

    own_seq = pltpu.make_async_copy(seq_ref.at[zs], start_ref.at[0], local_sem.at[len(table), 0])
    own_bias = pltpu.make_async_copy(bias_ref, biases_ref.at[0], local_sem.at[len(table), 1])
    own_seq.start()
    own_bias.start()
    for kind in kinds:
        for other in range(dp_size):
            local(kind, other).start()

    def pass_on(kind, hop):
        @pl.when(zs >= hop)
        def _():
            up(kind, hop - 1).wait_recv()
            if hop < seqs - 1:

                @pl.when(zs < seqs - 1)
                def _():
                    up(kind, hop).start()

            for other in range(1, dp_size):
                side(kind, seqs - hop, other).start()

        @pl.when(zs + hop < seqs)
        def _():
            down(kind, hop - 1).wait_recv()
            if hop < seqs - 1:

                @pl.when(zs > 0)
                def _():
                    down(kind, hop).start()

            for other in range(1, dp_size):
                side(kind, hop, other).start()

    def exchange():
        here, there = tokens_ref.at[:own_count, :], tokens_ref.at[own_count:, :]
        return to("tp", 1 - tp, here, there, x_sem.at[0], x_sem.at[1])

    def placed(block):
        member, chip = divmod(block, seqs)
        at = lax.rem(zs + chip, seqs) * tp_size + lax.rem(tp + member, tp_size)
        return pl.ds(pl.multiple_of(at * rows, 16), rows)

    load_start = pltpu.make_async_copy(start_ref, start_s, load_sem.at[0])
    load_joined = pltpu.make_async_copy(joined_ref, joined_s, load_sem.at[1])

    def tokens():
        own_seq.wait()
        for by in range(1, seqs):
            sequence(by).wait()
        load_start.start()
        load_start.wait()
        for block in range(seqs):
            at = slice(block * rows, (block + 1) * rows)
            residual = start_s[block].astype(f32) + time_ref[at, :] * time_weight[...] + time_bias[...]
            tokens_ref[at, :] = residual.astype(bf16)
        exchange().start()

    def joined_there():
        for kind in range(3):
            for other in range(dp_size):
                local(kind, other).wait()
            for slot in range(1, seqs):
                for other in range(1, dp_size):
                    side(kind, slot, other).wait()
        load_joined.start()
        own_bias.wait()
        for by in range(1, seqs):
            bias(by).wait()
        exchange().wait()
        load_joined.wait()

    def project(member):
        here = slice(member * own_count, (member + 1) * own_count)
        for third, target in enumerate((q_s, k_s, v_s)):
            cols = slice(third * heads_all, (third + 1) * heads_all)
            found = mm(tokens_ref[here, :], joined_s[:, cols])
            if third != 1:
                at = slice(third // 2 * hc, third // 2 * hc + hc)
                found = found + jnp.concatenate([biases_ref[slot, :, at] for slot in range(seqs)], axis=1)
            found = found.astype(bf16)
            qkv_ref[here, cols] = found
            for chip in range(seqs):
                target[placed(member * seqs + chip), :] = found[chip * rows : (chip + 1) * rows]

    def attention(tiles):
        def body(at, to):
            forward_tile(at, to, seg_c, seg_r, lse_ref, q_s, k_s, v_s, mixed_s)

        banded(tiles, length, body)

    def mixed_out():
        for block in range(seqs * tp_size):
            mixed_ref[block * rows : (block + 1) * rows, :] = mixed_s[placed(block), :]

    tiles = length // TILE
    for step in range(len(kinds) + seqs - 2):
        for hop in range(1, seqs):
            if 0 <= step - hop + 1 < len(kinds):
                pass_on(step - hop + 1, hop)
        if step + AHEAD < len(kinds):
            begin(step + AHEAD)
        if step == 2:
            tokens()
        if step == seqs:
            joined_there()
            for member in range(tp_size):
                project(member)
        if step == seqs + 1:
            attention(range(tiles // 3))
        if step == seqs + 2:
            attention(range(tiles // 3, 2 * tiles // 3))
        if step == seqs + 3:
            attention(range(2 * tiles // 3, tiles))
            mixed_out()

    for kind in kinds:
        if kind >= 3:
            for other in range(dp_size):
                local(kind, other).wait()
            for slot in range(1, seqs):
                for other in range(1, dp_size):
                    side(kind, slot, other).wait()
        for hop in range(seqs - 1):

            @pl.when((zs >= hop) & (zs < seqs - 1))
            def _():
                up(kind, hop).wait_send()

            @pl.when((zs + hop < seqs) & (zs > 0))
            def _():
                down(kind, hop).wait_send()


def gather_all(by_seq, biases, blocks, tokenwise, dp_size, tp_size):
    seqs, rows, width = by_seq.shape
    hc, units = blocks[0].shape[1], blocks[4].shape[1]
    length, heads_all = seqs * rows * tp_size, seqs * hc
    anywhere = pl.BlockSpec(memory_space=pl.ANY)
    inside = pl.BlockSpec(memory_space=pltpu.VMEM)
    low = lambda *shape: jax.ShapeDtypeStruct(shape, bf16)
    held = lambda *shape: pltpu.VMEM(shape, bf16)
    dma = pltpu.SemaphoreType.DMA
    kinds = 8
    return pl.pallas_call(
        functools.partial(gather_kernel, seqs, dp_size, tp_size),
        in_specs=[anywhere] * (2 + len(blocks)) + [inside] * 5,
        out_specs=[anywhere, inside] + [anywhere] * 4 + [inside] * 4,
        out_shape=[
            jax.ShapeDtypeStruct(by_seq.shape, bf16),
            jax.ShapeDtypeStruct((seqs,) + biases.shape, f32),
            low(width, 3 * heads_all),
            low(heads_all, width),
            low(width, seqs * units),
            low(seqs * units, width),
            low(length, width),
            low(length, 3 * heads_all),
            low(length, heads_all),
            jax.ShapeDtypeStruct((heads_all // PAIR, 2, length), f32),
        ],
        scratch_shapes=[
            dma((kinds + 1, max(dp_size, 2))),
            dma((2 * seqs,)),
            dma((2 * seqs,)),
            dma((kinds, seqs - 1)),
            dma((kinds, seqs - 1)),
            dma((kinds, seqs - 1)),
            dma((kinds, seqs - 1)),
            dma((kinds, seqs, dp_size)),
            dma((kinds, seqs, dp_size)),
            held(*by_seq.shape),
            held(width, 3 * heads_all),
            held(length, heads_all),
            held(length, heads_all),
            held(length, heads_all),
            held(length, heads_all),
            dma((2,)),
            dma((2,)),
        ],
        compiler_params=pltpu.CompilerParams(
            collective_id=0, has_side_effects=True, vmem_limit_bytes=56 * 1024 * 1024
        ),
    )(by_seq, biases, *blocks, *tokenwise)


def scatter_kernel(rows, seqs, dp_size, tp_size, *refs):
    seq_ref, small_ref, slots_ref = refs[:3]
    operands_before, operands_last = refs[3:9], refs[9:13]
    qkv_ref, lse_ref, column_ref, seg_r, joined_ref = refs[13:18]
    tokens_last, tokens_before, gq_before = refs[18:21]
    ffn_out_ref, slope_ref, in_ref, out_ref, second_ref, normed_ref, gain_ref = refs[21:28]
    seq_out, small_out, slots_out = refs[28:31]
    outs = refs[31:37]
    sides, ups, downs = refs[37:41], refs[41:45], refs[45:49]
    small_zs, small_all, slots_zs, slots_dp = refs[49:53]
    seq_send, seq_get, local_sem, small_send, small_get = refs[53:58]
    side_send, side_get, up_send, up_get, down_send, down_get = refs[58:64]
    wide_s, dq_s, dk_s, dv_s, gq_s, tokens_s = refs[64:70]
    x_send, x_get, seq_s, small_s, slots_s = refs[70:75]
    mine, theirs = refs[75:79], refs[79:83]
    place_sem, x_sem, load_sem, resid_ref, branch_s, more_sem = refs[83:89]
    joined_mine, joined_theirs = mine[3], theirs[3]
    heads_all = dq_s.shape[1]
    q_s, k_s, v_s, up_s = [wide_s.at[:, i * heads_all : (i + 1) * heads_all] for i in range(4)]
    first_stage = lax.axis_index("pipe") == 0
    zs, dp, tp = lax.axis_index("zs"), lax.axis_index("dp"), lax.axis_index("tp")
    units = mine[0].shape[0] // seqs
    hc = mine[2].shape[0] // seqs
    half = units // 2
    length = dq_s.shape[0]
    own_count, width = resid_ref.shape
    seg_c = column_ref
    part = width // dp_size
    kinds = [(0, 0, 0, half), (0, 0, half, half), (1, 1, 0, half), (1, 1, half, half), (2, 0, 0, hc)]
    kinds += [(3, 1, third * seqs * hc, hc) for third in range(3)]

    def cut(arrays, kind, slot):
        array, axis, first, size = kinds[kind]
        apart = units if array < 2 else hc
        at = slice(first + slot * apart, first + slot * apart + size)
        return arrays[array].at[at, :] if axis == 0 else arrays[array].at[:, at]

    def to(where, source, target, send, get):
        return pltpu.make_async_remote_copy(
            src_ref=source,
            dst_ref=target,
            send_sem=send,
            recv_sem=get,
            device_id=where,
            device_id_type=pl.DeviceIdType.MESH,
        )

    def sequence(by):
        at = lax.rem(zs + by, seqs)
        return to({"zs": at}, seq_s.at[by], seq_out.at[zs], seq_send.at[by], seq_get.at[by])

    def side(kind, slot):
        place = side_send.at[kind, slot], side_get.at[kind, slot]
        return to({"dp": 1 - dp}, cut(theirs, kind, slot), cut(sides, kind, slot), *place)

    def up(kind, far):
        place = up_send.at[kind, far], up_get.at[kind, far]
        return to({"zs": zs + 1}, cut(sides, kind, far), cut(ups, kind, far - 1), *place)

    def down(kind, far):
        place = down_send.at[kind, far], down_get.at[kind, far]
        return to({"zs": zs - 1}, cut(sides, kind, seqs - far), cut(downs, kind, far - 1), *place)

    def small(by):
        at = {"zs": lax.rem(zs + by, seqs)}
        return to(at, small_s, small_zs.at[by], small_send.at[0, by], small_get.at[0, by])

    def slots(by):
        at = {"zs": lax.rem(zs + by, seqs)}
        return to(at, slots_s.at[by], slots_zs.at[by], small_send.at[1, by], small_get.at[1, by])

    def small_across(by):
        at = lax.rem(dp * tp_size + tp + by, dp_size * tp_size)
        where = {"dp": lax.div(at, tp_size), "tp": lax.rem(at, tp_size)}
        return to(where, small_all.at[0], small_all.at[by], small_send.at[2, by], small_get.at[2, by])

    def slots_across():
        return to({"dp": 1 - dp}, slots_dp.at[0], slots_dp.at[1], small_send.at[3, 0], small_get.at[3, 0])

    def added(target, *others):
        rows = target.shape[0]
        step = 64

        def body(i, carry):
            at = pl.ds(pl.multiple_of(i * step, step), step)
            total = target[at, :].astype(f32)
            for other in others:
                total = total + other[at, :].astype(f32)
            target[at, :] = total.astype(target.dtype)
            return carry

        lax.fori_loop(0, rows // step, body, 0)

    barrier = pltpu.get_barrier_semaphore()
    greeted = [{"zs": lax.rem(zs + by, seqs)} for by in range(1, seqs)]
    for by in range(1, dp_size * tp_size):
        at = lax.rem(dp * tp_size + tp + by, dp_size * tp_size)
        greeted.append({"dp": lax.div(at, tp_size), "tp": lax.rem(at, tp_size)})
    for where in greeted:
        pl.semaphore_signal(barrier, inc=1, device_id=where, device_id_type=pl.DeviceIdType.MESH)
    pl.semaphore_wait(barrier, len(greeted))

    slot_order = list(range(1, seqs)) + [0]

    def begin(kind):
        for slot in slot_order:
            side(kind, slot).start()

    def placed(block, array):
        member, chip = divmod(block, seqs)
        at = lax.rem(zs + chip, seqs) * tp_size + lax.rem(tp + member, tp_size)
        at = pl.ds(pl.multiple_of(at * rows, 16), rows)
        here = slice(block * rows, (block + 1) * rows)
        source = qkv_ref.at[here, array * heads_all : (array + 1) * heads_all]
        target = (q_s, k_s, v_s)[array].at[at, :]
        return pltpu.make_async_copy(source, target, place_sem.at[array, block])

    def each_placed(act):
        for array in range(3):
            for block in range(length // rows):
                act(placed(block, array))

    own_tokens = pltpu.make_async_copy(tokens_last, tokens_s, local_sem.at[1])
    old_tokens = pltpu.make_async_copy(tokens_before, tokens_s, local_sem.at[1])
    old_grads = pltpu.make_async_copy(gq_before, gq_s, local_sem.at[2])
    old_seq = pltpu.make_async_copy(seq_ref, seq_s, local_sem.at[3])

    def attention(tiles):
        def body(at, to):
            back_tile(at, to, seg_c, seg_r, lse_ref, q_s, k_s, v_s, up_s, dq_s, dk_s, dv_s)

        banded(tiles, length, body)

    def attention_start():
        @pl.when(first_stage)
        def _():
            own_tokens.start()
            each_placed(lambda copy: copy.start())
            dk_s[...] = jnp.zeros_like(dk_s)
            dv_s[...] = jnp.zeros_like(dv_s)
            each_placed(lambda copy: copy.wait())
            attention(range(length // TILE // 2))

        @pl.when(jnp.logical_not(first_stage))
        def _():
            old_tokens.start()
            old_grads.start()
            old_seq.start()

    def attention_end():
        @pl.when(first_stage)
        def _():
            attention(range(length // TILE // 2, length // TILE))
            q_s[...] = (dk_s[...] * SCALE).astype(bf16)
            v_s[...] = dv_s[...].astype(bf16)
            for third, source in enumerate((dq_s, q_s, v_s)):
                cols = slice(third * heads_all, (third + 1) * heads_all)
                for block in range(length // rows):
                    member, chip = divmod(block, seqs)
                    at = lax.rem(zs + chip, seqs) * tp_size + lax.rem(tp + member, tp_size)
                    at = pl.ds(pl.multiple_of(at * rows, 16), rows)
                    gq_s[block * rows : (block + 1) * rows, cols] = source[at, :]
            own_tokens.wait()

        @pl.when(jnp.logical_not(first_stage))
        def _():
            old_tokens.wait()
            old_grads.wait()
            old_seq.wait()

    def joined_parts():
        step = 256
        for other in reversed(range(dp_size)):
            target = joined_mine if other == 0 else joined_theirs
            for third in range(3):
                cols = slice(third * heads_all, (third + 1) * heads_all)
                for at in range(0, part, step):
                    left = tokens_s[:, other * part + at : other * part + at + step]
                    target[at : at + step, cols] = mm(left, gq_s[:, cols], ((0,), (0,))).astype(bf16)

    def exchange(time):
        return to({"tp": 1 - tp}, x_send, x_get, x_sem.at[0, time], x_sem.at[1, time])

    def branch_exchange():
        here, there = branch_s.at[:own_count, :], branch_s.at[own_count:, :]
        return to({"tp": 1 - tp}, here, there, x_sem.at[0, 2], x_sem.at[1, 2])

    def fetched(*pairs):
        copies = [pltpu.make_async_copy(*pair, more_sem.at[i]) for i, pair in enumerate(pairs)]
        for copy in copies:
            copy.start()
        for copy in copies:
            copy.wait()

    def keep_sums(first, sums):
        for other in range(dp_size):
            cols = pl.ds(pl.multiple_of(lax.rem(dp + other, dp_size) * part, part), part)
            for i, values in enumerate(sums):
                small_s[first + i : first + i + 1, cols] = values[:, other * part : (other + 1) * part]

    members = [slice(member * own_count, (member + 1) * own_count) for member in range(tp_size)]

    def hidden_grads():
        for slot in range(seqs):
            at = slice(slot * units, (slot + 1) * units)
            fetched((ffn_out_ref.at[at, :], branch_s.at[:units, :]), (slope_ref.at[:, at], dq_s))
            total = jnp.zeros((1, units), f32)
            for here in members:
                found = mm(tokens_s[here, :], branch_s[:units, :], ((1,), (1,)))
                found = (found * dq_s[here, :].astype(f32)).astype(bf16)
                wide_s[here, at] = found
                total = total + jnp.sum(found.astype(f32), axis=0, keepdims=True)
            for i in range(units // 128):
                slots_s[slot, 2 + i : 3 + i, :] = total[:, i * 128 : (i + 1) * 128]

    def first_grads():
        half = seqs * units // 2
        low, high = mine[3].at[:, :half], theirs[3].at[:, :half]
        for other in range(dp_size):
            at = slice(other * part, (other + 1) * part)
            fetched((in_ref.at[at, :half], low), (in_ref.at[at, half:], high))

            def found(here):
                total = mm(wide_s[here, :half], low[...], ((1,), (1,)))
                return total + mm(wide_s[here, half:], high[...], ((1,), (1,)))

            x_send[:, at] = found(members[1]).astype(bf16)
            resid_ref[:, at] = found(members[0])
        exchange(0).start()

    def norm_grads():
        pairs = []
        for source, target in ((second_ref, dk_s), (normed_ref, dv_s)):
            for i, here in enumerate(members):
                pairs.append((source.at[:, i * heads_all : (i + 1) * heads_all], target.at[here, :]))
        fetched(*pairs)
        exchange(0).wait()

        def block(i, carry):
            at = pl.ds(pl.multiple_of(i * rows, 16), rows)
            late = pl.ds(pl.multiple_of(own_count + i * rows, 16), rows)
            grads = resid_ref[at, :] + x_get[at, :].astype(f32)
            grads = grads + jnp.concatenate([dk_s[at, :], dk_s[late, :]], axis=1)
            normed = jnp.concatenate([dv_s[at, :], dv_s[late, :]], axis=1)
            found = norm_back(grads, normed, column_ref[at, 2:3], gain_ref[...])
            lowered = found.astype(bf16)
            resid_ref[at, :] = found
            branch_s[at, :] = lowered
            terms = (lowered.astype(f32), grads * normed, grads)
            return tuple(c + jnp.sum(term, axis=0, keepdims=True) for c, term in zip(carry, terms))

        zero = jnp.zeros((1, width), f32)
        keep_sums(2, lax.fori_loop(0, seqs, block, (zero, zero, zero)))
        branch_exchange().start()
        fetched((operands_last[3], dq_s), (out_ref, x_send.at[:heads_all, :]))
        branch_exchange().wait()

    def mixed_grads():
        for member, here in enumerate(members):
            found = mm(branch_s[here, :], x_send[:heads_all, :], ((1,), (1,))).astype(bf16)
            for chip in range(seqs):
                at = lax.rem(zs + chip, seqs) * tp_size + lax.rem(tp + member, tp_size)
                at = pl.ds(pl.multiple_of(at * rows, 16), rows)
                up_s[at, :] = found[chip * rows : (chip + 1) * rows]

    def input_grads():
        @pl.when(first_stage)
        def _():
            def theirs_rows(i, carry):
                at = pl.multiple_of(i * rows, 16)
                x_send[pl.ds(at, rows), :] = mm(
                    gq_s[pl.ds(own_count + at, rows), :], joined_ref[...], ((1,), (1,))
                ).astype(bf16)
                return carry

            lax.fori_loop(0, seqs, theirs_rows, 0)
            exchange(1).start()
            for slot in range(seqs):
                cols = slice(slot * hc, (slot + 1) * hc)
                slots_s[slot, 0:1, :] = jnp.sum(gq_s[:, cols].astype(f32), axis=0, keepdims=True)
                cols = slice(2 * heads_all + slot * hc, 2 * heads_all + (slot + 1) * hc)
                slots_s[slot, 1:2, :] = jnp.sum(gq_s[:, cols].astype(f32), axis=0, keepdims=True)
            exchange(1).wait()

            def own_rows(i, carry):
                at = pl.ds(pl.multiple_of(i * rows, 16), rows)
                total = mm(gq_s[at, :], joined_ref[...], ((1,), (1,)))
                total = total + x_get[at, :].astype(f32) + resid_ref[at, :]
                lowered = total.astype(bf16)
                for other in range(dp_size):
                    cols = pl.ds(pl.multiple_of(lax.rem(dp + other, dp_size) * part, part), part)
                    seq_s[i, :, cols] = lowered[:, other * part : (other + 1) * part]
                timed = jnp.sum(total * column_ref[at, 1:2], axis=0, keepdims=True)
                plain = jnp.sum(total, axis=0, keepdims=True)
                return carry[0] + timed, carry[1] + plain

            zero = jnp.zeros((1, width), f32)
            timed, plain = lax.fori_loop(0, seqs, own_rows, (zero, zero))
            keep_sums(0, (timed, plain))

    own_seq = pltpu.make_async_copy(seq_s.at[0], seq_out.at[zs], local_sem.at[0])

    def send_small():
        for by in range(1, seqs):
            small(by).start()
            slots(by).start()
        for by in range(1, seqs):
            sequence(by).start()
        own_seq.start()

    def add_small():
        total, slot_total = small_s[...], slots_s[0]
        for by in range(1, seqs):
            small(by).wait()
            slots(by).wait()
            total = total + small_zs[by]
            slot_total = slot_total + slots_zs[by]
        small_all[0] = total
        slots_dp[0] = slot_total
        for by in range(1, dp_size * tp_size):
            small_across(by).start()
        slots_across().start()

    small_s[...] = small_ref[...]
    slots_s[...] = slots_ref[...]
    def taken(kind):
        for slot in slot_order:
            side(kind, slot).wait()
            added(cut(sides, kind, slot), cut(mine, kind, slot))

    def pass_on(kind, hop):
        @pl.when((zs == hop) & (zs < seqs - 1))
        def _():
            for far in range(seqs - 1 - hop, 0, -1):
                if hop > 0:
                    up(kind, far + 1).wait_recv()
                    added(cut(sides, kind, far), cut(ups, kind, far))
                up(kind, far).start()

        @pl.when((zs == seqs - 1 - hop) & (zs > 0))
        def _():
            for far in range(seqs - 1 - hop, 0, -1):
                if hop > 0:
                    down(kind, far + 1).wait_recv()
                    added(cut(sides, kind, seqs - far), cut(downs, kind, far))
                down(kind, far).start()

    def load(index, target):
        def copies(operands):
            return pltpu.make_async_copy(operands[index], target, load_sem.at[index])


        @pl.when(first_stage)
        def _():
            copies(operands_last).start()

        @pl.when(jnp.logical_not(first_stage))
        def _():
            copies(operands_before).start()

        return copies(operands_last)

    def product(kind, other):
        array, axis, first, size = kinds[kind]
        target = (mine if other == 0 else theirs)[array]
        features = slice(other * part, (other + 1) * part)
        for slot in range(seqs):
            apart = units if array < 2 else hc
            at = slice(first + slot * apart, first + slot * apart + size)
            if axis == 0:
                left = dq_s if array == 2 else wide_s
                right = branch_s if array == 2 else tokens_s
                target[at, :] = mm(left[:, at], right[:, features], ((0,), (0,))).astype(bf16)
            else:
                found = mm(tokens_s[:, features], wide_s[:, at], ((0,), (0,)))
                target[:, at] = found.astype(bf16)

    def old(index, target):
        return pltpu.make_async_copy(operands_before[index], target, load_sem.at[index])

    def relay(step):
        if step < len(kinds):
            taken(step)
        for hop in range(seqs - 1):
            if 0 <= step - hop < len(kinds):
                pass_on(step - hop, hop)

    hidden, grads = load(0, wide_s), load(1, tokens_s)
    hidden.wait()
    grads.wait()
    for kind in (0, 1):
        for other in reversed(range(dp_size)):
            product(kind, other)
            if other == 1:
                begin(kind)

    @pl.when(first_stage)
    def _():
        hidden_grads()

    @pl.when(jnp.logical_not(first_stage))
    def _():
        old(3, wide_s).start()
        old(3, wide_s).wait()

    load(2, tokens_s).wait()
    for kind in (2, 3):
        for other in reversed(range(dp_size)):
            product(kind, other)
        begin(kind)

    @pl.when(first_stage)
    def _():
        first_grads()

    relay(0)

    @pl.when(first_stage)
    def _():
        norm_grads()

    @pl.when(jnp.logical_not(first_stage))
    def _():
        old(4, dq_s).start()
        old(5, branch_s).start()
        old(4, dq_s).wait()
        old(5, branch_s).wait()

    for other in reversed(range(dp_size)):
        product(4, other)
    begin(4)

    @pl.when(first_stage)
    def _():
        mixed_grads()

    relay(1)
    attention_start()
    relay(2)
    attention_end()
    relay(3)
    joined_parts()
    for kind in range(5, len(kinds)):
        begin(kind)
    input_grads()
    send_small()
    for step in range(4, len(kinds) + seqs - 2):
        relay(step)
        if step == 6:
            add_small()

    total, slot_total = small_all[0], slots_dp[0]
    for by in range(1, dp_size * tp_size):
        small_across(by).wait()
        total = total + small_all[by]
    slots_across().wait()
    small_out[...] = total
    slots_out[...] = slot_total + slots_dp[1]

    for kind, (array, axis, first, size) in enumerate(kinds):
        out = outs[array] if array < 3 else outs[3 + first // (seqs * hc)]
        if array < 2:
            out = out.at[first : first + size, :] if axis == 0 else out.at[:, first : first + size]
        out[...] = cut(sides, kind, 0)[...].astype(f32)

        @pl.when(zs > 0)
        def _():
            up(kind, 1).wait_recv()
            added(out, cut(ups, kind, 0))

        @pl.when(zs < seqs - 1)
        def _():
            down(kind, 1).wait_recv()
            added(out, cut(downs, kind, 0))

        for far in range(1, seqs):

            @pl.when(zs + far < seqs)
            def _():
                up(kind, far).wait_send()

            @pl.when(zs >= far)
            def _():
                down(kind, far).wait_send()

    own_seq.wait()
    for by in range(1, seqs):
        sequence(by).wait()


def scatter_all(rows, by_block, small, slots, operands, attended, tokens, gq_before, onward, tp_size):
    seqs, _, width = by_block.shape
    dp_size = 2
    units, part = operands[0].shape[1] // seqs, width // dp_size
    length, heads_all = tokens[0].shape[0], gq_before.shape[1] // 3
    hc = heads_all // seqs
    own_count = length // tp_size
    anywhere = pl.BlockSpec(memory_space=pl.ANY)
    inside = pl.BlockSpec(memory_space=pltpu.VMEM)
    wide = lambda *shape: jax.ShapeDtypeStruct(shape, f32)
    low = lambda *shape: pltpu.VMEM(shape, bf16)
    dma = pltpu.SemaphoreType.DMA
    like = [low(seqs * units, part), low(part, seqs * units), low(heads_all, part), low(part, 3 * heads_all)]
    fewer = [low((seqs - 1) * units, part), low(part, (seqs - 1) * units), low((seqs - 1) * hc, part)]
    fewer.append(low(part, 3 * heads_all))
    kinds = 8
    return pl.pallas_call(
        functools.partial(scatter_kernel, rows, seqs, dp_size, tp_size),
        in_specs=[anywhere, inside, inside]
        + [anywhere] * 11
        + [inside] * 4
        + [anywhere] * 9
        + [inside],
        out_specs=[anywhere] + [inside] * 8,
        out_shape=[
            jax.ShapeDtypeStruct(by_block.shape, bf16),
            wide(*small.shape),
            wide(*slots.shape[1:]),
            wide(units, part),
            wide(part, units),
            wide(hc, part),
            wide(part, hc),
            wide(part, hc),
            wide(part, hc),
        ],
        scratch_shapes=like
        + fewer * 2
        + [
            pltpu.VMEM((seqs,) + small.shape, f32),
            pltpu.VMEM((dp_size * tp_size,) + small.shape, f32),
            pltpu.VMEM(slots.shape, f32),
            pltpu.VMEM((2,) + slots.shape[1:], f32),
            dma((seqs,)),
            dma((seqs,)),
            dma((4,)),
            dma((4, max(seqs, dp_size * tp_size))),
            dma((4, max(seqs, dp_size * tp_size))),
        ]
        + [dma((kinds, seqs))] * 6
        + [low(length, 4 * heads_all), low(length, heads_all)]
        + [pltpu.VMEM((length, heads_all), f32)] * 2
        + [
            low(length, 3 * heads_all),
            low(length, width),
            low(own_count, width),
            low(own_count, width),
            low(*by_block.shape),
            pltpu.VMEM(small.shape, f32),
            pltpu.VMEM(slots.shape, f32),
        ]
        + like * 2
        + [
            dma((3, length // rows)),
            dma((2, 3)),
            dma((6,)),
            pltpu.VMEM((own_count, width), f32),
            low(length, width),
            dma((4,)),
        ],
        compiler_params=pltpu.CompilerParams(
            collective_id=1, has_side_effects=True, vmem_limit_bytes=63 * 1024 * 1024
        ),
    )(by_block, small, slots, *operands, *attended, *tokens, gq_before, *onward)


def per_device(
    states,
    cotangent,
    lengths,
    timesteps,
    time_weight,
    time_bias,
    query_weight,
    query_bias,
    key_weight,
    value_weight,
    value_bias,
    out_weight,
    out_bias,
    attn_gain,
    attn_shift,
    ffn_in,
    ffn_in_bias,
    ffn_out,
    ffn_out_bias,
    ffn_gain,
    ffn_shift,
):
    rows, seqs, width = states.shape
    own_count = seqs * rows
    sections, section_at = lax.axis_size("pipe"), lax.axis_index("pipe")
    dp_size, dp_at = lax.axis_size("dp"), lax.axis_index("dp")
    zs_at = lax.axis_index("zs")
    tp_size, tp_at = lax.axis_size("tp"), lax.axis_index("tp")
    length = own_count * tp_size
    part = width // dp_size
    head_cols, unit_cols = query_weight.shape[2], ffn_in.shape[2]
    heads_all, units_all = head_cols * seqs, unit_cols * seqs

    def rotated(array, axis=-1):
        axis = axis % array.ndim
        twice = jnp.concatenate([array, array], axis=axis)
        return lax.dynamic_slice_in_dim(twice, dp_at * part, width, axis)

    def straightened(array):
        twice = jnp.concatenate([array, array], axis=-1)
        back = (dp_size - dp_at) % dp_size
        return lax.dynamic_slice_in_dim(twice, back * part, width, array.ndim - 1)

    vectors = rotated(
        jnp.concatenate(
            [time_weight, time_bias, out_bias, attn_gain, attn_shift, ffn_out_bias, ffn_gain, ffn_shift]
        )
    )
    time_weight, time_bias, out_bias, attn_gain = vectors[0], vectors[1], vectors[2], vectors[3]
    attn_shift, ffn_out_bias, ffn_gain, ffn_shift = vectors[4], vectors[5], vectors[6], vectors[7]


    def to_sequence(array):
        by_seq = rotated(jnp.transpose(array, (1, 0, 2)))
        got = []
        for by in range(seqs):
            block = lax.dynamic_index_in_dim(by_seq, (zs_at - by) % seqs, 0, keepdims=False)
            got.append(received(block, "zs", by))
        return got

    def to_positions(array):
        by_block = straightened(array).reshape(seqs, rows, width)
        return [received(by_block[(seqs - by) % seqs], "zs", by)[None] for by in range(seqs)]

    def in_positions(got, *before):
        got = [after(piece, *before)[0] for piece in got]
        by_seq = []
        for at in range(seqs):
            found = got[0]
            for by in range(1, seqs):
                found = jnp.where((zs_at + by) % seqs == at, got[by], found)
            by_seq.append(found)
        return jnp.stack(by_seq, axis=1)

    item_ends = jnp.cumsum(lax.dynamic_index_in_dim(lengths, zs_at, 0, keepdims=False))
    own_times = lax.dynamic_index_in_dim(timesteps, zs_at, 0, keepdims=False).astype(f32)
    member = (tp_at + jnp.arange(tp_size, dtype=jnp.int32)) % tp_size
    chips = (zs_at + jnp.arange(seqs, dtype=jnp.int32)) % seqs
    order = (chips[None, :] * tp_size + member[:, None]).reshape(seqs * tp_size).astype(jnp.int32)

    def segment_at(places):
        return jnp.sum((item_ends[None, :] <= places[:, None]).astype(jnp.int32), axis=1)

    segment = segment_at(jnp.arange(length, dtype=jnp.int32))
    span = key_spans(item_ends, length)
    own_places = order[:seqs, None] * rows + jnp.arange(rows, dtype=jnp.int32)[None, :]
    own_segment = segment_at(own_places.reshape(own_count))
    own_pick = own_segment[:, None] == jnp.arange(lengths.shape[1], dtype=jnp.int32)[None, :]
    time_rows = (jnp.sum(jnp.where(own_pick, own_times[None, :], 0.0), axis=1) / STEPS)[:, None]
    aligned = rows % 16 == 0
    kernel_rows = rows if aligned else length
    kernel_order = order if aligned else jnp.zeros((1,), jnp.int32)

    def by_position(array):
        if aligned:
            return array
        blocks = array.reshape(seqs * tp_size, rows, array.shape[1])
        return jnp.take(blocks, jnp.argsort(order), axis=0).reshape(array.shape)

    def by_distance(array):
        if aligned:
            return array
        blocks = array.reshape(seqs * tp_size, rows, array.shape[1])
        return jnp.take(blocks, order, axis=0).reshape(array.shape)


    def over_zs(block, axis, *before):
        mine = lax.dynamic_slice_in_dim(block, dp_at * part, part, axis)
        mine = after(mine, *before)
        return [received(mine, "zs", by) for by in range(1, seqs)]

    def over_dp(pieces):
        return [[received(piece, "dp", other) for other in range(dp_size)] for piece in pieces]

    def assembled(block, axis, pieces, thirds):
        across = 1 - axis
        each = block.shape[across] // thirds
        shape = [0, 0]
        shape[axis], shape[across] = width, block.shape[across] * seqs
        whole = jnp.zeros(shape, block.dtype)

        def put(whole, piece, slot, at):
            for third in range(thirds):
                start = [0, 0]
                start[axis], start[across] = at, (third * seqs + slot) * each
                cut = lax.slice_in_dim(piece, third * each, (third + 1) * each, axis=across)
                whole = lax.dynamic_update_slice(whole, cut, start)
            return whole

        whole = put(whole, rotated(block, axis), 0, 0)
        for slot, row in enumerate(pieces):
            for other, piece in enumerate(row):
                whole = put(whole, piece, slot + 1, other * part)
        return whole

    biases = jnp.concatenate([query_bias[0], value_bias[0], ffn_in_bias[0].astype(f32)])[None]
    in_kernels = sections == 2 and dp_size == 2 and tp_size == 2 and rows % 16 == 0
    in_kernels = in_kernels and head_cols == 128 and part % 256 == 0 and unit_cols % 256 == 0
    in_kernels = in_kernels and heads_all == unit_cols == part
    if in_kernels:
        by_seq = rotated(jnp.transpose(states, (1, 0, 2)))
        blocks = (query_weight, key_weight, value_weight, out_weight, ffn_in, ffn_out)
        tokenwise = (time_rows, time_weight[None], time_bias[None], segment[:, None], segment[None, :])
        start, bias_slots, joined, out_all, in_all, ffn_out_all, *attended_first = gather_all(
            by_seq, biases, [block[0] for block in blocks], tokenwise, dp_size, tp_size
        )
        start_rows = start.reshape(own_count, width)
        bias_slots = bias_slots[:, 0]
    else:
        joined_block = jnp.concatenate([query_weight[0], key_weight[0], value_weight[0]], axis=1)
        start_pieces = to_sequence(states)
        start_rows = jnp.concatenate(start_pieces)
        bias_slots = [received(biases, "zs", by)[0] for by in range(seqs)]
        joined_zs = over_zs(joined_block, 0)
        out_zs = over_zs(out_weight[0], 1, *joined_zs, *start_pieces)
        in_zs = over_zs(ffn_in[0], 0, *out_zs)
        ffn_out_zs = over_zs(ffn_out[0], 1, *in_zs)
        joined = assembled(joined_block, 0, over_dp(joined_zs), 3)
        out_all = assembled(out_weight[0], 1, over_dp(out_zs), 1)
        in_all = assembled(ffn_in[0], 0, over_dp(in_zs), 1)
        ffn_out_all = assembled(ffn_out[0], 1, over_dp(ffn_out_zs), 1)
    query_bias_all = jnp.concatenate([b[:head_cols] for b in bias_slots])
    value_bias_all = jnp.concatenate([b[head_cols : 2 * head_cols] for b in bias_slots])
    in_bias_all = jnp.concatenate([b[2 * head_cols :] for b in bias_slots])
    joined_bias = jnp.concatenate([query_bias_all, jnp.zeros_like(query_bias_all), value_bias_all])

    def everyone(own):
        return jnp.concatenate([received(own, "tp", by) for by in range(tp_size)])

    def returned(full, weight, dims):
        total = 0.0
        for by in range(1, tp_size):
            theirs = mm(full[by * own_count : (by + 1) * own_count], weight, dims).astype(bf16)
            total = total + received(theirs, "tp", -by).astype(f32)
        return total + mm(full[:own_count], weight, dims)

    kept = []
    layer_rows, stat_terms = None, None
    inputs = start_rows
    for tick in range(sections):
        residual = inputs.astype(f32) + time_rows * time_weight + time_bias
        if tick == 0 and in_kernels:
            rounded_all, qkv, mixed, lse = attended_first
        else:
            rounded_all = everyone(residual.astype(bf16))
            qkv = by_position((mm(rounded_all, joined) + joined_bias).astype(bf16))
            mixed, lse = attend(qkv, segment, span, kernel_order, kernel_rows)
        if tick == 1:
            mixed = after(mixed, *upstream_pieces)
        mixed = by_distance(mixed)
        branch = returned(mixed, out_all, ((1,), (0,))) + out_bias
        first_normed, first_inverse = norm_parts(residual + branch)
        first_out = first_normed * attn_gain + attn_shift
        first_all = everyone(first_out.astype(bf16))
        hidden, slope = widen(first_all, in_all, in_bias_all)
        ffn_branch = returned(hidden, ffn_out_all, ((1,), (0,))) + ffn_out_bias
        second_normed, second_inverse = norm_parts(first_out + ffn_branch)
        layer_y = (second_normed * ffn_gain + ffn_shift).astype(bf16)
        terms = jnp.stack([token_sum(each * each) for each in (residual, branch, ffn_branch)])
        kept.append(
            (
                rounded_all,
                qkv,
                mixed,
                lse,
                first_normed,
                first_inverse,
                first_all,
                hidden,
                slope,
                second_normed,
                second_inverse,
            )
        )
        if tick == 0:
            layer_rows, stat_terms = layer_y, terms
            upstream_pieces = to_sequence(after(cotangent, layer_y))
        else:
            here = section_at == tick
            layer_rows = jnp.where(here, layer_y, layer_rows)
            stat_terms = jnp.where(here, terms, stat_terms)
        if tick + 1 < sections:
            inputs = passed_along(layer_y, "pipe", 1)
    layer_pieces = to_positions(layer_rows)


    def parts_of(left, right, side):
        found = []
        for other in range(dp_size):
            cut = slice(other * part, (other + 1) * part)
            if side == 0:
                found.append(mm(left[:, cut], right, ((0,), (0,))).astype(bf16))
            else:
                found.append(mm(left, right[:, cut], ((0,), (0,))).astype(bf16))
        return found

    def chosen(found_at, operands):
        if sections == 1:
            return found_at(*operands[0])
        return lax.switch(
            sections - 1 - section_at, [functools.partial(found_at, *each) for each in operands]
        )

    def owned(parts, axis, thirds):
        total = parts[0].astype(f32)
        for other in range(1, dp_size):
            total = total + received(parts[other], "dp", -other).astype(f32)
        each = total.shape[axis] // (seqs * thirds)
        blocks = [
            jnp.concatenate(
                [
                    lax.slice_in_dim(total, (third * seqs + k) * each, (third * seqs + k + 1) * each, axis=axis)
                    for third in range(thirds)
                ],
                axis=axis,
            )
            for k in range(seqs)
        ]
        mine = blocks[0]
        for by in range(1, seqs):
            mine = mine + received(blocks[by].astype(bf16), "zs", -by).astype(f32)
        return mine

    results = None
    upstream_rows = jnp.concatenate(upstream_pieces)
    for_ffn, for_out, for_joined = [], [], []
    for step in range(sections):
        (
            rounded_all,
            qkv,
            mixed,
            lse,
            first_normed,
            first_inverse,
            first_all,
            hidden,
            slope,
            second_normed,
            second_inverse,
        ) = kept[sections - 1 - step]
        last = step + 1 == sections
        upstream = upstream_rows.astype(f32)
        gain_two, shift_two = token_sum(upstream * second_normed), token_sum(upstream)
        grad_second = norm_back(upstream, second_normed, second_inverse, ffn_gain)
        grad_ffn = grad_second.astype(bf16)
        ffn_out_bias_grad = token_sum(grad_ffn)
        grad_ffn_all = everyone(grad_ffn)
        if last and in_kernels:
            by_token = jnp.concatenate([time_rows, first_inverse], axis=1)
            by_token = jnp.pad(by_token, ((0, length - own_count), (0, 0)))
            columns = jnp.concatenate([segment.astype(f32)[:, None], by_token], axis=1)
            attended = (qkv, lse, columns, segment.astype(f32)[None, :], joined)
            onward = (
                ffn_out_all,
                slope,
                in_all,
                out_all,
                grad_second,
                first_normed,
                attn_gain[None],
            )
            (before,), (before_out,) = for_ffn, for_out
            operands = (*before, *before_out, hidden, grad_ffn_all, first_all, mixed)
            nothing = jnp.zeros((width,), f32)
            tw_grad, tb_grad, out_bias_grad, gain_one, shift_one = [nothing] * 5
            in_bias_sum, bias_sums = jnp.zeros((units_all,), f32), jnp.zeros((3 * heads_all,), f32)
            grad_in_before, grad_in = results[2], jnp.zeros((), bf16)
            results = (results[0], results[1], grad_in)
        else:
            grad_pre = (mm(grad_ffn_all, ffn_out_all, ((1,), (1,))) * slope.astype(f32)).astype(bf16)
            in_bias_sum = token_sum(grad_pre)
            for_ffn.append((hidden, grad_ffn_all, first_all, grad_pre))
            if last:
                ffn_out_parts = chosen(lambda a, b, c, d: parts_of(a, b, 1), for_ffn)
                ffn_in_parts = chosen(lambda a, b, c, d: parts_of(c, d, 0), for_ffn)
                grad_second = after(grad_second, *ffn_out_parts, *ffn_in_parts)
            grad_first = grad_second + returned(grad_pre, in_all, ((1,), (1,)))
            gain_one, shift_one = token_sum(grad_first * first_normed), token_sum(grad_first)
            grad_resid = norm_back(grad_first, first_normed, first_inverse, attn_gain)
            grad_branch = grad_resid.astype(bf16)
            out_bias_grad = token_sum(grad_branch)
            branch_all = everyone(grad_branch)
            grad_mixed = by_position(mm(branch_all, out_all, ((1,), (1,))).astype(bf16))
            for_out.append((mixed, branch_all))
            if last:
                out_parts = chosen(lambda a, b: parts_of(a, b, 1), for_out)
                grad_mixed = after(grad_mixed, *out_parts)
            grads = attend_back(qkv, segment, span, kernel_order, kernel_rows, grad_mixed, lse)
            grad_qkv = jnp.concatenate([by_distance(grad) for grad in grads], axis=1)
            bias_sums = token_sum(grad_qkv)
            for_joined.append((rounded_all, grad_qkv))
            if last:
                joined_parts = chosen(lambda a, b: parts_of(a, b, 0), for_joined)
            grad_input = grad_resid + returned(grad_qkv, joined, ((1,), (1,)))
            tw_grad, tb_grad = token_sum(grad_input * time_rows), token_sum(grad_input)
            grad_in = grad_input.astype(bf16)
        slot_sums = jnp.concatenate(
            [
                bias_sums[:heads_all].reshape(seqs, head_cols),
                bias_sums[2 * heads_all :].reshape(seqs, head_cols),
                in_bias_sum.reshape(seqs, unit_cols),
            ],
            axis=1,
        )
        vector_sums = jnp.stack(
            [tw_grad, tb_grad, out_bias_grad, gain_one, shift_one, ffn_out_bias_grad, gain_two, shift_two]
        )
        these = (vector_sums, slot_sums, grad_in)
        if step == 0:
            results = these
        else:
            here = section_at == sections - 1 - step
            results = jax.tree.map(lambda a, b: jnp.where(here, a, b), these, results)
        if not last:
            upstream_rows = passed_along(grad_in, "pipe", -1)
    vector_sums, slot_sums, grad_in = results
    shared = straightened(jnp.concatenate([vector_sums, stat_terms]))
    if in_kernels:
        small = jnp.concatenate([shared, jnp.zeros((5, width), f32)])
        padded = -(-slot_sums.shape[1] // 1024) * 1024
        slots = jnp.pad(slot_sums, ((0, 0), (0, padded - slot_sums.shape[1])))
        by_block = straightened(grad_in_before).reshape(seqs, rows, width)
        input_pieces, small, slots, *gradients = scatter_all(
            rows,
            by_block,
            small,
            slots.reshape(seqs, 8, padded // 8),
            operands,
            attended,
            (rounded_all, for_joined[0][0]),
            for_joined[0][1],
            onward,
            tp_size,
        )
        input_grad = jnp.transpose(input_pieces, (1, 0, 2))
        shared, own_slot = small[:11], slots.reshape(1, padded)[:, : slot_sums.shape[1]]
        ffn_out_grad, ffn_in_grad, out_grad = gradients[:3]
        triple = gradients[3:]
    else:
        input_grad = in_positions(to_positions(grad_in))
        shared = summed_over(summed_over(summed_over(shared, "tp"), "zs"), "dp")
        own_slot = slot_sums[0:1]
        for by in range(1, seqs):
            own_slot = own_slot + received(slot_sums[by : by + 1], "zs", -by)
        own_slot = summed_over(own_slot, "dp")
        ffn_out_grad = owned(ffn_out_parts, 0, 1)
        ffn_in_grad = owned(ffn_in_parts, 1, 1)
        out_grad = owned(out_parts, 0, 1)
        joined_grad = owned(joined_parts, 1, 3)
        triple = [joined_grad[:, i * head_cols : (i + 1) * head_cols] for i in range(3)]
    layer_out = in_positions(layer_pieces, grad_ffn_all)
    element_count = float(SEQ_LEN * seqs * dp_size * width)
    stats = jnp.sqrt(jnp.sum(shared[8:11], axis=1) / element_count)
    return (
        layer_out[None],
        input_grad[None],
        shared[0:1],
        shared[1:2],
        triple[0][None],
        own_slot[:, :head_cols],
        triple[1][None],
        triple[2][None],
        own_slot[:, head_cols : 2 * head_cols],
        out_grad[None],
        shared[2:3],
        shared[3:4],
        shared[4:5],
        ffn_in_grad[None],
        own_slot[:, 2 * head_cols :],
        ffn_out_grad[None],
        shared[5:6],
        shared[6:7],
        shared[7:8],
        stats[None],
    )


def solution(mesh):
    def run(states, *rest):
        sizes = mesh.shape
        seqs = states.shape[1] // sizes["dp"]
        grouped = Mesh(
            mesh.devices.reshape(sizes["pipe"], sizes["dp"], seqs, sizes["tensor"] // seqs),
            ("pipe", "dp", "zs", "tp"),
        )
        return jax.shard_map(
            per_device,
            mesh=grouped,
            in_specs=(
                P(TENSOR, "dp", None),
                P(TENSOR, "dp", None),
                P("dp", None),
                P("dp", None),
                P("pipe", None),
                P("pipe", None),
                P("pipe", None, TENSOR),
                P("pipe", TENSOR),
                P("pipe", None, TENSOR),
                P("pipe", None, TENSOR),
                P("pipe", TENSOR),
                P("pipe", TENSOR, None),
                P("pipe", None),
                P("pipe", None),
                P("pipe", None),
                P("pipe", None, TENSOR),
                P("pipe", TENSOR),
                P("pipe", TENSOR, None),
                P("pipe", None),
                P("pipe", None),
                P("pipe", None),
            ),
            out_specs=(
                P("pipe", TENSOR, "dp", None),
                P("pipe", TENSOR, "dp", None),
                P("pipe", None),
                P("pipe", None),
                P("pipe", "dp", TENSOR),
                P("pipe", TENSOR),
                P("pipe", "dp", TENSOR),
                P("pipe", "dp", TENSOR),
                P("pipe", TENSOR),
                P("pipe", TENSOR, "dp"),
                P("pipe", None),
                P("pipe", None),
                P("pipe", None),
                P("pipe", "dp", TENSOR),
                P("pipe", TENSOR),
                P("pipe", TENSOR, "dp"),
                P("pipe", None),
                P("pipe", None),
                P("pipe", None),
                P("pipe", None),
            ),
            check_vma=False,
        )(states, *rest)

    return run
```
